32 devices in a mesh: rep: 16 (over z, x, core), shard: 2 (over y).
Axes of the slice: x: 2, y: 2, z: 4, core: 2. Of those that a mesh axis runs over, the one named last changes fastest.
Arguments:
- latents: bfloat16 [64, 256, 768], P(('rep', 'shard')), may hold values from -3 to 3
- condition: bfloat16 [64, 768], P(('rep', 'shard')), may hold values from -3 to 3
- output_grad: bfloat16 [64, 256, 768], P(('rep', 'shard')), may hold values from -3 to 3
- w_ada: bfloat16 [2, 768, 4608], P(None, 'shard'), may hold values from -0.21875 to 0.21875
- b_ada: bfloat16 [2, 4608], P(None, 'shard'), may hold values from -0.9 to 0.9
- query_key_value_weight: bfloat16 [2, 768, 2304], P(None, 'shard'), may hold values from -0.21875 to 0.21875
- b_qv: bfloat16 [2, 1536], P(None, 'shard'), may hold values from -0.9 to 0.9
- output_matrix_weight: bfloat16 [2, 768, 768], P(None, 'shard'), may hold values from -0.875 to 0.875
- b_proj: bfloat16 [2, 768], P(None, 'shard'), may hold values from -0.9 to 0.9
- first_linear_weight: bfloat16 [2, 768, 3072], P(None, 'shard'), may hold values from -0.21875 to 0.21875
- b_fc1: bfloat16 [2, 3072], P(None, 'shard'), may hold values from -0.9 to 0.9
- second_linear_weight: bfloat16 [2, 3072, 768], P(None, 'shard'), may hold values from -0.109375 to 0.109375
- b_fc2: bfloat16 [2, 768], P(None, 'shard'), may hold values from -0.9 to 0.9
Outputs:
- outputs: bfloat16 [64, 256, 768], P(('rep', 'shard'))
- latents_grad: float32 [64, 256, 768], P(('rep', 'shard'))
- condition_grad: float32 [64, 768], P(('rep', 'shard'))
- g_w_ada: float32 [2, 768, 4608], P(None, 'shard')
- g_b_ada: float32 [2, 4608], P(None, 'shard')
- gradient_query_key_value: float32 [2, 768, 2304], P(None, 'shard')
- g_b_qv: float32 [2, 1536], P(None, 'shard')
- gradient_output_matrix: float32 [2, 768, 768], P(None, 'shard')
- g_b_proj: float32 [2, 768], P(None, 'shard')
- gradient_first_linear: float32 [2, 768, 3072], P(None, 'shard')
- g_b_fc1: float32 [2, 3072], P(None, 'shard')
- gradient_second_linear: float32 [2, 3072, 768], P(None, 'shard')
- g_b_fc2: float32 [2, 768], P(None, 'shard')
The draws below stay inside these ranges and needn't reach their ends.
All inputs are finite; a program needn't handle non-finite values.
Results may differ from the reference program's by a relative error of at most 0.018.
Values may be sent and summed in bfloat16 or wider, within the bound.
No kernel may reach another device: no remote copies, remote signals or barrier semaphores. Data moves between devices by JAX's collectives and lax.ppermute only.
A program may use at most 256 MiB of HBM per device.

```python
import jax
import jax.numpy as jnp
from jax import lax

D = 768
HEADS = 12
HEAD_DIM = 64
FF = 3072
LAYERS = 2
LEN = 256
SEQS = 64


def clipped_normal(key, shape, scale):
    return jax.random.truncated_normal(key, -3.0, 3.0, shape, jnp.float32) * scale


def draw_latents(key, part):
    key = jax.random.fold_in(key, 11)
    values = clipped_normal(key, (SEQS, LEN, D), 1.0)
    return values.astype(jnp.bfloat16)


def draw_condition(key, part):
    key = jax.random.fold_in(key, 12)
    values = clipped_normal(key, (SEQS, D), 1.0)
    return values.astype(jnp.bfloat16)


def draw_output_grad(key, part):
    key = jax.random.fold_in(key, 13)
    values = clipped_normal(key, (SEQS, LEN, D), 1.0)
    return values.astype(jnp.bfloat16)


def draw_b_ada(key, part):
    key = jax.random.fold_in(key, 14)
    values = clipped_normal(key, (LAYERS, 6 * D), 0.3)
    return values.astype(jnp.bfloat16)


def draw_b_qv(key, part):
    key = jax.random.fold_in(key, 15)
    values = clipped_normal(key, (LAYERS, 2 * D), 0.3)
    return values.astype(jnp.bfloat16)


def draw_b_proj(key, part):
    key = jax.random.fold_in(key, 16)
    values = clipped_normal(key, (LAYERS, D), 0.3)
    return values.astype(jnp.bfloat16)


def draw_b_fc1(key, part):
    key = jax.random.fold_in(key, 17)
    values = clipped_normal(key, (LAYERS, FF), 0.3)
    return values.astype(jnp.bfloat16)


def draw_b_fc2(key, part):
    key = jax.random.fold_in(key, 18)
    values = clipped_normal(key, (LAYERS, D), 0.3)
    return values.astype(jnp.bfloat16)


def steps_of(rng, shape, pieces, smallest, top_value):
    loudness, own = 1.0, jax.random.fold_in(rng, 6)
    for axis_at, blocks in pieces:
        heights = jnp.exp(jax.random.uniform(jax.random.fold_in(own, axis_at), (blocks,), jnp.float32, smallest / len(pieces), top_value / len(pieces)))
        loudness = loudness * jnp.repeat(heights, shape[axis_at] // blocks).reshape([-1 if axis == axis_at else 1 for axis in range(len(shape))])
    return loudness


def normal_values(own_key, dims, scale, reach, pieces=(), held_as=jnp.bfloat16):
    array = scale * jax.random.normal(own_key, dims, jnp.float32)
    if pieces:
        array = array * steps_of(own_key, dims, pieces, -0.22, 0.18)
    return jnp.clip(array, -reach, reach).astype(held_as)


def setup_inputs(seed: int = 0) -> dict:
    key_of = jax.random.split(jax.random.key(seed), 14)
    latents = draw_latents(jax.random.fold_in(key_of[13], 71), 0)
    condition = draw_condition(jax.random.fold_in(key_of[13], 71), 0)
    output_grad = draw_output_grad(jax.random.fold_in(key_of[13], 71), 0)
    w_ada = normal_values(key_of[3], (LAYERS, D, 6 * D), D ** -0.5, 0.21875, ((1, 2),))
    b_ada = draw_b_ada(jax.random.fold_in(key_of[13], 71), 0)
    query_key_value_weight = normal_values(key_of[5], (LAYERS, D, 3 * D), D ** -0.5, 0.21875, ((1, 2),))
    b_qv = draw_b_qv(jax.random.fold_in(key_of[13], 71), 0)
    output_matrix_weight = normal_values(key_of[7], (LAYERS, D, D), (D // 16) ** -0.5, 0.875, ((1, 2),))
    b_proj = draw_b_proj(jax.random.fold_in(key_of[13], 71), 0)
    first_linear_weight = normal_values(key_of[9], (LAYERS, D, FF), D ** -0.5, 0.21875, ((1, 2),))
    b_fc1 = draw_b_fc1(jax.random.fold_in(key_of[13], 71), 0)
    second_linear_weight = normal_values(key_of[11], (LAYERS, FF, D), FF ** -0.5, 0.109375, ((1, 2),))
    b_fc2 = draw_b_fc2(jax.random.fold_in(key_of[13], 71), 0)
    return dict(latents=latents, condition=condition, output_grad=output_grad, w_ada=w_ada, b_ada=b_ada, query_key_value_weight=query_key_value_weight, b_qv=b_qv, output_matrix_weight=output_matrix_weight, b_proj=b_proj, first_linear_weight=first_linear_weight, b_fc1=b_fc1, second_linear_weight=second_linear_weight, b_fc2=b_fc2)


eps = 1e-06
highest = lax.Precision.HIGHEST

@jax.custom_vjp
def low(v):
    return lax.optimization_barrier(v.astype(jnp.bfloat16)).astype(jnp.float32)

@jax.custom_vjp
def low_back(v):
    return v

def low_keep(v):
    return (low(v), None)

def low_pass(kept, grad):
    return (grad,)

def back_keep(v):
    return (v, None)

def back_low(kept, grad):
    return (low(grad),)
low.defvjp(low_keep, low_pass)
low_back.defvjp(back_keep, back_low)

def layer_norm(rows):
    centred = rows - lax.optimization_barrier(jnp.mean(rows, axis=-1, keepdims=True))
    return centred * lax.rsqrt(lax.optimization_barrier(jnp.mean(centred * centred, axis=-1, keepdims=True)) + eps)

def project(rows, matrix):
    return jnp.einsum('gld,de->gle', rows, matrix, precision=highest)

def block(stream, silu_low, params):
    w_ada, b_ada, query_key_value_weight, b_qv, output_matrix_weight, b_proj, first_linear_weight, b_fc1, second_linear_weight, b_fc2 = params
    modulation = jnp.dot(silu_low, w_ada, precision=highest) + b_ada
    shift_a, scale_a, gate_a, shift_m, scale_m, gate_m = jnp.split(modulation[:, None, :], 6, axis=-1)
    group_count, length = (stream.shape[0], stream.shape[1])
    attention_input = low(layer_norm(stream) * (1.0 + scale_a) + shift_a)
    query_key_value_bias = jnp.concatenate([b_qv[:D], jnp.zeros((D,), jnp.float32), b_qv[D:]])
    qkv = low(low_back(project(attention_input, query_key_value_weight) + query_key_value_bias))
    query_rows = qkv[..., :D].reshape(group_count, length, HEADS, HEAD_DIM)
    key_rows = qkv[..., D:2 * D].reshape(group_count, length, HEADS, HEAD_DIM)
    value_rows = qkv[..., 2 * D:].reshape(group_count, length, HEADS, HEAD_DIM)
    scores = low_back(jnp.einsum('gqhd,gkhd->ghqk', query_rows, key_rows, precision=highest) * HEAD_DIM ** (-0.5))
    attn_probs = low(jax.nn.softmax(scores, axis=-1))
    attention_output = low(low_back(jnp.einsum('ghqk,gkhd->gqhd', attn_probs, value_rows, precision=highest)))
    attention_output = attention_output.reshape(group_count, length, D)
    branch = low_back(project(attention_output, output_matrix_weight) + b_proj)
    middle = stream + gate_a * branch
    feedforward_input = low(layer_norm(middle) * (1.0 + scale_m) + shift_m)
    hidden_pre = low_back(project(feedforward_input, first_linear_weight) + b_fc1)
    hidden_units = low(jax.nn.gelu(hidden_pre, approximate=True))
    output = low_back(project(hidden_units, second_linear_weight) + b_fc2)
    return middle + gate_m * output

def forward(rows, conds, params):
    silu_low = low(jax.nn.silu(conds))
    stream = rows
    for layer_index in range(LAYERS):
        stream = block(stream, silu_low, tuple((p[layer_index] for p in params)))
    return stream

def reference(latents, condition, output_grad, w_ada, b_ada, query_key_value_weight, b_qv, output_matrix_weight, b_proj, first_linear_weight, b_fc1, second_linear_weight, b_fc2):
    params = tuple((p.astype(jnp.float32) for p in (w_ada, b_ada, query_key_value_weight, b_qv, output_matrix_weight, b_proj, first_linear_weight, b_fc1, second_linear_weight, b_fc2)))
    group_size = min(16, SEQS)
    block_count = SEQS // group_size
    rows_all = latents.astype(jnp.float32).reshape(block_count, group_size, LEN, D)
    cond_all = condition.astype(jnp.float32).reshape(block_count, group_size, D)
    grads_all = output_grad.astype(jnp.float32).reshape(block_count, group_size, LEN, D)

    def step(totals, item):
        block_rows, block_cond, block_grad = item
        forward_out, pullback = jax.vjp(forward, block_rows, block_cond, params)
        grad_rows, grad_cond, grad_params = pullback(block_grad)
        totals = tuple((t + g for t, g in zip(totals, grad_params)))
        return (totals, (forward_out.astype(jnp.bfloat16), grad_rows, grad_cond))
    starts = tuple((jnp.zeros_like(p) for p in params))
    totals, (results, grad_rows, grad_cond) = lax.scan(step, starts, (rows_all, cond_all, grads_all))
    outputs = results.reshape(SEQS, LEN, D)
    latents_grad = grad_rows.reshape(SEQS, LEN, D)
    condition_grad = grad_cond.reshape(SEQS, D)
    return (outputs, latents_grad, condition_grad, totals[0], totals[1], totals[2], totals[3], totals[4], totals[5], totals[6], totals[7], totals[8], totals[9])
```

```python
import functools

import jax
import jax.numpy as jnp
import numpy as np
from jax import lax
from jax.sharding import Mesh
from jax.sharding import PartitionSpec as P

HEADS = 12
eps = 1e-06
f32 = jnp.float32
bf16 = jnp.bfloat16


def normalize(rows):
    centred = rows - jnp.mean(rows, axis=-1, keepdims=True)
    inverse = lax.rsqrt(jnp.mean(centred * centred, axis=-1, keepdims=True) + eps)
    return (centred * inverse, inverse)


def norm_back(upstream, normed, inverse):
    return inverse * (
        upstream
        - jnp.mean(upstream, axis=-1, keepdims=True)
        - normed * jnp.mean(upstream * normed, axis=-1, keepdims=True)
    )


def gelu_tanh(values):
    return jax.nn.gelu(values, approximate=True)


def mm(a, b):
    return jnp.dot(a, b, preferred_element_type=f32)


def mm_t(a, b):
    return lax.dot_general(a, b, (((1,), (1,)), ((), ())), preferred_element_type=f32)


def t_mm(a, b):
    return lax.dot_general(a, b, (((0,), (0,)), ((), ())), preferred_element_type=f32)


def pick(array, index, axis=0):
    return lax.dynamic_index_in_dim(array, index, axis, keepdims=False)


def after(value, token):
    value, _ = lax.optimization_barrier((value, token))
    return value


SWAP = [(0, 1), (1, 0)]


def swap(value, axis):
    return lax.ppermute(value, axis, SWAP)


class Fast:
    def __init__(self):
        self.far = lax.axis_index("far")
        self.near = lax.axis_index("near")
        self.core = lax.axis_index("core")
        self.shard = lax.axis_index("shard")
        self.left = self.far < 2
        self.is_end = jnp.logical_or(self.far == 0, self.far == 3)

    def fetch_first(self, own):
        quarter = own.shape[0] // 4
        piece = lax.dynamic_slice_in_dim(
            own, (self.near * 2 + self.core) * quarter, quarter, 0
        )
        return piece

    def fetch_rest(self, own, a):
        rows, cols = own.shape
        quarter = rows // 4
        b = swap(a, "near")
        a2 = swap(a, "core")
        b2 = swap(b, "core")
        full = jnp.zeros((2 * rows, cols), own.dtype)
        full = lax.dynamic_update_slice(full, own, (self.shard * rows, 0))
        base = (1 - self.shard) * rows
        for value, near, core in (
            (a, self.near, self.core),
            (b, 1 - self.near, self.core),
            (a2, self.near, 1 - self.core),
            (b2, 1 - self.near, 1 - self.core),
        ):
            full = lax.dynamic_update_slice(full, value, (base + (near * 2 + core) * quarter, 0))
        return full

    def relative(self, stack, step):
        return pick(stack, jnp.where(self.left, step, 3 - step))

    def line_sum(self, stack):
        end, inner, inner2, end2 = [self.relative(stack, step) for step in range(4)]
        a = lax.ppermute(jnp.stack([inner, inner2, end2]), "far", [(0, 1), (3, 2)])
        b = lax.ppermute(
            jnp.stack(
                [
                    (inner2.astype(f32) + a[1].astype(f32)).astype(bf16),
                    (end2.astype(f32) + a[2].astype(f32)).astype(bf16),
                ]
            ),
            "far",
            [(1, 2), (2, 1)],
        )
        c = lax.ppermute(
            (end.astype(f32) + b[1].astype(f32)).astype(bf16), "far", [(1, 0), (2, 3)]
        )
        return jnp.where(
            self.is_end,
            end.astype(f32) + c.astype(f32),
            inner.astype(f32) + a[0].astype(f32) + b[0].astype(f32),
        ).astype(bf16)

    def line_gather(self, own):
        a = lax.ppermute(own, "far", [(0, 1), (3, 2)])
        b = lax.ppermute(jnp.stack([own, a]), "far", [(1, 2), (2, 1)])
        c = lax.ppermute(jnp.concatenate([own[None], b], 0), "far", [(1, 0), (2, 3)])
        end = jnp.where(self.is_end, own, a)
        inner = jnp.where(self.is_end, c[0], own)
        inner2 = jnp.where(self.is_end, c[1], b[0])
        end2 = jnp.where(self.is_end, c[2], b[1])
        return jnp.stack(
            [
                jnp.where(self.left, end, end2),
                jnp.where(self.left, inner, inner2),
                jnp.where(self.left, inner2, inner),
                jnp.where(self.left, end2, end),
            ]
        )

    def pair_sum(self, stack, axis, at):
        me = lax.axis_index(axis)
        got = swap(pick(stack, 1 - me, at), axis)
        return (pick(stack, me, at).astype(f32) + got.astype(f32)).astype(bf16)

    def pair_gather(self, own, axis, at=0):
        got = swap(own, axis)
        me = lax.axis_index(axis)
        return jnp.stack(
            [jnp.where(me == 0, own, got), jnp.where(me == 0, got, own)], axis=at
        )

    def reduce_weight(self, lhs, rhs, order):
        rows, cols = lhs.shape[1], rhs.shape[1]
        half = cols // 2
        theirs = lax.dynamic_slice_in_dim(rhs, (1 - self.core) * half, half, 1)
        mine = lax.dynamic_slice_in_dim(rhs, self.core * half, half, 1)
        got = swap(t_mm(lhs, theirs).astype(bf16), "core")
        part = (t_mm(lhs, mine) + got.astype(f32)).astype(bf16)
        part = part.reshape(2, 2, 4, rows // 16, half)
        if order == "yzx":
            part = self.pair_sum(part, "shard", 0)
            part = jnp.stack([part[:, place] for place in range(4)])
            part = self.line_sum(part)
            part = self.pair_sum(part, "near", 0)
            part = self.pair_gather(part, "near")
            part = self.line_gather(part)
            part = jnp.stack([part[:, 0], part[:, 1]])
        else:
            part = self.pair_sum(part, "near", 1)
            part = self.pair_sum(part, "shard", 0)
            part = self.line_sum(part)
            part = self.line_gather(part)
            part = self.pair_gather(part, "near")
        part = part.reshape(rows // 2, half)
        got = swap(part, "core")
        mine_first = self.core == 0
        return jnp.concatenate(
            [jnp.where(mine_first, part, got), jnp.where(mine_first, got, part)], axis=1
        ).astype(f32)

    def gather_own(self, value):
        got = swap(value, "shard")
        first = self.shard == 0
        return jnp.stack([jnp.where(first, value, got), jnp.where(first, got, value)])

    def gather_every(self, value):
        value = value[None]
        for axis in ("core", "shard", "near"):
            value = jnp.concatenate([value, swap(value, axis)], 0)
        others = [
            lax.ppermute(value, "far", [(i, i ^ step) for i in range(4)]) for step in (1, 2, 3)
        ]
        return jnp.concatenate([value] + others, 0)

    def to_partner_rows(self, part):
        part = part.reshape(2, -1, part.shape[-1])
        got = swap(pick(part, 1 - self.shard), "shard")
        return pick(part, self.shard) + got


class Plain:
    def __init__(self):
        self.shard = lax.axis_index("shard")

    def fetch_first(self, own):
        return None

    def fetch_rest(self, own, a):
        return lax.all_gather(own, "shard", axis=0, tiled=True)

    def reduce_weight(self, lhs, rhs, order):
        grad = t_mm(lhs, rhs).astype(bf16)
        grad = lax.psum_scatter(grad, "shard", scatter_dimension=0, tiled=True)
        return lax.psum(grad, ("far", "near", "core")).astype(f32)

    def gather_own(self, value):
        return lax.all_gather(value, "shard", axis=0)

    def gather_every(self, value):
        return lax.all_gather(value, ("far", "near", "core", "shard"), axis=0)

    def to_partner_rows(self, part):
        return lax.psum_scatter(part, "shard", scatter_dimension=0, tiled=True)


def heads_of(rows, count):
    return rows.reshape(count, -1, HEADS, rows.shape[-1] // HEADS)


def attention_forward(qkv, count):
    width = qkv.shape[1] // 3
    q, k, v = [heads_of(qkv[:, i * width : (i + 1) * width], count) for i in range(3)]
    factor = q.shape[-1] ** (-0.5)
    scores = jnp.einsum("sqhd,skhd->shqk", q, k, preferred_element_type=f32) * factor
    log_total = jax.nn.logsumexp(scores, axis=-1, keepdims=True)
    probs = jnp.exp(scores - log_total).astype(bf16)
    out = jnp.einsum("shqk,skhd->sqhd", probs, v, preferred_element_type=f32)
    return out.astype(bf16).reshape(qkv.shape[0], width), log_total


def attention_backward(qkv, log_total, grad, count):
    width = qkv.shape[1] // 3
    q, k, v = [heads_of(qkv[:, i * width : (i + 1) * width], count) for i in range(3)]
    grad = heads_of(grad, count)
    factor = q.shape[-1] ** (-0.5)
    scores = jnp.einsum("sqhd,skhd->shqk", q, k, preferred_element_type=f32) * factor
    exact = jnp.exp(scores - log_total)
    grad_probs = jnp.einsum("sqhd,skhd->shqk", grad, v, preferred_element_type=f32)
    row_terms = jnp.sum(grad_probs * exact, axis=-1, keepdims=True)
    grad_scores = (exact * (grad_probs - row_terms)).astype(bf16)
    grad_q = jnp.einsum("shqk,skhd->sqhd", grad_scores, k, preferred_element_type=f32) * factor
    grad_k = jnp.einsum("shqk,sqhd->skhd", grad_scores, q, preferred_element_type=f32) * factor
    grad_v = jnp.einsum("shqk,sqhd->skhd", exact.astype(bf16), grad, preferred_element_type=f32)
    flat = [g.astype(bf16).reshape(qkv.shape[0], width) for g in (grad_q, grad_k, grad_v)]
    return jnp.concatenate(flat, axis=1)


def local(
    fast,
    latents,
    condition,
    output_grad,
    w_ada,
    b_ada,
    query_key_value_weight,
    b_qv,
    output_matrix_weight,
    b_proj,
    first_linear_weight,
    b_fc1,
    second_linear_weight,
    b_fc2,
):
    comm = Fast() if fast else Plain()
    layer_count, owned_rows, ada_width = w_ada.shape
    seq_count, length, features = latents.shape
    tokens = seq_count * length
    shard_count = lax.axis_size("shard")

    cond_value = condition.astype(f32)
    silu_low = jax.nn.silu(cond_value).astype(bf16)
    silu_pair = comm.gather_own(silu_low).reshape(shard_count * seq_count, features)
    silu_mine = lax.dynamic_slice_in_dim(silu_pair, comm.shard * owned_rows, owned_rows, 1)
    biases = (b_ada, b_qv, b_proj, b_fc1, b_fc2)
    widths = [b.shape[1] for b in biases]
    bias_all = comm.gather_own(jnp.concatenate(biases, axis=1))
    cuts = np.cumsum(widths)[:-1]
    full_biases = [
        jnp.moveaxis(part, 0, 1).reshape(layer_count, -1).astype(f32)
        for part in jnp.split(bias_all, cuts, axis=2)
    ]
    mod_part = jnp.concatenate([mm(silu_mine, w_ada[l]) for l in range(layer_count)], axis=1)
    mod_both = comm.to_partner_rows(mod_part).reshape(seq_count, layer_count, ada_width)
    mods = []
    for l in range(layer_count):
        mod = mod_both[:, l] + full_biases[0][l]
        mods.append(jnp.split(mod[:, None, :], 6, axis=-1))
    silu_every = comm.gather_every(silu_low).reshape(-1, features)

    owns = []
    for l in range(layer_count):
        for w in (
            query_key_value_weight,
            output_matrix_weight,
            first_linear_weight,
            second_linear_weight,
        ):
            owns.append(w[l])
    weights = []
    firsts = []
    for index, own in enumerate(owns):
        piece = comm.fetch_first(own)
        if piece is not None:
            if index >= 2:
                piece = after(piece, firsts[index - 2])
            piece = swap(piece, "shard")
        firsts.append(piece)
        weights.append(comm.fetch_rest(own, piece))
    layers = [weights[4 * l : 4 * l + 4] for l in range(layer_count)]

    def spread(rows):
        return rows.reshape(seq_count, length, -1)

    def flat(rows):
        return rows.reshape(tokens, -1)

    stream = latents.astype(f32)
    stored = []
    for l in range(layer_count):
        w_qkv, w_out, w_fc1, w_fc2 = layers[l]
        _, bias_qv, bias_proj, bias_fc1, bias_fc2 = [b[l] for b in full_biases]
        shift_a, scale_a, gate_a, shift_m, scale_m, gate_m = mods[l]
        normed_a, inverse_a = normalize(stream)
        attn_in = flat((normed_a * (1.0 + scale_a) + shift_a).astype(bf16))
        bias_qkv = jnp.concatenate(
            [bias_qv[:features], jnp.zeros((features,), f32), bias_qv[features:]]
        )
        qkv = (mm(attn_in, w_qkv) + bias_qkv).astype(bf16)
        attn_out, log_total = attention_forward(qkv, seq_count)
        branch = spread(mm(attn_out, w_out) + bias_proj)
        middle = stream + gate_a * branch
        normed_m, inverse_m = normalize(middle)
        mlp_in = flat((normed_m * (1.0 + scale_m) + shift_m).astype(bf16))
        hidden_pre = mm(mlp_in, w_fc1) + bias_fc1
        hidden = gelu_tanh(hidden_pre).astype(bf16)
        output = spread(mm(hidden, w_fc2) + bias_fc2)
        stream = middle + gate_m * output
        stored.append(
            (
                normed_a, inverse_a, attn_in, qkv, log_total, attn_out, branch,
                normed_m, inverse_m, mlp_in, hidden_pre, hidden, output,
            )
        )
    outputs = stream.astype(bf16)

    dh = output_grad.astype(f32)
    grads = [None] * layer_count
    small = [None] * layer_count
    grad_mods = [None] * layer_count
    for l in reversed(range(layer_count)):
        w_qkv, w_out, w_fc1, w_fc2 = layers[l]
        shift_a, scale_a, gate_a, shift_m, scale_m, gate_m = mods[l]
        (
            normed_a, inverse_a, attn_in, qkv, log_total, attn_out, branch,
            normed_m, inverse_m, mlp_in, hidden_pre, hidden, output,
        ) = stored[l]
        grad_out = flat((gate_m * dh).astype(bf16))
        g_fc2 = comm.reduce_weight(hidden, grad_out, "yzx" if l else "xyz")
        d_gate_m = jnp.sum(dh * output, axis=1)
        g_b_fc2 = jnp.sum(grad_out.astype(f32), axis=0)
        grad_hidden = mm_t(grad_out, w_fc2)
        _, gelu_pull = jax.vjp(gelu_tanh, hidden_pre)
        grad_pre = gelu_pull(grad_hidden)[0].astype(bf16)
        g_fc1 = comm.reduce_weight(mlp_in, grad_pre, "xyz" if l else "yzx")
        g_b_fc1 = jnp.sum(grad_pre.astype(f32), axis=0)
        grad_mlp_in = spread(mm_t(grad_pre, w_fc1))
        d_shift_m = jnp.sum(grad_mlp_in, axis=1)
        d_scale_m = jnp.sum(grad_mlp_in * normed_m, axis=1)
        grad_mid = dh + norm_back(grad_mlp_in * (1.0 + scale_m), normed_m, inverse_m)
        grad_branch = flat((gate_a * grad_mid).astype(bf16))
        d_gate_a = jnp.sum(grad_mid * branch, axis=1)
        g_b_proj = jnp.sum(grad_branch.astype(f32), axis=0)
        g_out = comm.reduce_weight(attn_out, grad_branch, "xyz")
        grad_attn = mm_t(grad_branch, w_out).astype(bf16)
        grad_qkv = attention_backward(qkv, log_total, grad_attn, seq_count)
        qkv_sums = jnp.sum(grad_qkv.astype(f32), axis=0)
        g_b_qv = jnp.concatenate([qkv_sums[:features], qkv_sums[2 * features :]])
        g_qkv = comm.reduce_weight(attn_in, grad_qkv, "yzx")
        grad_attn_in = spread(mm_t(grad_qkv, w_qkv))
        d_shift_a = jnp.sum(grad_attn_in, axis=1)
        d_scale_a = jnp.sum(grad_attn_in * normed_a, axis=1)
        dh = grad_mid + norm_back(grad_attn_in * (1.0 + scale_a), normed_a, inverse_a)
        grad_mod = jnp.concatenate(
            [d_shift_a, d_scale_a, d_gate_a, d_shift_m, d_scale_m, d_gate_m], axis=-1
        ).astype(bf16)
        grad_mods[l] = grad_mod
        grads[l] = (g_qkv, g_out, g_fc1, g_fc2)
        vector = jnp.concatenate(
            [grad_mod.reshape(-1)] + [g.astype(bf16) for g in (g_b_qv, g_b_proj, g_b_fc1, g_b_fc2)]
        )
        small[l] = comm.gather_every(vector.reshape(-1, 128))

    silu_parts = []
    for l in reversed(range(layer_count)):
        pair = comm.gather_own(grad_mods[l]).reshape(shard_count * seq_count, ada_width)
        silu_parts.append(mm_t(pair, w_ada[l]))
    silu_part = functools.reduce(jnp.add, silu_parts)
    if fast:
        by_owner = silu_part.reshape(2, seq_count, owned_rows)
        got = swap(pick(by_owner, 1 - comm.shard), "shard")
        mine = pick(by_owner, comm.shard)
        first = comm.shard == 0
        grad_silu = jnp.concatenate(
            [jnp.where(first, mine, got), jnp.where(first, got, mine)], axis=1
        )
    else:
        by_owner = silu_part.reshape(shard_count, seq_count, owned_rows)
        got = lax.all_to_all(by_owner, "shard", 0, 0)
        grad_silu = jnp.moveaxis(got, 0, 1).reshape(seq_count, features)
    _, silu_pull = jax.vjp(jax.nn.silu, cond_value)
    condition_grad = silu_pull(grad_silu)[0]

    silu_owned = lax.dynamic_slice_in_dim(silu_every, comm.shard * owned_rows, owned_rows, 1)
    g_w_ada, g_biases = [], []
    for l in range(layer_count):
        devices = small[l].shape[0]
        every_vector = small[l].reshape(devices, -1)
        mod_every = every_vector[:, : seq_count * ada_width].reshape(-1, ada_width)
        g_w_ada.append(t_mm(silu_owned, mod_every))
        sums = [jnp.sum(mod_every.astype(f32), axis=0)]
        rest = jnp.sum(every_vector[:, seq_count * ada_width :].astype(f32), axis=0)
        at = 0
        for width in widths[1:]:
            sums.append(rest[at : at + width * shard_count])
            at += width * shard_count
        g_biases.append(
            [
                lax.dynamic_slice_in_dim(total, comm.shard * width, width, 0)
                for total, width in zip(sums, widths)
            ]
        )
    bias_out = [jnp.stack([g[m] for g in g_biases]) for m in range(5)]
    weight_out = [jnp.stack([g[m] for g in grads]) for m in range(4)]
    return (
        outputs,
        dh,
        condition_grad,
        jnp.stack(g_w_ada),
        bias_out[0],
        weight_out[0],
        bias_out[1],
        weight_out[1],
        bias_out[2],
        weight_out[2],
        bias_out[3],
        weight_out[3],
        bias_out[4],
    )


def solution(mesh):
    rep, shard = mesh.shape["rep"], mesh.shape["shard"]
    core = 2 if rep % 2 == 0 else 1
    near = 2 if rep == 16 else 1
    far = rep // (core * near)
    fast = (far, near, core, shard) == (4, 2, 2, 2)
    fine = Mesh(
        np.asarray(mesh.devices).reshape(far, near, core, shard),
        ("far", "near", "core", "shard"),
    )
    every = ("far", "near", "core", "shard")
    row, row3 = P(every, None), P(every, None, None)
    bias, weight = P(None, "shard"), P(None, "shard", None)
    return jax.shard_map(
        functools.partial(local, fast),
        mesh=fine,
        in_specs=(
            row3, row, row3, weight, bias, weight, bias, weight, bias, weight, bias, weight, bias,
        ),
        out_specs=(
            row3, row3, row, weight, bias, weight, bias, weight, bias, weight, bias, weight, bias,
        ),
        check_vma=False,
    )
```

```python
import functools

import jax
import jax.numpy as jnp
import numpy as np
from jax import lax
from jax.experimental import pallas as pl
from jax.experimental.pallas import tpu as pltpu
from jax.sharding import Mesh
from jax.sharding import PartitionSpec as P

HEADS = 12
eps = 1e-06
f32 = jnp.float32
bf16 = jnp.bfloat16


def normalize(rows):
    centred = rows - jnp.mean(rows, axis=-1, keepdims=True)
    inverse = lax.rsqrt(jnp.mean(centred * centred, axis=-1, keepdims=True) + eps)
    return (centred * inverse, inverse)


def norm_back(upstream, normed, inverse):
    return inverse * (
        upstream
        - jnp.mean(upstream, axis=-1, keepdims=True)
        - normed * jnp.mean(upstream * normed, axis=-1, keepdims=True)
    )


def gelu_parts(u):
    inner = 0.7978845608028654 * (u + 0.044715 * u * u * u)
    return jnp.tanh(inner)


def gelu(u):
    return 0.5 * u * (1.0 + gelu_parts(u))


def gelu_slope(u):
    t = gelu_parts(u)
    return 0.5 * (1.0 + t) + 0.5 * u * (1.0 - t * t) * 0.7978845608028654 * (
        1.0 + 3.0 * 0.044715 * u * u
    )


def mm(a, b):
    return jnp.dot(a, b, preferred_element_type=f32)


def mm_t(a, b):
    return lax.dot_general(a, b, (((1,), (1,)), ((), ())), preferred_element_type=f32)


def t_mm(a, b):
    return lax.dot_general(a, b, (((0,), (0,)), ((), ())), preferred_element_type=f32)


def pick(array, index, axis=0):
    return lax.dynamic_index_in_dim(array, index, axis, keepdims=False)


SWAP = [(0, 1), (1, 0)]
CHEAP = pl.CostEstimate(flops=1, bytes_accessed=1, transcendentals=0)
PARAMS = pltpu.CompilerParams(vmem_limit_bytes=40 * 2**20)


def swap(value, axis):
    return lax.ppermute(value, axis, SWAP)


def gate(tree):
    values, shape = jax.tree.flatten(tree)
    count = len(values)

    def nothing(*refs):
        pass

    out = pl.pallas_call(
        nothing,
        out_shape=[jax.ShapeDtypeStruct(v.shape, v.dtype) for v in values],
        in_specs=[pl.BlockSpec(memory_space=pl.ANY)] * count,
        out_specs=[pl.BlockSpec(memory_space=pl.ANY)] * count,
        input_output_aliases={i: i for i in range(count)},
        cost_estimate=CHEAP,
    )(*values)
    return jax.tree.unflatten(shape, out)


def call(kernel, grid, ins, outs, prefetch=(), aliases=None):
    def spec(block, index, once=False):
        if block is None:
            return pl.BlockSpec(memory_space=pl.ANY)
        if once:
            return pl.BlockSpec(block, index, pipeline_mode=pl.Buffered(1))
        return pl.BlockSpec(block, index)

    return pl.pallas_call(
        kernel,
        out_shape=[jax.ShapeDtypeStruct(shape, dtype) for shape, dtype, _, _ in outs],
        grid_spec=pltpu.PrefetchScalarGridSpec(
            num_scalar_prefetch=len(prefetch),
            grid=grid,
            in_specs=[spec(*entry[1:]) for entry in ins],
            out_specs=[spec(block, index) for _, _, block, index in outs],
        ),
        input_output_aliases=aliases or {},
        cost_estimate=CHEAP,
        compiler_params=PARAMS,
    )(*prefetch, *[entry[0] for entry in ins])


class Block:
    def __init__(self, mod, biases, seq_count, length):
        self.mod = mod.reshape(seq_count, 6, -1)
        self.biases = biases
        self.seq_count, self.length = seq_count, length
        self.features = self.mod.shape[2]

    def rows(self, array):
        return (array, (self.length, array.shape[1]), lambda s: (s, 0))

    def rows_out(self, width, dtype):
        shape = (self.seq_count * self.length, width)
        return (shape, dtype, (self.length, width), lambda s: (s, 0))

    def mods(self):
        return (self.mod, (None, 6, self.features), lambda s: (s, 0, 0))

    def sums_out(self):
        return (
            (self.seq_count, 8, self.features),
            f32,
            (None, 8, self.features),
            lambda s: (s, 0, 0),
        )

    @staticmethod
    def whole(array):
        return (array, array.shape, lambda s: (0,) * array.ndim, True)

    def attention(self, stream, w_qkv):
        bias_qv, features = self.biases[0], self.features
        bias = jnp.concatenate(
            [bias_qv[:features], jnp.zeros((features,), f32), bias_qv[features:]]
        )[None]

        def kernel(stream_ref, mod_ref, w_ref, bias_ref, in_ref, qkv_ref):
            normed, _ = normalize(stream_ref[...])
            attn_in = (normed * (1.0 + mod_ref[1:2]) + mod_ref[0:1]).astype(bf16)
            in_ref[...] = attn_in
            qkv_ref[...] = (mm(attn_in, w_ref[...]) + bias_ref[...]).astype(bf16)

        self.stream = stream
        self.attn_in, self.qkv = call(
            kernel,
            (self.seq_count,),
            [self.rows(stream), self.mods(), self.whole(w_qkv), self.whole(bias)],
            [self.rows_out(features, bf16), self.rows_out(3 * features, bf16)],
        )
        self.attn_out = attention_forward(self.qkv, self.seq_count)

    def project(self, w_out):
        def kernel(out_ref, stream_ref, mod_ref, w_ref, bias_ref, branch_ref, middle_ref, in_ref):
            branch = mm(out_ref[...], w_ref[...]) + bias_ref[...]
            middle = stream_ref[...] + mod_ref[2:3] * branch
            normed, _ = normalize(middle)
            branch_ref[...] = branch
            middle_ref[...] = middle
            in_ref[...] = (normed * (1.0 + mod_ref[4:5]) + mod_ref[3:4]).astype(bf16)

        self.branch, self.middle, self.mlp_in = call(
            kernel,
            (self.seq_count,),
            [
                self.rows(self.attn_out),
                self.rows(self.stream),
                self.mods(),
                self.whole(w_out),
                self.whole(self.biases[1][None]),
            ],
            [
                self.rows_out(self.features, f32),
                self.rows_out(self.features, f32),
                self.rows_out(self.features, bf16),
            ],
        )

    def wide(self, array, tile):
        return (array, (self.length, tile), lambda j, s: (s, j))

    def hidden_layer(self, w_fc1):
        hidden, tile = w_fc1.shape[1], self.features
        shape = (self.seq_count * self.length, hidden)

        def kernel(in_ref, w_ref, bias_ref, pre_ref, hidden_ref):
            pre = mm(in_ref[...], w_ref[...]) + bias_ref[...]
            pre_ref[...] = pre
            hidden_ref[...] = gelu(pre).astype(bf16)

        self.hidden_pre, self.hidden = call(
            kernel,
            (hidden // tile, self.seq_count),
            [
                (self.mlp_in, (self.length, self.features), lambda j, s: (s, 0)),
                (w_fc1, (self.features, tile), lambda j, s: (0, j)),
                (self.biases[2][None], (1, tile), lambda j, s: (0, j)),
            ],
            [
                (shape, f32, (self.length, tile), lambda j, s: (s, j)),
                (shape, bf16, (self.length, tile), lambda j, s: (s, j)),
            ],
        )

    def output_layer(self, w_fc2, dtype):
        def kernel(hidden_ref, middle_ref, mod_ref, w_ref, bias_ref, output_ref, stream_ref):
            output = mm(hidden_ref[...], w_ref[...]) + bias_ref[...]
            output_ref[...] = output
            stream_ref[...] = (middle_ref[...] + mod_ref[5:6] * output).astype(dtype)

        self.output, stream = call(
            kernel,
            (self.seq_count,),
            [
                self.rows(self.hidden),
                self.rows(self.middle),
                self.mods(),
                self.whole(w_fc2),
                self.whole(self.biases[3][None]),
            ],
            [self.rows_out(self.features, f32), self.rows_out(self.features, dtype)],
        )
        return stream

    def back_start(self, dh):
        def kernel(dh_ref, mod_ref, grad_ref, sums_ref):
            grad_out = (mod_ref[5:6] * dh_ref[...].astype(f32)).astype(bf16)
            grad_ref[...] = grad_out
            sums_ref[0:1] = jnp.sum(grad_out.astype(f32), axis=0, keepdims=True)

        self.dh = dh
        self.grad_out, self.sums_out2 = call(
            kernel,
            (self.seq_count,),
            [self.rows(dh), self.mods()],
            [self.rows_out(self.features, bf16), self.sums_out()],
        )
        return (self.hidden, self.grad_out)

    def back_hidden(self, w_fc2):
        hidden, tile = w_fc2.shape[0], self.features
        shape = (self.seq_count * self.length, hidden)

        def kernel(grad_ref, pre_ref, w_ref, out_ref, sum_ref):
            grad_hidden = mm_t(grad_ref[...], w_ref[...])
            grad_pre = (grad_hidden * gelu_slope(pre_ref[...])).astype(bf16)
            out_ref[...] = grad_pre
            sum_ref[...] = jnp.sum(grad_pre.astype(f32), axis=0, keepdims=True)

        self.grad_pre, self.sum_fc1 = call(
            kernel,
            (hidden // tile, self.seq_count),
            [
                (self.grad_out, (self.length, self.features), lambda j, s: (s, 0)),
                self.wide(self.hidden_pre, tile),
                (w_fc2, (tile, self.features), lambda j, s: (j, 0)),
            ],
            [
                (shape, bf16, (self.length, tile), lambda j, s: (s, j)),
                ((self.seq_count, 1, hidden), f32, (None, 1, tile), lambda j, s: (s, 0, j)),
            ],
        )
        return (self.mlp_in, self.grad_pre)

    def back_middle(self, w_fc1, w_out):
        def kernel(
            grad_ref, w1_ref, dh_ref, output_ref, middle_ref, mod_ref, branch_ref, wo_ref,
            mid_ref, gb_ref, ga_ref, sums_ref,
        ):
            grad_in = mm_t(grad_ref[...], w1_ref[...])
            normed, inverse = normalize(middle_ref[...])
            dh = dh_ref[...].astype(f32)
            mid = dh + norm_back(grad_in * (1.0 + mod_ref[4:5]), normed, inverse)
            grad_branch = (mod_ref[2:3] * mid).astype(bf16)
            mid_ref[...] = mid
            gb_ref[...] = grad_branch
            ga_ref[...] = mm_t(grad_branch, wo_ref[...]).astype(bf16)
            for at, value in enumerate(
                (
                    mid * branch_ref[...],
                    grad_in,
                    grad_in * normed,
                    dh * output_ref[...],
                    grad_branch.astype(f32),
                )
            ):
                sums_ref[at : at + 1] = jnp.sum(value, axis=0, keepdims=True)

        self.grad_mid, self.grad_branch, self.grad_attn, self.sums_mid = call(
            kernel,
            (self.seq_count,),
            [
                self.rows(self.grad_pre),
                self.whole(w_fc1),
                self.rows(self.dh),
                self.rows(self.output),
                self.rows(self.middle),
                self.mods(),
                self.rows(self.branch),
                self.whole(w_out),
            ],
            [
                self.rows_out(self.features, f32),
                self.rows_out(self.features, bf16),
                self.rows_out(self.features, bf16),
                self.sums_out(),
            ],
        )
        return (self.attn_out, self.grad_branch)

    def back_attention(self):
        self.grad_qkv = attention_backward(self.qkv, self.grad_attn, self.seq_count)
        return (self.attn_in, self.grad_qkv)

    def back_end(self, w_qkv):
        features = self.features

        def kernel(grad_ref, w_ref, stream_ref, mod_ref, mid_ref, dh_ref, sums_ref):
            grad_qkv = grad_ref[...]
            grad_in = mm_t(grad_qkv, w_ref[...])
            normed, inverse = normalize(stream_ref[...].astype(f32))
            dh_ref[...] = mid_ref[...] + norm_back(
                grad_in * (1.0 + mod_ref[1:2]), normed, inverse
            )
            for at, value in enumerate((grad_in, grad_in * normed)):
                sums_ref[at : at + 1] = jnp.sum(value, axis=0, keepdims=True)
            for part in range(3):
                columns = grad_qkv[:, part * features : (part + 1) * features].astype(f32)
                sums_ref[2 + part : 3 + part] = jnp.sum(columns, axis=0, keepdims=True)

        dh, sums = call(
            kernel,
            (self.seq_count,),
            [
                self.rows(self.grad_qkv),
                self.whole(w_qkv),
                self.rows(self.stream),
                self.mods(),
                self.rows(self.grad_mid),
            ],
            [self.rows_out(features, f32), self.sums_out()],
        )
        grad_mod = jnp.concatenate([sums[:, 0:2], self.sums_mid[:, 0:4]], axis=1)
        grad_mod = grad_mod.reshape(self.seq_count, 6 * features).astype(bf16)
        totals = jnp.sum(sums, axis=0)
        bias_sums = jnp.concatenate(
            [
                totals[2],
                totals[4],
                jnp.sum(self.sums_mid[:, 4], axis=0),
                jnp.sum(self.sum_fc1[:, 0], axis=0),
                jnp.sum(self.sums_out2[:, 0], axis=0),
            ]
        ).astype(bf16)
        return dh, grad_mod, bias_sums


def softmax_of(q, k, factor):
    scores = mm_t(q, k) * factor
    raised = jnp.exp(scores - jnp.max(scores, axis=-1, keepdims=True))
    return raised * (1.0 / jnp.sum(raised, axis=-1, keepdims=True))


def head_masks(rows, head):
    lane = lax.broadcasted_iota(jnp.int32, (rows, 128), 1)
    return [jnp.logical_and(lane >= at, lane < at + head) for at in range(0, 128, head)]


def attention_forward(qkv, count):
    tokens, triple = qkv.shape
    width, length = triple // 3, tokens // count
    groups, head = width // 128, width // HEADS
    factor = head ** (-0.5)

    def kernel(q_ref, k_ref, v_ref, out_ref):
        q, k, v = q_ref[...], k_ref[...], v_ref[...]
        total = jnp.zeros((length, 128), f32)
        for mask in head_masks(length, head):
            probs = softmax_of(jnp.where(mask, q, 0), k, factor).astype(bf16)
            total = total + mm(probs, jnp.where(mask, v, 0))
        out_ref[...] = total.astype(bf16)

    def part(which):
        return pl.BlockSpec((length, 128), lambda s, g: (s, which * groups + g))

    return pl.pallas_call(
        kernel,
        out_shape=jax.ShapeDtypeStruct((tokens, width), bf16),
        grid=(count, groups),
        in_specs=[part(0), part(1), part(2)],
        out_specs=part(0),
        cost_estimate=CHEAP,
    )(qkv, qkv, qkv)


def attention_backward(qkv, grad, count):
    tokens, triple = qkv.shape
    width, length = triple // 3, tokens // count
    groups, head = width // 128, width // HEADS
    factor = head ** (-0.5)

    def kernel(q_ref, k_ref, v_ref, g_ref, out_ref):
        q, k, v, g = q_ref[...], k_ref[...], v_ref[...], g_ref[...]
        grad_q = jnp.zeros((length, 128), f32)
        grad_k = jnp.zeros((length, 128), f32)
        grad_v = jnp.zeros((length, 128), f32)
        for mask in head_masks(length, head):
            own_q, own_g = jnp.where(mask, q, 0), jnp.where(mask, g, 0)
            probs = softmax_of(own_q, k, factor)
            grad_probs = mm_t(own_g, v)
            row_terms = jnp.sum(grad_probs * probs, axis=-1, keepdims=True)
            grad_scores = (probs * (grad_probs - row_terms)).astype(bf16)
            grad_q = grad_q + mm(grad_scores, jnp.where(mask, k, 0))
            grad_k = grad_k + t_mm(grad_scores, own_q)
            grad_v = grad_v + t_mm(probs.astype(bf16), own_g)
        at = pl.program_id(1) * 128
        for part, value in enumerate((grad_q * factor, grad_k * factor, grad_v)):
            columns = pl.ds(pl.multiple_of(part * width + at, 128), 128)
            out_ref[:, columns] = value.astype(bf16)

    def part(which):
        return pl.BlockSpec((length, 128), lambda s, g: (s, which * groups + g))

    return pl.pallas_call(
        kernel,
        out_shape=jax.ShapeDtypeStruct((tokens, triple), bf16),
        grid=(count, groups),
        in_specs=[part(0), part(1), part(2), part(0)],
        out_specs=pl.BlockSpec((length, triple), lambda s, g: (s, 0)),
        cost_estimate=CHEAP,
    )(qkv, qkv, qkv, grad)


TILE = 384


def product_part(lhs, rhs, row_part, col_half, got=None, into=None, at=0, width=None):
    tokens, rows = lhs.shape
    half = rhs.shape[1] // 2
    row_at, row_count = row_part
    rows = rows // row_count
    width = width or half
    place = jnp.stack([jnp.asarray(row_at, jnp.int32), jnp.asarray(col_half, jnp.int32)])
    row_tiles, col_tiles, shift = rows // TILE, half // TILE, at // TILE
    ins = [
        (lhs, (tokens, TILE), lambda j, i, p: (0, p[0] * row_tiles + i)),
        (rhs, (tokens, TILE), lambda j, i, p: (0, p[1] * col_tiles + j)),
    ]
    if got is not None:
        ins.append((got, (TILE, TILE), lambda j, i, p: (p[0] * row_tiles + i, shift + j)))
    aliases = {}
    if into is not None:
        aliases = {1 + len(ins): 0}
        ins.append((into, None, None))

    def kernel(place_ref, lhs_ref, rhs_ref, *refs):
        total = t_mm(lhs_ref[...], rhs_ref[...])
        if got is not None:
            total = total + refs[0][...].astype(f32)
        refs[-1][...] = total.astype(bf16)

    return call(
        kernel,
        (col_tiles, row_tiles),
        ins,
        [((rows, width), bf16, (TILE, TILE), lambda j, i, p: (i, shift + j))],
        prefetch=(place,),
        aliases=aliases,
    )[0]


def unit_part(pairs, row_part, col_half, got=None):
    width = sum(rhs.shape[1] // 2 for _, rhs in pairs)
    out, at = None, 0
    for lhs, rhs in pairs:
        out = product_part(lhs, rhs, row_part, col_half, got, out, at, width)
        at += rhs.shape[1] // 2
    return out


class Fast:
    def __init__(self):
        self.near = lax.axis_index("near")
        self.core = lax.axis_index("core")
        self.shard = lax.axis_index("shard")
        self.place = jnp.stack([self.shard, self.near, self.core]).astype(jnp.int32)

    def ordered(self, mine, got, axis, at=0):
        first = lax.axis_index(axis) == 0
        return jnp.stack([jnp.where(first, mine, got), jnp.where(first, got, mine)], axis=at)

    def split(self, stack, axis, at=0):
        me = lax.axis_index(axis)
        return pick(stack, 1 - me, at), pick(stack, me, at)

    def quarter(self, stacked, layer):
        size = stacked.shape[1] // 4
        start = (self.near * 2 + self.core) * size
        return lax.dynamic_slice(stacked, (layer, start, 0), (1, size, stacked.shape[2]))[0]

    def assemble(self, stacked, layer, pieces, column):
        _, rows, width = stacked.shape
        size = rows // 4
        across = column // width

        def out_block(step, place):
            shard, near, core = place[0], place[1], place[2]
            piece = jnp.maximum(step - 4, 0)
            near_at = jnp.where(piece % 2 == 0, near, 1 - near)
            core_at = jnp.where(piece < 2, core, 1 - core)
            theirs = (1 - shard) * 4 + near_at * 2 + core_at
            return jnp.where(step < 4, shard * 4 + step, theirs), 0

        def kernel(place_ref, own_ref, *refs):
            step, out_ref = pl.program_id(0), refs[-1]

            @pl.when(step < 4)
            def _():
                out_ref[...] = own_ref[...]

            for at in range(4):

                @pl.when(step == 4 + at)
                def _(value=refs[at]):
                    out_ref[...] = value[...]

        ins = [
            (
                stacked,
                (None, size, width),
                lambda s, p: (layer, jnp.minimum(s, 3), 0),
            )
        ]
        ins += [(piece, (size, width), lambda s, p: (0, across)) for piece in pieces]
        return call(
            kernel,
            (8,),
            ins,
            [((2 * rows, width), stacked.dtype, (size, width), out_block)],
            prefetch=(self.place,),
        )[0]

    def final(self, pieces, layer, column, width, into):
        rows = pieces[0].shape[0]
        tiles, shift = width // TILE, column // TILE

        def out_block(j, piece, place):
            near, core = place[1], place[2]
            near_at = jnp.where(piece % 2 == 0, near, 1 - near)
            core_at = jnp.where(piece < 2, core, 1 - core)
            return layer, near_at, core_at * tiles + j

        def kernel(place_ref, *refs):
            piece, out_ref = pl.program_id(1), refs[-1]
            for at in range(4):

                @pl.when(piece == at)
                def _(value=refs[at]):
                    out_ref[...] = value[...].astype(f32)

        ins = [(piece, (rows, TILE), lambda j, i, p: (0, shift + j)) for piece in pieces]
        aliases = {}
        if into is not None:
            aliases = {5: 0}
            ins.append((into, None, None))
        return call(
            kernel,
            (tiles, 4),
            ins,
            [((2, 2 * rows, 2 * width), f32, (None, rows, TILE), out_block)],
            prefetch=(self.place,),
            aliases=aliases,
        )[0]


def ada_weight(silu, mods, layer, layers, into):
    count, rows = silu.shape
    width = mods.shape[1]
    tile = 768 if width % 768 == 0 else width

    def kernel(silu_ref, mods_ref, *refs):
        refs[-1][...] = t_mm(silu_ref[...], mods_ref[...])

    ins = [
        (silu, (count, rows), lambda j: (0, 0)),
        (mods, (count, tile), lambda j: (0, j)),
    ]
    aliases = {}
    if into is not None:
        aliases = {2: 0}
        ins.append((into, None, None))
    return call(
        kernel,
        (width // tile,),
        ins,
        [((layers, rows, width), f32, (None, rows, tile), lambda j: (layer, 0, j))],
        aliases=aliases,
    )[0]


def silu_grad(cond_value, grad_silu):
    _, silu_pull = jax.vjp(jax.nn.silu, cond_value)
    return silu_pull(grad_silu)[0]


def owned_biases(mod_every, bias_sums, shard, widths, shard_count):
    totals, at = [jnp.sum(mod_every.astype(f32), axis=0)], 0
    for width in widths[1:]:
        totals.append(bias_sums[at : at + width * shard_count])
        at += width * shard_count
    return [
        lax.dynamic_slice_in_dim(total, shard * width, width, 0)
        for total, width in zip(totals, widths)
    ]


def unpack_biases(bias_all, widths):
    cuts = np.cumsum(widths)[:-1]
    parts = [
        jnp.moveaxis(part, 0, 1).reshape(bias_all.shape[1], -1).astype(f32)
        for part in jnp.split(bias_all, cuts, axis=2)
    ]
    return [[part[l] for part in parts] for l in range(bias_all.shape[1])]


def in_order(outputs, dh, condition_grad, g_w_ada, biases, weights):
    return (
        outputs,
        dh,
        condition_grad,
        g_w_ada,
        biases[0],
        weights[0],
        biases[1],
        weights[1],
        biases[2],
        weights[2],
        biases[3],
        weights[3],
        biases[4],
    )


def local_plain(
    latents,
    condition,
    output_grad,
    w_ada,
    b_ada,
    query_key_value_weight,
    b_qv,
    output_matrix_weight,
    b_proj,
    first_linear_weight,
    b_fc1,
    second_linear_weight,
    b_fc2,
):
    layer_count, owned_rows, ada_width = w_ada.shape
    seq_count, length, features = latents.shape
    shard, shards = lax.axis_index("shard"), lax.axis_size("shard")
    every = ("far", "near", "core", "shard")
    biases = (b_ada, b_qv, b_proj, b_fc1, b_fc2)
    widths = [b.shape[1] for b in biases]

    cond_value = condition.astype(f32)
    silu_low = jax.nn.silu(cond_value).astype(bf16)
    silu_group = lax.all_gather(silu_low, "shard", axis=0, tiled=True)
    silu_mine = lax.dynamic_slice_in_dim(silu_group, shard * owned_rows, owned_rows, 1)
    bias_all = lax.all_gather(jnp.concatenate(biases, axis=1), "shard", axis=0)
    full_biases = unpack_biases(bias_all, widths)
    mod_part = jnp.concatenate([mm(silu_mine, w_ada[l]) for l in range(layer_count)], axis=1)
    mod = lax.psum_scatter(mod_part, "shard", scatter_dimension=0, tiled=True)
    mod = mod.reshape(seq_count, layer_count, ada_width)
    silu_every = lax.all_gather(silu_low, every, axis=0, tiled=True)

    tokens = seq_count * length
    stream, blocks, weights = latents.astype(f32).reshape(tokens, features), [], []
    for l in range(layer_count):
        block = Block(mod[:, l] + full_biases[l][0], full_biases[l][1:], seq_count, length)
        full = [
            lax.all_gather(w[l], "shard", axis=0, tiled=True)
            for w in (
                query_key_value_weight,
                output_matrix_weight,
                first_linear_weight,
                second_linear_weight,
            )
        ]
        block.attention(stream, full[0])
        block.project(full[1])
        block.hidden_layer(full[2])
        stream = block.output_layer(full[3], bf16 if l == layer_count - 1 else f32)
        blocks.append(block)
        weights.append(full)

    def reduce(pair):
        grad = t_mm(*pair).astype(bf16)
        grad = lax.psum_scatter(grad, "shard", scatter_dimension=0, tiled=True)
        return lax.psum(grad, ("far", "near", "core")).astype(f32)

    dh = output_grad.reshape(tokens, features)
    grads, ada, owned, grad_silu = [None] * layer_count, None, [None] * layer_count, 0.0
    silu_owned = lax.dynamic_slice_in_dim(silu_every, shard * owned_rows, owned_rows, 1)
    for l in reversed(range(layer_count)):
        block, full = blocks[l], weights[l]
        second = block.back_start(dh)
        first = block.back_hidden(full[3])
        out = block.back_middle(full[2], full[1])
        qkv = block.back_attention()
        dh, grad_mod, bias_sums = block.back_end(full[0])
        grads[l] = [reduce(pair) for pair in (qkv, out, first, second)]
        mod_every = lax.all_gather(grad_mod, every, axis=0, tiled=True)
        ada = ada_weight(silu_owned, mod_every, l, layer_count, ada)
        sums = lax.psum(bias_sums.astype(f32), every)
        owned[l] = owned_biases(mod_every, sums, shard, widths, shards)
        mods_group = lax.all_gather(grad_mod, "shard", axis=0, tiled=True)
        grad_silu = grad_silu + mm_t(mods_group, w_ada[l])
    by_owner = grad_silu.reshape(shards, seq_count, owned_rows)
    got = lax.all_to_all(by_owner, "shard", 0, 0)
    grad_silu = jnp.moveaxis(got, 0, 1).reshape(seq_count, features)
    return in_order(
        stream.reshape(latents.shape),
        dh.reshape(latents.shape),
        silu_grad(cond_value, grad_silu),
        ada,
        [jnp.stack([o[m] for o in owned]) for m in range(5)],
        [jnp.stack([g[m] for g in grads]) for m in range(4)],
    )


def local_fast(
    latents,
    condition,
    output_grad,
    w_ada,
    b_ada,
    query_key_value_weight,
    b_qv,
    output_matrix_weight,
    b_proj,
    first_linear_weight,
    b_fc1,
    second_linear_weight,
    b_fc2,
):
    comm = Fast()
    layer_count, owned_rows, ada_width = w_ada.shape
    seq_count, length, features = latents.shape
    tokens = seq_count * length
    shard = comm.shard
    biases = (b_ada, b_qv, b_proj, b_fc1, b_fc2)
    widths = [b.shape[1] for b in biases]

    chunk_of = []
    for l in range(layer_count):
        chunk_of.append((l, (query_key_value_weight, output_matrix_weight)))
        chunk_of.append((l, (first_linear_weight,)))
        chunk_of.append((l, (second_linear_weight,)))
    chunks = len(chunk_of)
    sends = []
    for l, members in chunk_of:
        quarters = [comm.quarter(member, l) for member in members]
        sends.append(quarters[0] if len(quarters) == 1 else jnp.concatenate(quarters, axis=1))

    cond_value = condition.astype(f32)
    silu_low = jax.nn.silu(cond_value).astype(bf16)
    bias_mine = jnp.concatenate(biases, axis=1)
    latents_flat = latents.reshape(tokens, features)
    stream = latents_flat
    pieces = [[None] * 4 for _ in range(chunks)]
    weights = [None] * chunks
    blocks = [None] * layer_count
    silu_all = silu_low.reshape(1, -1, 128)
    outputs = None
    for step in range(0, chunks + 2):
        live = {}
        if step < chunks:
            live["a"] = swap(sends[step], "shard")
        at = step - 1
        if 0 <= at < chunks:
            live["b"] = swap(pieces[at][0], "near")
            live["a2"] = swap(pieces[at][0], "core")
        at = step - 2
        if 0 <= at < chunks:
            live["b2"] = swap(pieces[at][1], "core")
        if step == 0:
            live["silu"] = swap(silu_low, "shard")
            live["bias"] = swap(bias_mine, "shard")
        elif step == 1:
            live["mod"] = swap(mod_send, "shard")
        elif step in (2, 3, 4):
            live["every"] = swap(silu_all, ("core", "shard", "near")[step - 2])
        elif step == 5:
            live["every"] = [
                lax.ppermute(silu_all, "far", [(i, i ^ k) for i in range(4)]) for k in (1, 2, 3)
            ]
        at = step - 3
        if at >= 0:
            l, part = at // 3, at % 3
            block = blocks[l]
            if part == 0:
                block.attention(stream, weights[at][0])
                block.project(weights[at][1])
                live["done"] = block.mlp_in
            elif part == 1:
                block.hidden_layer(weights[at][0])
                live["done"] = block.hidden
            else:
                stream = block.output_layer(weights[at][0], f32)
                live["done"] = stream
        if step + 1 < chunks:
            live["send"] = sends[step + 1]
        live = gate(live)
        if step + 1 < chunks:
            sends[step + 1] = live["send"]
        if step < chunks:
            pieces[step][0] = live["a"]
        if at >= 0:
            if part == 0:
                block.mlp_in = live["done"]
            elif part == 1:
                block.hidden = live["done"]
            else:
                stream = live["done"]
        at = step - 1
        if 0 <= at < chunks:
            pieces[at][1], pieces[at][2] = live["b"], live["a2"]
        at = step - 2
        if 0 <= at < chunks:
            pieces[at][3] = live["b2"]
            column, weights[at] = 0, []
            l, members = chunk_of[at]
            for member in members:
                weights[at].append(comm.assemble(member, l, pieces[at], column))
                column += member.shape[2]
        if step == 0:
            full_biases = unpack_biases(comm.ordered(bias_mine, live["bias"], "shard"), widths)
            silu_pair = comm.ordered(silu_low, live["silu"], "shard")
            silu_pair = silu_pair.reshape(2 * seq_count, features)
            silu_mine = lax.dynamic_slice_in_dim(silu_pair, shard * owned_rows, owned_rows, 1)
            mod_part = jnp.concatenate(
                [mm(silu_mine, w_ada[l]) for l in range(layer_count)], axis=1
            )
            mod_send, mod_keep = comm.split(mod_part.reshape(2, seq_count, -1), "shard")
        elif step == 1:
            mod = (mod_keep + live["mod"]).reshape(seq_count, layer_count, ada_width)
            for l in range(layer_count):
                blocks[l] = Block(
                    mod[:, l] + full_biases[l][0], full_biases[l][1:], seq_count, length
                )
            stream = stream.astype(f32)
        elif step in (2, 3, 4):
            silu_all = jnp.concatenate([silu_all, live["every"]], 0)
        elif step == 5:
            silu_all = jnp.concatenate([silu_all] + live["every"], 0)
    silu_every = silu_all.reshape(-1, features)
    silu_owned = lax.dynamic_slice_in_dim(silu_every, shard * owned_rows, owned_rows, 1)

    units = 3 * layer_count
    first_send, keep, total, late = [[None] * units for _ in range(4)]
    done = [[None] * 4 for _ in range(units)]
    grad_mods, small = [None] * layer_count, [None] * layer_count
    mod_every, bias_sums = [None] * layer_count, [None] * layer_count
    small_from = [units - 3 * l for l in range(layer_count)]
    dh = output_grad.reshape(tokens, features)
    weight_out, ada = [None] * 4, None
    chain = None
    last_mods, last_silu = units, units + 1
    for step in range(0, units + 6):
        live = {}
        at = step - 1
        if 0 <= at < units:
            live["shard"] = swap(first_send[at], "shard")
        at = step - 2
        if 0 <= at < units:
            live["near"] = swap(late[at], "near")
        at = step - 3
        if 0 <= at < units:
            if chain is not None:
                total[at], total[at - 1] = gate((total[at], chain))
            chain = total[at] = lax.psum(total[at], "far")
        at = step - 4
        if 0 <= at < units:
            live["far"] = total[at]
        at = step - 5
        if 0 <= at < units:
            live["near_back"] = swap(done[at][0], "near")
            live["core_back"] = swap(done[at][0], "core")
        at = step - 6
        if 0 <= at < units:
            live["both_back"] = swap(done[at][1], "core")
        for l in range(layer_count):
            stage = step - small_from[l]
            if 0 <= stage < 3:
                live["small", l] = swap(small[l], ("core", "shard", "near")[stage])
            elif stage == 3:
                live["small", l] = [
                    lax.ppermute(small[l], "far", [(i, i ^ k) for i in range(4)])
                    for k in (1, 2, 3)
                ]
        if step == last_mods:
            live["mods"] = swap(jnp.stack(grad_mods), "shard")
        elif step == last_silu:
            live["silu"] = swap(silu_send, "shard")
        if step < units:
            l, part = layer_count - 1 - step // 3, step % 3
            block = blocks[l]
            w_qkv, w_out = weights[3 * l]
            w_fc1, w_fc2 = weights[3 * l + 1][0], weights[3 * l + 2][0]
            if part == 0:
                pairs = [block.back_start(dh)]
                live["next"] = block.grad_out
            elif part == 1:
                pairs = [block.back_hidden(w_fc2)]
                live["next"] = block.grad_pre
            else:
                pairs = [block.back_middle(w_fc1, w_out), block.back_attention()]
            got = swap(unit_part(pairs, (0, 1), 1 - comm.core), "core")
            if part == 0 and l == layer_count - 1:
                outputs = block.output_layer(w_fc2, bf16)
            live["send"] = unit_part(pairs, (1 - shard, 2), comm.core, got)
            keep[step] = unit_part(pairs, (shard, 2), comm.core, got)
            live["keep"] = keep[step]
            if part == 2:
                dh, grad_mods[l], sums = block.back_end(w_qkv)
                small[l] = jnp.concatenate(
                    [grad_mods[l].reshape(-1, 128), sums.reshape(-1, 128)], 0
                )
                live["next"] = (dh, small[l])
        live = gate({str(key): value for key, value in live.items()})
        if step < units:
            first_send[step], keep[step] = live["send"], live["keep"]
            if part == 0:
                block.grad_out = live["next"]
            elif part == 1:
                block.grad_pre = live["next"]
            else:
                dh, small[l] = live["next"]
        at = step - 1
        if 0 <= at < units:
            shape = (2, keep[at].shape[0] // 2, keep[at].shape[1])
            sent, kept = comm.split(keep[at].reshape(shape), "near")
            got_sent, got_kept = comm.split(live["shard"].reshape(shape), "near")
            late[at] = (sent.astype(f32) + got_sent.astype(f32)).astype(bf16)
            total[at] = (kept.astype(f32) + got_kept.astype(f32)).astype(bf16)
        at = step - 2
        if 0 <= at < units:
            total[at] = (total[at].astype(f32) + live["near"].astype(f32)).astype(bf16)
        at = step - 4
        if 0 <= at < units:
            done[at][0] = live["far"]
            if chain is total[at]:
                chain = live["far"]
        at = step - 5
        if 0 <= at < units:
            done[at][1], done[at][2] = live["near_back"], live["core_back"]
        at = step - 6
        if 0 <= at < units:
            done[at][3] = live["both_back"]
        for at in [step - 6] if step - 6 < units - 1 else []:
            if at >= 0:
                weight_out = finish(comm, done[at], at, layer_count, features, weight_out)
        mod_rows = seq_count * ada_width // 128
        bias_rows = 2 * sum(widths[1:]) // 128
        for l in range(layer_count):
            stage = step - small_from[l]
            if stage == 0:
                mod_every[l], bias_sums[l] = small[l][:mod_rows], small[l][mod_rows:]
            if 0 <= stage < 3:
                got = live[str(("small", l))]
                mod_every[l] = jnp.concatenate([mod_every[l], got[:-bias_rows]], 0)
                bias_sums[l] = (
                    bias_sums[l].astype(f32) + got[-bias_rows:].astype(f32)
                ).astype(bf16)
                small[l] = jnp.concatenate([mod_every[l], bias_sums[l]], 0)
            elif stage == 3:
                got = live[str(("small", l))]
                mod_every[l] = jnp.concatenate([mod_every[l]] + [g[:-bias_rows] for g in got], 0)
                mod_every[l] = mod_every[l].reshape(-1, ada_width)
                total_sums = bias_sums[l].astype(f32)
                for g in got:
                    total_sums = total_sums + g[-bias_rows:].astype(f32)
                bias_sums[l] = total_sums.reshape(-1)
                ada = ada_weight(silu_owned, mod_every[l], l, layer_count, ada)
        if step == last_mods:
            mods_both = comm.ordered(jnp.stack(grad_mods), live["mods"], "shard")
            silu_part = functools.reduce(
                jnp.add,
                [
                    mm_t(mods_both[:, l].reshape(2 * seq_count, ada_width), w_ada[l])
                    for l in range(layer_count)
                ],
            )
            silu_send, silu_keep = comm.split(
                silu_part.reshape(2, seq_count, owned_rows), "shard"
            )
        elif step == last_silu:
            grad_silu = comm.ordered(silu_keep, live["silu"], "shard", at=1)
            grad_silu = grad_silu.reshape(seq_count, features)
    at = units - 1
    done[at][3] = swap(done[at][1], "core")
    weight_out = finish(comm, done[at], at, layer_count, features, weight_out)
    owned = [
        owned_biases(mod_every[l], bias_sums[l], shard, widths, 2) for l in range(layer_count)
    ]
    return in_order(
        outputs.reshape(latents.shape),
        dh.reshape(latents.shape),
        silu_grad(cond_value, grad_silu),
        ada,
        [jnp.stack([o[m] for o in owned]) for m in range(5)],
        weight_out,
    )


def finish(comm, pieces, unit, layer_count, features, weight_out):
    layer, part = layer_count - 1 - unit // 3, unit % 3
    width = pieces[0].shape[1]
    qkv, out, first, second = weight_out
    if part == 0:
        second = comm.final(pieces, layer, 0, width, second)
    elif part == 1:
        first = comm.final(pieces, layer, 0, width, first)
    else:
        out = comm.final(pieces, layer, 0, features // 2, out)
        qkv = comm.final(pieces, layer, features // 2, width - features // 2, qkv)
    return [qkv, out, first, second]


def solution(mesh):
    rep, shard = mesh.shape["rep"], mesh.shape["shard"]
    core = 2 if rep % 2 == 0 else 1
    near = 2 if rep == 16 else 1
    far = rep // (core * near)
    fast = (far, near, core, shard) == (4, 2, 2, 2)
    fine = Mesh(
        np.asarray(mesh.devices).reshape(far, near, core, shard),
        ("far", "near", "core", "shard"),
    )
    every = ("far", "near", "core", "shard")
    row, row3 = P(every, None), P(every, None, None)
    bias, weight = P(None, "shard"), P(None, "shard", None)
    return jax.shard_map(
        local_fast if fast else local_plain,
        mesh=fine,
        in_specs=(
            row3, row, row3, weight, bias, weight, bias, weight, bias, weight, bias, weight, bias,
        ),
        out_specs=(
            row3, row3, row, weight, bias, weight, bias, weight, bias, weight, bias, weight, bias,
        ),
        check_vma=False,
    )
```

```python
import functools

import jax
import jax.numpy as jnp
import numpy as np
from jax import lax
from jax.experimental import pallas as pl
from jax.experimental.pallas import tpu as pltpu
from jax.sharding import Mesh
from jax.sharding import PartitionSpec as P

HEADS = 12
eps = 1e-06
f32 = jnp.float32
bf16 = jnp.bfloat16


def normalize(rows):
    centred = rows - jnp.mean(rows, axis=-1, keepdims=True)
    inverse = lax.rsqrt(jnp.mean(centred * centred, axis=-1, keepdims=True) + eps)
    return (centred * inverse, inverse)


def norm_back(upstream, normed, inverse):
    return inverse * (
        upstream
        - jnp.mean(upstream, axis=-1, keepdims=True)
        - normed * jnp.mean(upstream * normed, axis=-1, keepdims=True)
    )


def gelu_and_slope(u):
    square = u * u
    t = jnp.tanh(u * (0.7978845608028654 + 0.7978845608028654 * 0.044715 * square))
    half = 0.5 + 0.5 * t
    inner_slope = 0.7978845608028654 + 3.0 * 0.7978845608028654 * 0.044715 * square
    return u * half, half + 0.5 * u * (1.0 - t * t) * inner_slope


def mm(a, b):
    return jnp.dot(a, b, preferred_element_type=f32)


def mm_t(a, b):
    return lax.dot_general(a, b, (((1,), (1,)), ((), ())), preferred_element_type=f32)


def t_mm(a, b):
    return lax.dot_general(a, b, (((0,), (0,)), ((), ())), preferred_element_type=f32)


def pick(array, index, axis=0):
    return lax.dynamic_index_in_dim(array, index, axis, keepdims=False)


SWAP = [(0, 1), (1, 0)]
CHEAP = pl.CostEstimate(flops=1, bytes_accessed=1, transcendentals=0)
PARAMS = pltpu.CompilerParams(vmem_limit_bytes=60 * 2**20)


def swap(value, axis):
    return lax.ppermute(value, axis, SWAP)


def gate(tree):
    values, shape = jax.tree.flatten(tree)
    count = len(values)

    def nothing(*refs):
        pass

    out = pl.pallas_call(
        nothing,
        out_shape=[jax.ShapeDtypeStruct(v.shape, v.dtype) for v in values],
        in_specs=[pl.BlockSpec(memory_space=pl.ANY)] * count,
        out_specs=[pl.BlockSpec(memory_space=pl.ANY)] * count,
        input_output_aliases={i: i for i in range(count)},
        cost_estimate=CHEAP,
        compiler_params=PARAMS,
    )(*values)
    return jax.tree.unflatten(shape, out)


def call(kernel, grid, ins, outs, prefetch=(), aliases=None):
    def spec(block, index, once=False):
        if block is None:
            return pl.BlockSpec(memory_space=pl.ANY)
        if once:
            return pl.BlockSpec(block, index, pipeline_mode=pl.Buffered(1))
        return pl.BlockSpec(block, index)

    return pl.pallas_call(
        kernel,
        out_shape=[jax.ShapeDtypeStruct(shape, dtype) for shape, dtype, _, _ in outs],
        grid_spec=pltpu.PrefetchScalarGridSpec(
            num_scalar_prefetch=len(prefetch),
            grid=grid,
            in_specs=[spec(*entry[1:]) for entry in ins],
            out_specs=[spec(block, index) for _, _, block, index in outs],
        ),
        input_output_aliases=aliases or {},
        cost_estimate=CHEAP,
        compiler_params=PARAMS,
    )(*prefetch, *[entry[0] for entry in ins])


class Block:
    def __init__(self, mod, biases, seq_count, length):
        self.mod = mod.reshape(seq_count, 6, -1)
        self.biases = biases
        self.seq_count, self.length = seq_count, length
        self.features = self.mod.shape[2]

    def rows(self, array):
        return (array, (self.length, array.shape[1]), lambda s: (s, 0))

    def rows_out(self, width, dtype):
        shape = (self.seq_count * self.length, width)
        return (shape, dtype, (self.length, width), lambda s: (s, 0))

    def mods(self):
        return (self.mod, (None, 6, self.features), lambda s: (s, 0, 0))

    def sums_out(self):
        return (
            (self.seq_count, 8, self.features),
            f32,
            (None, 8, self.features),
            lambda s: (s, 0, 0),
        )

    @staticmethod
    def whole(array):
        return (array, array.shape, lambda s: (0,) * array.ndim, True)

    @staticmethod
    def columns(array, start, width):
        return (array, (array.shape[0], width), lambda s: (0, start // width), True)

    def attention(self, stream, w_attn):
        bias_qv, features = self.biases[0], self.features
        bias = jnp.concatenate(
            [bias_qv[:features], jnp.zeros((features,), f32), bias_qv[features:]]
        )[None]

        def kernel(stream_ref, mod_ref, w_ref, bias_ref, in_ref, qkv_ref):
            normed, _ = normalize(stream_ref[...])
            attn_in = (normed * (1.0 + mod_ref[1:2]) + mod_ref[0:1]).astype(bf16)
            in_ref[...] = attn_in
            qkv_ref[...] = (mm(attn_in, w_ref[...]) + bias_ref[...]).astype(bf16)

        self.stream = stream
        self.attn_in, self.qkv = call(
            kernel,
            (self.seq_count,),
            [
                self.rows(stream),
                self.mods(),
                self.columns(w_attn, 0, 3 * features),
                self.whole(bias),
            ],
            [self.rows_out(features, bf16), self.rows_out(3 * features, bf16)],
        )
        self.attn_out = attention_forward(self.qkv, self.seq_count)

    def project(self, w_attn):
        def kernel(out_ref, stream_ref, mod_ref, w_ref, bias_ref, branch_ref, middle_ref, in_ref):
            branch = mm(out_ref[...], w_ref[...]) + bias_ref[...]
            middle = stream_ref[...] + mod_ref[2:3] * branch
            normed, _ = normalize(middle)
            branch_ref[...] = branch
            middle_ref[...] = middle
            in_ref[...] = (normed * (1.0 + mod_ref[4:5]) + mod_ref[3:4]).astype(bf16)

        self.branch, self.middle, self.mlp_in = call(
            kernel,
            (self.seq_count,),
            [
                self.rows(self.attn_out),
                self.rows(self.stream),
                self.mods(),
                self.columns(w_attn, 3 * self.features, self.features),
                self.whole(self.biases[1][None]),
            ],
            [
                self.rows_out(self.features, f32),
                self.rows_out(self.features, f32),
                self.rows_out(self.features, bf16),
            ],
        )

    def hidden_layer(self, w_fc1):
        hidden, tile, tokens = w_fc1.shape[1], self.features, self.seq_count * self.length
        tile = tile // 2

        def kernel(in_ref, w_ref, bias_ref, slope_ref, hidden_ref):
            value, slope = gelu_and_slope(mm(in_ref[...], w_ref[...]) + bias_ref[...])
            slope_ref[...] = slope.astype(bf16)
            hidden_ref[...] = value.astype(bf16)

        out = ((tokens, hidden), bf16, (tokens, tile), lambda j: (0, j))
        self.slope, self.hidden = call(
            kernel,
            (hidden // tile,),
            [
                (self.mlp_in, (tokens, self.features), lambda j: (0, 0)),
                (w_fc1, (self.features, tile), lambda j: (0, j)),
                (self.biases[2][None], (1, tile), lambda j: (0, j)),
            ],
            [out, out],
        )

    def output_layer(self, w_fc2, dtype):
        def kernel(hidden_ref, middle_ref, mod_ref, w_ref, bias_ref, output_ref, stream_ref):
            output = mm(hidden_ref[...], w_ref[...]) + bias_ref[...]
            output_ref[...] = output
            stream_ref[...] = (middle_ref[...] + mod_ref[5:6] * output).astype(dtype)

        self.output, stream = call(
            kernel,
            (self.seq_count,),
            [
                self.rows(self.hidden),
                self.rows(self.middle),
                self.mods(),
                self.whole(w_fc2),
                self.whole(self.biases[3][None]),
            ],
            [self.rows_out(self.features, f32), self.rows_out(self.features, dtype)],
        )
        return stream

    def back_start(self, dh):
        def kernel(dh_ref, mod_ref, grad_ref, sums_ref):
            grad_out = (mod_ref[5:6] * dh_ref[...].astype(f32)).astype(bf16)
            grad_ref[...] = grad_out
            sums_ref[0:1] = jnp.sum(grad_out.astype(f32), axis=0, keepdims=True)

        self.dh = dh
        self.grad_out, self.sums_out2 = call(
            kernel,
            (self.seq_count,),
            [self.rows(dh), self.mods()],
            [self.rows_out(self.features, bf16), self.sums_out()],
        )
        return (self.hidden, self.grad_out)

    def back_hidden(self, w_fc2):
        hidden, tile, tokens = w_fc2.shape[0], self.features, self.seq_count * self.length

        def kernel(grad_ref, slope_ref, w_ref, out_ref, sum_ref):
            grad_hidden = mm_t(grad_ref[...], w_ref[...])
            grad_pre = (grad_hidden * slope_ref[...].astype(f32)).astype(bf16)
            out_ref[...] = grad_pre
            sum_ref[...] = jnp.sum(grad_pre.astype(f32), axis=0, keepdims=True)

        self.grad_pre, self.sum_fc1 = call(
            kernel,
            (hidden // tile,),
            [
                (self.grad_out, (tokens, self.features), lambda j: (0, 0)),
                (self.slope, (tokens, tile), lambda j: (0, j)),
                (w_fc2, (tile, self.features), lambda j: (j, 0)),
            ],
            [
                ((tokens, hidden), bf16, (tokens, tile), lambda j: (0, j)),
                ((1, hidden), f32, (1, tile), lambda j: (0, j)),
            ],
        )
        return (self.mlp_in, self.grad_pre)

    def back_middle(self, w_fc1, w_attn):
        def kernel(
            grad_ref, w1_ref, dh_ref, middle_ref, mod_ref, branch_ref, wo_ref,
            mid_ref, gb_ref, ga_ref, sums_ref,
        ):
            grad_in = mm_t(grad_ref[...], w1_ref[...])
            normed, inverse = normalize(middle_ref[...])
            dh = dh_ref[...].astype(f32)
            mid = dh + norm_back(grad_in * (1.0 + mod_ref[4:5]), normed, inverse)
            grad_branch = (mod_ref[2:3] * mid).astype(bf16)
            mid_ref[...] = mid
            gb_ref[...] = grad_branch
            ga_ref[...] = mm_t(grad_branch, wo_ref[...]).astype(bf16)
            for at, value in enumerate(
                (
                    mid * branch_ref[...],
                    grad_in,
                    grad_in * normed,
                    grad_branch.astype(f32),
                )
            ):
                sums_ref[at : at + 1] = jnp.sum(value, axis=0, keepdims=True)

        self.grad_mid, self.grad_branch, self.grad_attn, self.sums_mid = call(
            kernel,
            (self.seq_count,),
            [
                self.rows(self.grad_pre),
                self.whole(w_fc1),
                self.rows(self.dh),
                self.rows(self.middle),
                self.mods(),
                self.rows(self.branch),
                self.columns(w_attn, 3 * self.features, self.features),
            ],
            [
                self.rows_out(self.features, f32),
                self.rows_out(self.features, bf16),
                self.rows_out(self.features, bf16),
                self.sums_out(),
            ],
        )
        return (self.attn_out, self.grad_branch)

    def gate_sum(self):
        def kernel(dh_ref, output_ref, sums_ref):
            product = dh_ref[...].astype(f32) * output_ref[...]
            sums_ref[0:1] = jnp.sum(product, axis=0, keepdims=True)

        self.sums_gate = call(
            kernel,
            (self.seq_count,),
            [self.rows(self.dh), self.rows(self.output)],
            [self.sums_out()],
        )[0]

    def back_attention(self):
        self.grad_qkv = attention_backward(self.qkv, self.grad_attn, self.seq_count)
        return (self.attn_in, self.grad_qkv)

    def back_end(self, w_attn):
        features = self.features

        def kernel(grad_ref, w_ref, stream_ref, mod_ref, mid_ref, dh_ref, sums_ref):
            grad_qkv = grad_ref[...]
            grad_in = mm_t(grad_qkv, w_ref[...])
            normed, inverse = normalize(stream_ref[...].astype(f32))
            dh_ref[...] = mid_ref[...] + norm_back(
                grad_in * (1.0 + mod_ref[1:2]), normed, inverse
            )
            for at, value in enumerate((grad_in, grad_in * normed)):
                sums_ref[at : at + 1] = jnp.sum(value, axis=0, keepdims=True)
            for part in range(3):
                columns = grad_qkv[:, part * features : (part + 1) * features].astype(f32)
                sums_ref[2 + part : 3 + part] = jnp.sum(columns, axis=0, keepdims=True)

        dh, self.sums_end = call(
            kernel,
            (self.seq_count,),
            [
                self.rows(self.grad_qkv),
                self.columns(w_attn, 0, 3 * features),
                self.rows(self.stream),
                self.mods(),
                self.rows(self.grad_mid),
            ],
            [self.rows_out(features, f32), self.sums_out()],
        )
        return dh

    def back_sums(self):
        features, sums = self.features, self.sums_end
        grad_mod = jnp.concatenate(
            [sums[:, 0:2], self.sums_mid[:, 0:3], self.sums_gate[:, 0:1]], axis=1
        )
        grad_mod = grad_mod.reshape(self.seq_count, 6 * features).astype(bf16)
        totals = jnp.sum(sums, axis=0)
        bias_sums = jnp.concatenate(
            [
                totals[2],
                totals[4],
                jnp.sum(self.sums_mid[:, 3], axis=0),
                self.sum_fc1[0],
                jnp.sum(self.sums_out2[:, 0], axis=0),
            ]
        ).astype(bf16)
        return grad_mod, bias_sums


def probs_of(q, k, factor):
    scores = mm_t(q, k) * factor
    raised = jnp.exp(scores - jnp.max(scores, axis=-1, keepdims=True))
    return raised * (1.0 / jnp.sum(raised, axis=-1, keepdims=True))


def head_masks(rows, head):
    lane = lax.broadcasted_iota(jnp.int32, (rows, 128), 1)
    return [jnp.logical_and(lane >= at, lane < at + head) for at in range(0, 128, head)]


def attention_forward(qkv, count):
    tokens, triple = qkv.shape
    width, length, head = triple // 3, tokens // count, triple // 3 // HEADS
    tile = 384 if width % 384 == 0 else width
    steps = width // tile
    factor = head ** (-0.5)

    def kernel(q_ref, k_ref, v_ref, out_ref):
        for start in range(0, tile, 128):
            group = slice(start, start + 128)
            q, k, v = q_ref[:, group], k_ref[:, group], v_ref[:, group]
            total = jnp.zeros((length, 128), f32)
            for mask in head_masks(length, head):
                probs = probs_of(jnp.where(mask, q, 0), k, factor).astype(bf16)
                total = total + mm(probs, jnp.where(mask, v, 0))
            out_ref[:, group] = total.astype(bf16)

    def part(which):
        return (qkv, (length, tile), lambda s, g: (s, which * steps + g))

    return call(
        kernel,
        (count, steps),
        [part(0), part(1), part(2)],
        [((tokens, width), bf16, (length, tile), lambda s, g: (s, g))],
    )[0]


def attention_backward(qkv, grad, count):
    tokens, triple = qkv.shape
    width, length, head = triple // 3, tokens // count, triple // 3 // HEADS
    tile = 384 if width % 384 == 0 else width
    steps = width // tile
    factor = head ** (-0.5)

    def kernel(q_ref, k_ref, v_ref, g_ref, out_ref):
        for start in range(0, tile, 128):
            group = slice(start, start + 128)
            q, k, v, g = q_ref[:, group], k_ref[:, group], v_ref[:, group], g_ref[:, group]
            grad_q = jnp.zeros((length, 128), f32)
            grad_k = jnp.zeros((length, 128), f32)
            grad_v = jnp.zeros((length, 128), f32)
            for mask in head_masks(length, head):
                own_q, own_g = jnp.where(mask, q, 0), jnp.where(mask, g, 0)
                probs = probs_of(own_q, k, factor)
                grad_probs = mm_t(own_g, v)
                row_terms = jnp.sum(grad_probs * probs, axis=-1, keepdims=True)
                grad_scores = (probs * (grad_probs - row_terms)).astype(bf16)
                grad_q = grad_q + mm(grad_scores, jnp.where(mask, k, 0))
                grad_k = grad_k + t_mm(grad_scores, own_q)
                grad_v = grad_v + t_mm(probs.astype(bf16), own_g)
            at = pl.program_id(1) * tile + start
            for part, value in enumerate((grad_q * factor, grad_k * factor, grad_v)):
                columns = pl.ds(pl.multiple_of(part * width + at, 128), 128)
                out_ref[:, columns] = value.astype(bf16)

    def part(which):
        return (qkv, (length, tile), lambda s, g: (s, which * steps + g))

    return call(
        kernel,
        (count, steps),
        [part(0), part(1), part(2), (grad, (length, tile), lambda s, g: (s, g))],
        [((tokens, triple), bf16, (length, triple), lambda s, g: (s, 0))],
    )[0]


TILE = 384


def product_part(lhs, rhs, col_half, into, at, width):
    tokens, rows = lhs.shape
    half = rhs.shape[1] // 2
    tile = TILE if half > 1024 else 2 * TILE
    shift = at // half
    place = jnp.asarray(col_half, jnp.int32).reshape(1)
    ins = [
        (lhs, (tokens, tile), lambda i, p: (0, i)),
        (rhs, (tokens, half), lambda i, p: (0, p[0])),
    ]
    aliases = {}
    if into is not None:
        aliases = {3: 0}
        ins.append((into, None, None))

    def kernel(place_ref, lhs_ref, rhs_ref, *refs):
        refs[-1][...] = t_mm(lhs_ref[...], rhs_ref[...]).astype(bf16)

    return call(
        kernel,
        (rows // tile,),
        ins,
        [((rows, width), bf16, (tile, half), lambda i, p: (i, shift))],
        prefetch=(place,),
        aliases=aliases,
    )[0]


def product_sums(lhs, rhs, shard, col_half, got, into, at, width):
    tokens, rows = lhs.shape
    half = rhs.shape[1] // 2
    tile = min(TILE if half > 1024 else 2 * TILE, rows // 2)
    tiles, shift = rows // 2 // tile, at // half
    place = jnp.stack([shard, col_half]).astype(jnp.int32)

    def row_tile(side, i, p):
        return jnp.where(side == 0, 1 - p[0], p[0]) * tiles + i

    ins = [
        (lhs, (tokens, tile), lambda side, i, p: (0, row_tile(side, i, p))),
        (rhs, (tokens, half), lambda side, i, p: (0, p[1])),
        (got, (tile, half), lambda side, i, p: (row_tile(side, i, p), shift)),
    ]
    aliases = {}
    if into is not None:
        aliases = {4: 0, 5: 1}
        ins += [(part, None, None) for part in into]

    def kernel(place_ref, lhs_ref, rhs_ref, got_ref, *refs):
        send_ref, keep_ref = refs[-2:]
        total = t_mm(lhs_ref[...], rhs_ref[...]) + got_ref[...].astype(f32)

        @pl.when(pl.program_id(0) == 0)
        def _():
            send_ref[...] = total.astype(bf16)

        @pl.when(pl.program_id(0) == 1)
        def _():
            keep_ref[...] = total.astype(bf16)

    shape = (rows // 2, width)
    return call(
        kernel,
        (2, tiles),
        ins,
        [
            (shape, bf16, (tile, half), lambda s, i, p: (jnp.where(s == 0, i, tiles - 1), shift)),
            (shape, bf16, (tile, half), lambda s, i, p: (jnp.where(s == 0, 0, i), shift)),
        ],
        prefetch=(place,),
        aliases=aliases,
    )


def unit_part(pairs, col_half):
    width = sum(rhs.shape[1] // 2 for _, rhs in pairs)
    out, at = None, 0
    for lhs, rhs in pairs:
        out = product_part(lhs, rhs, col_half, out, at, width)
        at += rhs.shape[1] // 2
    return out


def unit_sums(pairs, shard, col_half, got):
    width = sum(rhs.shape[1] // 2 for _, rhs in pairs)
    out, at = None, 0
    for lhs, rhs in pairs:
        out = product_sums(lhs, rhs, shard, col_half, got, out, at, width)
        at += rhs.shape[1] // 2
    return out


class Fast:
    def __init__(self):
        self.near = lax.axis_index("near")
        self.core = lax.axis_index("core")
        self.shard = lax.axis_index("shard")
        self.place = jnp.stack([self.shard, self.near, self.core]).astype(jnp.int32)

    def ordered(self, mine, got, axis, at=0):
        first = lax.axis_index(axis) == 0
        return jnp.stack([jnp.where(first, mine, got), jnp.where(first, got, mine)], axis=at)

    def split(self, stack, axis, at=0):
        me = lax.axis_index(axis)
        return pick(stack, 1 - me, at), pick(stack, me, at)

    def quarter(self, stacked, layer):
        size = stacked.shape[1] // 4
        start = (self.near * 2 + self.core) * size
        return lax.dynamic_slice(stacked, (layer, start, 0), (1, size, stacked.shape[2]))[0]

    def assemble_own(self, members, layer, place):
        rows = members[0].shape[1]
        widths = [member.shape[2] for member in members]
        size = rows // 4

        def kernel(place_ref, *refs):
            at = 0
            for member_ref, member_width in zip(refs, widths):
                refs[-1][:, at : at + member_width] = member_ref[...]
                at += member_width

        ins = [
            (member, (None, size, member.shape[2]), lambda s, p: (layer, s, 0))
            for member in members
        ]
        shape = (2 * rows, sum(widths))
        block = (size, sum(widths))
        return call(
            kernel,
            (4,),
            ins,
            [(shape, members[0].dtype, block, lambda s, p: (p[0] * 4 + s, 0))],
            prefetch=(place,),
        )[0]

    def assemble_rest(self, whole, pieces):
        size, width = pieces[0].shape

        def out_block(piece, place):
            shard, near, core = place[0], place[1], place[2]
            near_at = jnp.where(piece % 2 == 0, near, 1 - near)
            core_at = jnp.where(piece < 2, core, 1 - core)
            return (1 - shard) * 4 + near_at * 2 + core_at, 0

        def kernel(place_ref, *refs):
            for at in range(4):

                @pl.when(pl.program_id(0) == at)
                def _(value=refs[at]):
                    refs[-1][...] = value[...]

        ins = [(piece, (size, width), lambda s, p: (0, 0)) for piece in pieces]
        ins.append((whole, None, None))
        return call(
            kernel,
            (4,),
            ins,
            [(whole.shape, whole.dtype, (size, width), out_block)],
            prefetch=(self.place,),
            aliases={5: 0},
        )[0]

    def final(self, mine, got, layer, column, width, into):
        rows = mine.shape[1]
        tile = width if column % width == 0 else TILE
        tiles, shift = width // tile, column // tile

        def out_block(j, piece, place):
            near, core = place[1], place[2]
            near_at = jnp.where(piece % 2 == 0, near, 1 - near)
            core_at = jnp.where(piece < 2, core, 1 - core)
            return layer, near_at, core_at * tiles + j

        def kernel(place_ref, mine_ref, got_ref, *refs):
            piece, out_ref = pl.program_id(1), refs[-1]

            @pl.when(piece < 2)
            def _():
                out_ref[...] = mine_ref[...].astype(f32)

            @pl.when(piece >= 2)
            def _():
                out_ref[...] = got_ref[...].astype(f32)

        block = (None, rows, tile)
        ins = [
            (mine, block, lambda j, i, p: (jnp.minimum(i, 1), 0, shift + j)),
            (got, block, lambda j, i, p: (jnp.maximum(i - 2, 0), 0, shift + j)),
        ]
        aliases = {}
        if into is not None:
            aliases = {3: 0}
            ins.append((into, None, None))
        return call(
            kernel,
            (tiles, 4),
            ins,
            [((2, 2 * rows, 2 * width), f32, (None, rows, tile), out_block)],
            prefetch=(self.place,),
            aliases=aliases,
        )[0]

    def far_swap(self, value, name):
        step = 1 if name == "z1" else 2
        return lax.ppermute(value, "far", [(i, i ^ step) for i in range(4)])

    def any_swap(self, value, name):
        return self.far_swap(value, name) if name in ("z1", "z2") else swap(value, name)


def ada_weight(silu, mods, start, width, layer, layers, into, place):
    count, rows = silu[1]
    tile = 768 if width % 768 == 0 and start % 768 == 0 else width
    first = start // tile

    def kernel(place_ref, silu_ref, mods_ref, *refs):
        refs[-1][...] = t_mm(silu_ref[...], mods_ref[...])

    ins = [silu, (mods, (count, tile), lambda j, p: (0, first + j))]
    aliases = {}
    if into is not None:
        aliases = {3: 0}
        ins.append((into, None, None))
    return call(
        kernel,
        (width // tile,),
        ins,
        [((layers, rows, width), f32, (None, rows, tile), lambda j, p: (layer, 0, j))],
        prefetch=(place,),
        aliases=aliases,
    )[0]


def add(a, b):
    return (a.astype(f32) + b.astype(f32)).astype(bf16)


def silu_grad(cond_value, grad_silu):
    _, silu_pull = jax.vjp(jax.nn.silu, cond_value)
    return silu_pull(grad_silu)[0]


def owned_biases(mod_every, bias_sums, shard, widths, shard_count):
    totals, at = [jnp.sum(mod_every.astype(f32), axis=0)], 0
    for width in widths[1:]:
        totals.append(bias_sums[at : at + width * shard_count])
        at += width * shard_count
    return [
        lax.dynamic_slice_in_dim(total, shard * width, width, 0)
        for total, width in zip(totals, widths)
    ]


def unpack_biases(bias_all, widths):
    cuts = np.cumsum(widths)[:-1]
    parts = [
        jnp.moveaxis(part, 0, 1).reshape(bias_all.shape[1], -1).astype(f32)
        for part in jnp.split(bias_all, cuts, axis=2)
    ]
    return [[part[l] for part in parts] for l in range(bias_all.shape[1])]


def in_order(outputs, dh, condition_grad, g_w_ada, biases, weights):
    return (
        outputs,
        dh,
        condition_grad,
        g_w_ada,
        biases[0],
        weights[0],
        biases[1],
        weights[1],
        biases[2],
        weights[2],
        biases[3],
        weights[3],
        biases[4],
    )


def local_plain(
    latents,
    condition,
    output_grad,
    w_ada,
    b_ada,
    query_key_value_weight,
    b_qv,
    output_matrix_weight,
    b_proj,
    first_linear_weight,
    b_fc1,
    second_linear_weight,
    b_fc2,
):
    layer_count, owned_rows, ada_width = w_ada.shape
    seq_count, length, features = latents.shape
    shard, shards = lax.axis_index("shard"), lax.axis_size("shard")
    every = ("far", "near", "core", "shard")
    biases = (b_ada, b_qv, b_proj, b_fc1, b_fc2)
    widths = [b.shape[1] for b in biases]

    cond_value = condition.astype(f32)
    silu_low = jax.nn.silu(cond_value).astype(bf16)
    silu_group = lax.all_gather(silu_low, "shard", axis=0, tiled=True)
    silu_mine = lax.dynamic_slice_in_dim(silu_group, shard * owned_rows, owned_rows, 1)
    bias_all = lax.all_gather(jnp.concatenate(biases, axis=1), "shard", axis=0)
    full_biases = unpack_biases(bias_all, widths)
    mod_part = jnp.concatenate([mm(silu_mine, w_ada[l]) for l in range(layer_count)], axis=1)
    mod = lax.psum_scatter(mod_part, "shard", scatter_dimension=0, tiled=True)
    mod = mod.reshape(seq_count, layer_count, ada_width)
    silu_every = lax.all_gather(silu_low, every, axis=0, tiled=True)

    tokens = seq_count * length
    stream, blocks, weights = latents.astype(f32).reshape(tokens, features), [], []
    for l in range(layer_count):
        block = Block(mod[:, l] + full_biases[l][0], full_biases[l][1:], seq_count, length)
        full = [
            lax.all_gather(w[l], "shard", axis=0, tiled=True)
            for w in (
                query_key_value_weight,
                output_matrix_weight,
                first_linear_weight,
                second_linear_weight,
            )
        ]
        full[:2] = [jnp.concatenate(full[:2], axis=1)]
        block.attention(stream, full[0])
        block.project(full[0])
        block.hidden_layer(full[1])
        stream = block.output_layer(full[2], bf16 if l == layer_count - 1 else f32)
        blocks.append(block)
        weights.append(full)

    def reduce(pair):
        grad = t_mm(*pair).astype(bf16)
        grad = lax.psum_scatter(grad, "shard", scatter_dimension=0, tiled=True)
        return lax.psum(grad, ("far", "near", "core")).astype(f32)

    dh = output_grad.reshape(tokens, features)
    grads, ada, owned, grad_silu = [None] * layer_count, None, [None] * layer_count, 0.0
    silu_owned = lax.dynamic_slice_in_dim(silu_every, shard * owned_rows, owned_rows, 1)
    for l in reversed(range(layer_count)):
        block, full = blocks[l], weights[l]
        second = block.back_start(dh)
        first = block.back_hidden(full[2])
        out = block.back_middle(full[1], full[0])
        qkv = block.back_attention()
        dh = block.back_end(full[0])
        block.gate_sum()
        grad_mod, bias_sums = block.back_sums()
        grads[l] = [reduce(pair) for pair in (qkv, out, first, second)]
        mod_every = lax.all_gather(grad_mod, every, axis=0, tiled=True)
        silu = (silu_owned, silu_owned.shape, lambda j, p: (0, 0))
        place = jnp.zeros((1,), jnp.int32)
        ada = ada_weight(silu, mod_every, 0, ada_width, l, layer_count, ada, place)
        sums = lax.psum(bias_sums.astype(f32), every)
        owned[l] = owned_biases(mod_every, sums, shard, widths, shards)
        mods_group = lax.all_gather(grad_mod, "shard", axis=0, tiled=True)
        grad_silu = grad_silu + mm_t(mods_group, w_ada[l])
    by_owner = grad_silu.reshape(shards, seq_count, owned_rows)
    got = lax.all_to_all(by_owner, "shard", 0, 0)
    grad_silu = jnp.moveaxis(got, 0, 1).reshape(seq_count, features)
    return in_order(
        stream.reshape(latents.shape),
        dh.reshape(latents.shape),
        silu_grad(cond_value, grad_silu),
        ada,
        [jnp.stack([o[m] for o in owned]) for m in range(5)],
        [jnp.stack([g[m] for g in grads]) for m in range(4)],
    )


def local_fast(
    latents,
    condition,
    output_grad,
    w_ada,
    b_ada,
    query_key_value_weight,
    b_qv,
    output_matrix_weight,
    b_proj,
    first_linear_weight,
    b_fc1,
    second_linear_weight,
    b_fc2,
):
    comm = Fast()
    layer_count, owned_rows, ada_width = w_ada.shape
    seq_count, length, features = latents.shape
    tokens = seq_count * length
    shard = comm.shard
    biases = (b_ada, b_qv, b_proj, b_fc1, b_fc2)
    widths = [b.shape[1] for b in biases]

    chunk_of = []
    for l in range(layer_count):
        chunk_of.append((l, (query_key_value_weight, output_matrix_weight)))
        chunk_of.append((l, (first_linear_weight,)))
        chunk_of.append((l, (second_linear_weight,)))
    chunks = len(chunk_of)
    sends = []
    for l, members in chunk_of:
        quarters = [comm.quarter(member, l) for member in members]
        sends.append(quarters[0] if len(quarters) == 1 else jnp.concatenate(quarters, axis=1))

    cond_value = condition.astype(f32)
    silu_low = jax.nn.silu(cond_value).astype(bf16)
    bias_mine = jnp.concatenate(biases, axis=1)
    latents_flat = latents.reshape(tokens, features)
    stream = latents_flat
    pieces = [[None] * 4 for _ in range(chunks)]
    weights = [None] * chunks
    blocks = [None] * layer_count
    outputs, place = None, comm.place + 0
    for step in range(0, chunks + 2):
        live = {}
        if step < chunks:
            live["a"] = swap(sends[step], "shard")
        at = step - 1
        if 0 <= at < chunks:
            live["b"] = swap(pieces[at][0], "near")
            live["a2"] = swap(pieces[at][0], "core")
        at = step - 2
        if 0 <= at < chunks:
            live["b2"] = swap(pieces[at][1], "core")
        if step == 0:
            live["silu"] = swap(silu_low, "shard")
            live["bias"] = swap(bias_mine, "shard")
        elif step == 2:
            live["mod"] = swap(mod_send, "shard")
        at = step - 3
        if at >= 0:
            l, part = at // 3, at % 3
            block = blocks[l]
            if part == 0:
                block.attention(stream, weights[at])
                block.project(weights[at])
                live["done"] = block.mlp_in
            elif part == 1:
                block.hidden_layer(weights[at])
                live["done"] = block.hidden
            else:
                stream = block.output_layer(weights[at], f32)
                live["done"] = stream
        if step + 1 < chunks:
            live["send"] = sends[step + 1]
        early = range(2 * step, min(2 * step + 2, chunks))
        live["own"] = [
            comm.assemble_own(chunk_of[k][1], chunk_of[k][0], place) for k in early
        ]
        if early:
            live["place"] = place
        if step == 1:
            live["mod_send"], live["mod_keep"] = mod_send, mod_keep
        live = gate(live)
        for k, own in zip(early, live["own"]):
            weights[k] = own
        place = live.get("place")
        if step + 1 < chunks:
            sends[step + 1] = live["send"]
        if step < chunks:
            pieces[step][0] = live["a"]
        if at >= 0:
            if part == 0:
                block.mlp_in = live["done"]
            elif part == 1:
                block.hidden = live["done"]
            else:
                stream = live["done"]
        at = step - 1
        if 0 <= at < chunks:
            pieces[at][1], pieces[at][2] = live["b"], live["a2"]
        at = step - 2
        if 0 <= at < chunks:
            pieces[at][3] = live["b2"]
            weights[at] = comm.assemble_rest(weights[at], pieces[at])
        if step == 0:
            full_biases = unpack_biases(comm.ordered(bias_mine, live["bias"], "shard"), widths)
            silu_pair = comm.ordered(silu_low, live["silu"], "shard")
            silu_pair = silu_pair.reshape(2 * seq_count, features)
            silu_mine = lax.dynamic_slice_in_dim(silu_pair, shard * owned_rows, owned_rows, 1)
            mod_part = jnp.concatenate(
                [mm(silu_mine, w_ada[l]) for l in range(layer_count)], axis=1
            )
            mod_send, mod_keep = comm.split(mod_part.reshape(2, seq_count, -1), "shard")
        elif step == 1:
            mod_send, mod_keep = live["mod_send"], live["mod_keep"]
        elif step == 2:
            mod = (mod_keep + live["mod"]).reshape(seq_count, layer_count, ada_width)
            for l in range(layer_count):
                blocks[l] = Block(
                    mod[:, l] + full_biases[l][0], full_biases[l][1:], seq_count, length
                )
            stream = stream.astype(f32)

    units = 3 * layer_count
    last_step = units + 5
    pairs, core_send, first_send, keep, late, total, back, both = [
        [None] * units for _ in range(8)
    ]
    grad_mods = [None] * layer_count
    packed, bias_sums, ada = None, None, None
    bias_width = 2 * sum(widths[1:])
    packed_width = layer_count * ada_width + features
    small_plan = {
        (units + 1, 0): "core",
        (units + 1, 1): "shard",
        (units + 2, 0): "near",
        (units + 2, 1): "z1",
        (units + 3, 0): "z2",
    }
    dh = output_grad.reshape(tokens, features)
    next_in = dh
    weight_out, arrived = [None] * 4, None
    for step in range(0, last_step + 1):

        def unit_at(lag):
            return step - lag if 0 <= step - lag < units else None

        on_core, on_shard, on_near = unit_at(1), unit_at(2), unit_at(3)
        on_far, on_back, on_end = unit_at(4), unit_at(5), unit_at(6)
        live, fin = {}, {}
        if arrived is not None:
            weight_out = finish(comm, *arrived, layer_count, features, weight_out)
            live["finals"], arrived = weight_out, None
        if on_core is not None:
            live["core"] = swap(core_send[on_core], "core")
        if on_shard is not None:
            fin["shard"] = swap(first_send[on_shard], "shard")
        if on_near is not None:
            fin["near"] = swap(late[on_near], "near")
        if on_far is not None:
            fin["far"] = lax.psum(total[on_far], "far")
        if on_back is not None:
            fin["back"] = swap(back[on_back], "near")
        if on_end is not None:
            fin["end"] = swap(both[on_end], "core")
        if (step, 0) in small_plan:
            live["small"] = comm.any_swap(packed, small_plan[step, 0])
        if step == units + 3:
            live["silu"] = swap(silu_send, "shard")
        if on_core is not None:
            got, next_in = gate((live.pop("core"), next_in))
            if on_core % 3 < 2:
                pairs[on_core] = [(pairs[on_core][0][0], next_in)]
            live["made"] = tuple(unit_sums(pairs[on_core], shard, comm.core, got))
        if step < units:
            l, part = layer_count - 1 - step // 3, step % 3
            block = blocks[l]
            w_attn, w_fc1, w_fc2 = weights[3 * l : 3 * l + 3]
            if part == 0:
                pairs[step] = [block.back_start(next_in)]
                next_in = block.grad_out
            elif part == 1:
                block.grad_out = next_in
                pairs[step] = [block.back_hidden(w_fc2)]
                next_in = block.grad_pre
            else:
                block.grad_pre = next_in
                middle = block.back_middle(w_fc1, w_attn)
                next_in = block.grad_attn
            live["next"] = next_in
        sums_of = None
        if step == units // 2:
            sums_of = layer_count - 1
            outputs = blocks[sums_of].output_layer(weights[3 * sums_of + 2], bf16)
            fin["outputs"] = outputs
        elif step == units:
            sums_of = 0
        if sums_of is not None:
            blocks[sums_of].gate_sum()
            grad_mods[sums_of], bias_mine = blocks[sums_of].back_sums()
            fin["sums"] = grad_mods[sums_of], bias_mine
        live = gate(live) if live else live
        if "finals" in live:
            weight_out = live["finals"]
        if on_core is not None:
            first_send[on_core], keep[on_core] = live["made"]
        if "small" in live:
            packed = pack(packed, live["small"])
        if step == units + 3:
            grad_silu = comm.ordered(silu_keep, live["silu"], "shard", at=1)
            grad_silu = grad_silu.reshape(seq_count, features)
            count = packed.shape[0] - 1
            every = packed[:count].reshape(count * seq_count, packed_width)
            owned = [
                owned_biases(
                    every[:, l * ada_width : (l + 1) * ada_width],
                    packed[count, l, :bias_width].astype(f32),
                    shard,
                    widths,
                    2,
                )
                for l in range(layer_count)
            ]
            silu_block = (every.shape[0], owned_rows)
            silu_at = layer_count * ada_width // owned_rows
            for l in range(layer_count):
                ada = ada_weight(
                    (every, silu_block, lambda j, p: (0, silu_at + p[0])),
                    every,
                    l * ada_width,
                    ada_width,
                    l,
                    layer_count,
                    ada,
                    comm.place,
                )
            fin["ada"] = ada
        if (step, 1) in small_plan:
            fin["small"] = comm.any_swap(packed, small_plan[step, 1])
        if step == units + 2:
            fin["mods"] = swap(jnp.stack(grad_mods), "shard")
        if step < units:
            next_in = live["next"]
            if part < 2:
                pairs[step] = [(pairs[step][0][0], next_in)]
            else:
                block.grad_attn = next_in
                pairs[step] = [block.back_attention(), middle]
                dh = block.back_end(w_attn)
                next_in = dh
            fin["next"] = next_in
            fin["send"] = unit_part(pairs[step], 1 - comm.core)
        if step == last_step:
            live = fin
        else:
            live = gate(fin)
        if step < units:
            core_send[step], next_in = live["send"], live["next"]
            if part < 2:
                pairs[step] = [(pairs[step][0][0], next_in)]
            else:
                dh = next_in
        if on_shard is not None:
            shape = (2, keep[on_shard].shape[0] // 2, keep[on_shard].shape[1])
            sent, kept = comm.split(keep[on_shard].reshape(shape), "near")
            got_sent, got_kept = comm.split(live["shard"].reshape(shape), "near")
            late[on_shard], total[on_shard] = add(sent, got_sent), add(kept, got_kept)
        if on_near is not None:
            total[on_near] = add(total[on_near], live["near"])
        if on_far is not None:
            back[on_far] = live["far"]
        if on_back is not None:
            both[on_back] = jnp.stack([back[on_back], live["back"]])
        if on_end is not None:
            arrived = both[on_end], live["end"], on_end
        if "ada" in live:
            ada = live["ada"]
        if "outputs" in live:
            outputs = live["outputs"]
        if sums_of is not None:
            grad_mods[sums_of], bias_mine = live["sums"]
            bias_sums = [bias_mine] + (bias_sums or [])
        if sums_of == 0:
            filler = jnp.zeros((layer_count, packed_width - bias_width), bf16)
            packed = jnp.stack(
                [
                    jnp.concatenate(grad_mods + [silu_low], axis=1),
                    jnp.concatenate([jnp.stack(bias_sums), filler], axis=1),
                ]
            )
        if "small" in live:
            packed = pack(packed, live["small"])
        if step == units + 2:
            mods_both = comm.ordered(jnp.stack(grad_mods), live["mods"], "shard")
            silu_part = functools.reduce(
                jnp.add,
                [
                    mm_t(mods_both[:, l].reshape(2 * seq_count, ada_width), w_ada[l])
                    for l in range(layer_count)
                ],
            )
            silu_send, silu_keep = comm.split(
                silu_part.reshape(2, seq_count, owned_rows), "shard"
            )
    weight_out = finish(comm, *arrived, layer_count, features, weight_out)
    return in_order(
        outputs.reshape(latents.shape),
        dh.reshape(latents.shape),
        silu_grad(cond_value, grad_silu),
        ada,
        [jnp.stack([o[m] for o in owned]) for m in range(5)],
        weight_out,
    )


def pack(mine, got):
    count = mine.shape[0] - 1
    return jnp.concatenate([mine[:count], got[:count], add(mine[count:], got[count:])], 0)


def finish(comm, mine, got, unit, layer_count, features, weight_out):
    layer, part = layer_count - 1 - unit // 3, unit % 3
    width = mine.shape[2]
    qkv, out, first, second = weight_out
    if part == 0:
        second = comm.final(mine, got, layer, 0, width, second)
    elif part == 1:
        first = comm.final(mine, got, layer, 0, width, first)
    else:
        qkv = comm.final(mine, got, layer, 0, width - features // 2, qkv)
        out = comm.final(mine, got, layer, width - features // 2, features // 2, out)
    return [qkv, out, first, second]


def solution(mesh):
    rep, shard = mesh.shape["rep"], mesh.shape["shard"]
    core = 2 if rep % 2 == 0 else 1
    near = 2 if rep == 16 else 1
    far = rep // (core * near)
    fast = (far, near, core, shard) == (4, 2, 2, 2)
    fine = Mesh(
        np.asarray(mesh.devices).reshape(far, near, core, shard),
        ("far", "near", "core", "shard"),
    )
    every = ("far", "near", "core", "shard")
    row, row3 = P(every, None), P(every, None, None)
    bias, weight = P(None, "shard"), P(None, "shard", None)
    return jax.shard_map(
        local_fast if fast else local_plain,
        mesh=fine,
        in_specs=(
            row3, row, row3, weight, bias, weight, bias, weight, bias, weight, bias, weight, bias,
        ),
        out_specs=(
            row3, row3, row, weight, bias, weight, bias, weight, bias, weight, bias, weight, bias,
        ),
        check_vma=False,
    )
```

```python
import functools

import jax
import jax.numpy as jnp
import numpy as np
from jax import lax
from jax.experimental import pallas as pl
from jax.experimental.pallas import tpu as pltpu
from jax.sharding import Mesh
from jax.sharding import PartitionSpec as P

HEADS = 12
eps = 1e-06
f32 = jnp.float32
bf16 = jnp.bfloat16


def normalize(rows):
    centred = rows - jnp.mean(rows, axis=-1, keepdims=True)
    inverse = lax.rsqrt(jnp.mean(centred * centred, axis=-1, keepdims=True) + eps)
    return (centred * inverse, inverse)


def norm_back(upstream, normed, inverse):
    return inverse * (
        upstream
        - jnp.mean(upstream, axis=-1, keepdims=True)
        - normed * jnp.mean(upstream * normed, axis=-1, keepdims=True)
    )


def gelu_and_slope(u):
    square = u * u
    t = jnp.tanh(u * (0.7978845608028654 + 0.7978845608028654 * 0.044715 * square))
    half = 0.5 + 0.5 * t
    inner_slope = 0.7978845608028654 + 3.0 * 0.7978845608028654 * 0.044715 * square
    return u * half, half + 0.5 * u * (1.0 - t * t) * inner_slope


def mm(a, b):
    return jnp.dot(a, b, preferred_element_type=f32)


def mm_t(a, b):
    return lax.dot_general(a, b, (((1,), (1,)), ((), ())), preferred_element_type=f32)


def t_mm(a, b):
    return lax.dot_general(a, b, (((0,), (0,)), ((), ())), preferred_element_type=f32)


def pick(array, index, axis=0):
    return lax.dynamic_index_in_dim(array, index, axis, keepdims=False)


SWAP = [(0, 1), (1, 0)]
CHEAP = pl.CostEstimate(flops=1, bytes_accessed=1, transcendentals=0)
PARAMS = pltpu.CompilerParams(vmem_limit_bytes=60 * 2**20)


def swap(value, axis):
    return lax.ppermute(value, axis, SWAP)


def gate(tree):
    values, shape = jax.tree.flatten(tree)
    count = len(values)

    def nothing(*refs):
        pass

    out = pl.pallas_call(
        nothing,
        out_shape=[jax.ShapeDtypeStruct(v.shape, v.dtype) for v in values],
        in_specs=[pl.BlockSpec(memory_space=pl.ANY)] * count,
        out_specs=[pl.BlockSpec(memory_space=pl.ANY)] * count,
        input_output_aliases={i: i for i in range(count)},
        cost_estimate=CHEAP,
        compiler_params=PARAMS,
    )(*values)
    return jax.tree.unflatten(shape, out)


def call(kernel, grid, ins, outs, prefetch=(), aliases=None):
    def spec(block, index, once=False):
        if block is None:
            return pl.BlockSpec(memory_space=pl.ANY)
        if once:
            return pl.BlockSpec(block, index, pipeline_mode=pl.Buffered(1))
        return pl.BlockSpec(block, index)

    return pl.pallas_call(
        kernel,
        out_shape=[jax.ShapeDtypeStruct(shape, dtype) for shape, dtype, _, _ in outs],
        grid_spec=pltpu.PrefetchScalarGridSpec(
            num_scalar_prefetch=len(prefetch),
            grid=grid,
            in_specs=[spec(*entry[1:]) for entry in ins],
            out_specs=[spec(block, index) for _, _, block, index in outs],
        ),
        input_output_aliases=aliases or {},
        cost_estimate=CHEAP,
        compiler_params=PARAMS,
    )(*prefetch, *[entry[0] for entry in ins])


class Block:
    def __init__(self, mod, biases, seq_count, length):
        self.mod = mod.reshape(seq_count, 6, -1)
        self.biases = biases
        self.seq_count, self.length = seq_count, length
        self.features = self.mod.shape[2]

    def rows(self, array):
        return (array, (self.length, array.shape[1]), lambda s: (s, 0))

    def rows_out(self, width, dtype):
        shape = (self.seq_count * self.length, width)
        return (shape, dtype, (self.length, width), lambda s: (s, 0))

    def mods(self):
        return (self.mod, (None, 6, self.features), lambda s: (s, 0, 0))

    def sums_out(self):
        return (
            (self.seq_count, 8, self.features),
            f32,
            (None, 8, self.features),
            lambda s: (s, 0, 0),
        )

    @staticmethod
    def whole(array):
        return (array, array.shape, lambda s: (0,) * array.ndim, True)

    @staticmethod
    def columns(array, start, width):
        return (array, (array.shape[0], width), lambda s: (0, start // width), True)

    def attention(self, stream, w_attn):
        features, length = self.features, self.length
        bias_qv = self.biases[0]
        bias = jnp.concatenate(
            [bias_qv[:features], jnp.zeros((features,), f32), bias_qv[features:], self.biases[1]]
        )[None]
        head = features // HEADS
        factor = head ** (-0.5)

        def kernel(
            stream_ref, mod_ref, w_ref, bias_ref,
            in_ref, qkv_ref, out_ref, branch_ref, middle_ref, mlp_ref,
        ):
            normed, _ = normalize(stream_ref[...])
            attn_in = (normed * (1.0 + mod_ref[1:2]) + mod_ref[0:1]).astype(bf16)
            in_ref[...] = attn_in
            wide = 3 * features
            for at in range(0, wide, features):
                columns = slice(at, at + features)
                qkv_ref[:, columns] = (
                    mm(attn_in, w_ref[:, columns]) + bias_ref[:, columns]
                ).astype(bf16)
            for start in range(0, features, 128):
                q, k, v = [
                    qkv_ref[:, part * features + start : part * features + start + 128]
                    for part in range(3)
                ]
                total = jnp.zeros((length, 128), f32)
                for mask in head_masks(length, head):
                    probs = probs_of(jnp.where(mask, q, 0), k, factor).astype(bf16)
                    total = total + mm(probs, jnp.where(mask, v, 0))
                out_ref[:, start : start + 128] = total.astype(bf16)
            branch = mm(out_ref[...], w_ref[:, wide:]) + bias_ref[:, wide:]
            middle = stream_ref[...] + mod_ref[2:3] * branch
            normed, _ = normalize(middle)
            branch_ref[...] = branch
            middle_ref[...] = middle
            mlp_ref[...] = (normed * (1.0 + mod_ref[4:5]) + mod_ref[3:4]).astype(bf16)

        self.stream = stream
        self.attn_in, self.qkv, self.attn_out, self.branch, self.middle, self.mlp_in = call(
            kernel,
            (self.seq_count,),
            [self.rows(stream), self.mods(), self.whole(w_attn), self.whole(bias)],
            [
                self.rows_out(features, bf16),
                self.rows_out(3 * features, bf16),
                self.rows_out(features, bf16),
                self.rows_out(features, f32),
                self.rows_out(features, f32),
                self.rows_out(features, bf16),
            ],
        )

    def hidden_layer(self, w_fc1):
        hidden, tile, tokens = w_fc1.shape[1], self.features, self.seq_count * self.length

        def kernel(in_ref, w_ref, bias_ref, slope_ref, hidden_ref):
            value, slope = gelu_and_slope(mm(in_ref[...], w_ref[...]) + bias_ref[...])
            slope_ref[...] = slope.astype(bf16)
            hidden_ref[...] = value.astype(bf16)

        out = ((tokens, hidden), bf16, (tokens, tile), lambda j: (0, j))
        self.slope, self.hidden = call(
            kernel,
            (hidden // tile,),
            [
                (self.mlp_in, (tokens, self.features), lambda j: (0, 0)),
                (w_fc1, (self.features, tile), lambda j: (0, j)),
                (self.biases[2][None], (1, tile), lambda j: (0, j)),
            ],
            [out, out],
        )

    def output_layer(self, w_fc2, dtype):
        def kernel(hidden_ref, middle_ref, mod_ref, w_ref, bias_ref, output_ref, stream_ref):
            output = mm(hidden_ref[...], w_ref[...]) + bias_ref[...]
            output_ref[...] = output
            stream_ref[...] = (middle_ref[...] + mod_ref[5:6] * output).astype(dtype)

        self.output, stream = call(
            kernel,
            (self.seq_count,),
            [
                self.rows(self.hidden),
                self.rows(self.middle),
                self.mods(),
                self.whole(w_fc2),
                self.whole(self.biases[3][None]),
            ],
            [self.rows_out(self.features, f32), self.rows_out(self.features, dtype)],
        )
        return stream

    def back_start(self, dh):
        def kernel(dh_ref, mod_ref, grad_ref, sums_ref):
            grad_out = (mod_ref[5:6] * dh_ref[...].astype(f32)).astype(bf16)
            grad_ref[...] = grad_out
            sums_ref[0:1] = jnp.sum(grad_out.astype(f32), axis=0, keepdims=True)

        self.dh = dh
        self.grad_out, self.sums_out2 = call(
            kernel,
            (self.seq_count,),
            [self.rows(dh), self.mods()],
            [self.rows_out(self.features, bf16), self.sums_out()],
        )
        return (self.hidden, self.grad_out)

    def back_hidden(self, w_fc2):
        hidden, tile, tokens = w_fc2.shape[0], self.features, self.seq_count * self.length

        def kernel(grad_ref, slope_ref, w_ref, out_ref, sum_ref):
            grad_hidden = mm_t(grad_ref[...], w_ref[...])
            grad_pre = (grad_hidden * slope_ref[...].astype(f32)).astype(bf16)
            out_ref[...] = grad_pre
            sum_ref[...] = jnp.sum(grad_pre.astype(f32), axis=0, keepdims=True)

        self.grad_pre, self.sum_fc1 = call(
            kernel,
            (hidden // tile,),
            [
                (self.grad_out, (tokens, self.features), lambda j: (0, 0)),
                (self.slope, (tokens, tile), lambda j: (0, j)),
                (w_fc2, (tile, self.features), lambda j: (j, 0)),
            ],
            [
                ((tokens, hidden), bf16, (tokens, tile), lambda j: (0, j)),
                ((1, hidden), f32, (1, tile), lambda j: (0, j)),
            ],
        )
        return (self.mlp_in, self.grad_pre)

    def back_middle(self, w_fc1, w_attn):
        def kernel(
            grad_ref, w1_ref, dh_ref, middle_ref, mod_ref, branch_ref, wo_ref,
            mid_ref, gb_ref, ga_ref, sums_ref,
        ):
            grad_in = mm_t(grad_ref[...], w1_ref[...])
            normed, inverse = normalize(middle_ref[...])
            dh = dh_ref[...].astype(f32)
            mid = dh + norm_back(grad_in * (1.0 + mod_ref[4:5]), normed, inverse)
            grad_branch = (mod_ref[2:3] * mid).astype(bf16)
            mid_ref[...] = mid
            gb_ref[...] = grad_branch
            ga_ref[...] = mm_t(grad_branch, wo_ref[...]).astype(bf16)
            for at, value in enumerate(
                (
                    mid * branch_ref[...],
                    grad_in,
                    grad_in * normed,
                    grad_branch.astype(f32),
                )
            ):
                sums_ref[at : at + 1] = jnp.sum(value, axis=0, keepdims=True)

        self.grad_mid, self.grad_branch, self.grad_attn, self.sums_mid = call(
            kernel,
            (self.seq_count,),
            [
                self.rows(self.grad_pre),
                self.whole(w_fc1),
                self.rows(self.dh),
                self.rows(self.middle),
                self.mods(),
                self.rows(self.branch),
                self.columns(w_attn, 3 * self.features, self.features),
            ],
            [
                self.rows_out(self.features, f32),
                self.rows_out(self.features, bf16),
                self.rows_out(self.features, bf16),
                self.sums_out(),
            ],
        )
        return (self.attn_out, self.grad_branch)

    def gate_sum(self):
        def kernel(dh_ref, output_ref, sums_ref):
            product = dh_ref[...].astype(f32) * output_ref[...]
            sums_ref[0:1] = jnp.sum(product, axis=0, keepdims=True)

        self.sums_gate = call(
            kernel,
            (self.seq_count,),
            [self.rows(self.dh), self.rows(self.output)],
            [self.sums_out()],
        )[0]

    def back_attention(self):
        self.grad_qkv = attention_backward(self.qkv, self.grad_attn, self.seq_count)
        return (self.attn_in, self.grad_qkv)

    def back_end(self, w_attn, grad_qkv):
        features = self.features

        def kernel(grad_ref, w_ref, stream_ref, mod_ref, mid_ref, dh_ref, sums_ref):
            grad_qkv = grad_ref[...]
            grad_in = mm_t(grad_qkv, w_ref[...])
            normed, inverse = normalize(stream_ref[...].astype(f32))
            dh_ref[...] = mid_ref[...] + norm_back(
                grad_in * (1.0 + mod_ref[1:2]), normed, inverse
            )
            for at, value in enumerate((grad_in, grad_in * normed)):
                sums_ref[at : at + 1] = jnp.sum(value, axis=0, keepdims=True)
            for part in range(3):
                columns = grad_qkv[:, part * features : (part + 1) * features].astype(f32)
                sums_ref[2 + part : 3 + part] = jnp.sum(columns, axis=0, keepdims=True)

        dh, self.sums_end = call(
            kernel,
            (self.seq_count,),
            [
                self.rows(grad_qkv),
                self.columns(w_attn, 0, 3 * features),
                self.rows(self.stream),
                self.mods(),
                self.rows(self.grad_mid),
            ],
            [self.rows_out(features, f32), self.sums_out()],
        )
        return dh

    def sum_parts(self):
        return [self.sums_end, self.sums_mid, self.sums_gate, self.sums_out2, self.sum_fc1]


def packed_sums(blocks, silu_low, width):
    seq_count, features = silu_low.shape
    parts = [part for block in blocks for part in block.sum_parts()]

    def kernel(*refs):
        silu_ref, out_ref = refs[-2], refs[-1]
        out_ref[...] = jnp.zeros(out_ref.shape, bf16)
        for l in range(len(blocks)):
            end, mid, gate_m, out2, fc1 = refs[5 * l : 5 * l + 5]
            rows = [(end, 0), (end, 1), (mid, 0), (mid, 1), (mid, 2), (gate_m, 0)]
            for s in range(seq_count):
                for k, (ref, row) in enumerate(rows):
                    at = (6 * l + k) * features
                    out_ref[0, s : s + 1, at : at + features] = ref[s, row : row + 1].astype(
                        bf16
                    )
            at = 0
            for ref, row in ((end, 2), (end, 4), (mid, 3), (fc1, None), (out2, 0)):
                if row is None:
                    total = ref[...]
                else:
                    total = ref[0, row : row + 1]
                    for s in range(1, seq_count):
                        total = total + ref[s, row : row + 1]
                out_ref[1, l : l + 1, at : at + total.shape[1]] = total.astype(bf16)
                at += total.shape[1]
        at = 6 * len(blocks) * features
        out_ref[0, :, at : at + features] = silu_ref[...]

    shape = (2, seq_count, width)
    return call(
        kernel,
        (1,),
        [Block.whole(part) for part in parts + [silu_low]],
        [(shape, bf16, shape, lambda s: (0, 0, 0))],
    )[0]


def probs_of(q, k, factor):
    scores = mm_t(q, k) * factor
    raised = jnp.exp(scores - jnp.max(scores, axis=-1, keepdims=True))
    return raised * (1.0 / jnp.sum(raised, axis=-1, keepdims=True))


def head_masks(rows, head):
    lane = lax.broadcasted_iota(jnp.int32, (rows, 128), 1)
    return [jnp.logical_and(lane >= at, lane < at + head) for at in range(0, 128, head)]


def attention_backward(qkv, grad, count):
    tokens, triple = qkv.shape
    width, length, head = triple // 3, tokens // count, triple // 3 // HEADS
    tile = 384 if width % 384 == 0 else width
    steps = width // tile
    factor = head ** (-0.5)

    def kernel(q_ref, k_ref, v_ref, g_ref, out_ref):
        for start in range(0, tile, 128):
            group = slice(start, start + 128)
            q, k, v, g = q_ref[:, group], k_ref[:, group], v_ref[:, group], g_ref[:, group]
            grad_q = jnp.zeros((length, 128), f32)
            grad_k = jnp.zeros((length, 128), f32)
            grad_v = jnp.zeros((length, 128), f32)
            for mask in head_masks(length, head):
                own_q, own_g = jnp.where(mask, q, 0), jnp.where(mask, g, 0)
                probs = probs_of(own_q, k, factor)
                grad_probs = mm_t(own_g, v)
                row_terms = jnp.sum(grad_probs * probs, axis=-1, keepdims=True)
                grad_scores = (probs * (grad_probs - row_terms)).astype(bf16)
                grad_q = grad_q + mm(grad_scores, jnp.where(mask, k, 0))
                grad_k = grad_k + t_mm(grad_scores, own_q)
                grad_v = grad_v + t_mm(probs.astype(bf16), own_g)
            at = pl.program_id(1) * tile + start
            for part, value in enumerate((grad_q * factor, grad_k * factor, grad_v)):
                columns = pl.ds(pl.multiple_of(part * width + at, 128), 128)
                out_ref[:, columns] = value.astype(bf16)

    def part(which):
        return (qkv, (length, tile), lambda s, g: (s, which * steps + g))

    return call(
        kernel,
        (count, steps),
        [part(0), part(1), part(2), (grad, (length, tile), lambda s, g: (s, g))],
        [((tokens, triple), bf16, (length, triple), lambda s, g: (s, 0))],
    )[0]


TILE = 384


def product_part(lhs, rhs, col_half, into, at, width):
    tokens, rows = lhs.shape
    half = rhs.shape[1] // 2
    tile = TILE if half > 1024 else min(rows, 4 * TILE)
    shift = at // half
    place = jnp.asarray(col_half, jnp.int32).reshape(1)
    ins = [
        (lhs, (tokens, tile), lambda i, p: (0, i)),
        (rhs, (tokens, half), lambda i, p: (0, p[0])),
    ]
    aliases = {}
    if into is not None:
        aliases = {3: 0}
        ins.append((into, None, None))

    def kernel(place_ref, lhs_ref, rhs_ref, *refs):
        refs[-1][...] = t_mm(lhs_ref[...], rhs_ref[...]).astype(bf16)

    return call(
        kernel,
        (rows // tile,),
        ins,
        [((rows, width), bf16, (tile, half), lambda i, p: (i, shift))],
        prefetch=(place,),
        aliases=aliases,
    )[0]


def product_sums(lhs, rhs, shard, col_half, got, into, at, width):
    tokens, rows = lhs.shape
    half = rhs.shape[1] // 2
    place = jnp.stack([shard, col_half]).astype(jnp.int32)
    size = rows // 2
    shape = (size, width)
    aliases = {}
    if into is not None:
        aliases = {4: 0, 5: 1}
    extra = [(part, None, None) for part in into or ()]
    if half > TILE or rows <= 2 * TILE:
        tile = 512 if half % 512 == 0 and at % 512 == 0 else TILE
        tiles, shift = half // tile, at // tile

        def kernel(place_ref, lhs_ref, rhs_ref, got_ref, *refs):
            send_ref, keep_ref = refs[-2:]
            total = t_mm(lhs_ref[...], rhs_ref[...]) + got_ref[...].astype(f32)
            total = total.astype(bf16)
            first = place_ref[0] == 0
            send_ref[...] = jnp.where(first, total[size:], total[:size])
            keep_ref[...] = jnp.where(first, total[:size], total[size:])

        out = (shape, bf16, (size, tile), lambda j, p: (0, shift + j))
        return call(
            kernel,
            (tiles,),
            [
                (lhs, (tokens, rows), lambda j, p: (0, 0)),
                (rhs, (tokens, tile), lambda j, p: (0, p[1] * tiles + j)),
                (got, (rows, tile), lambda j, p: (0, shift + j)),
            ]
            + extra,
            [out, out],
            prefetch=(place,),
            aliases=aliases,
        )
    shift = at // half

    def row_tile(side, p):
        return jnp.where(side == 0, 1 - p[0], p[0])

    def tall_kernel(place_ref, lhs_ref, rhs_ref, got_ref, *refs):
        send_ref, keep_ref = refs[-2:]
        total = t_mm(lhs_ref[...], rhs_ref[...]) + got_ref[...].astype(f32)

        @pl.when(pl.program_id(0) == 0)
        def _():
            send_ref[...] = total.astype(bf16)

        @pl.when(pl.program_id(0) == 1)
        def _():
            keep_ref[...] = total.astype(bf16)

    out = (shape, bf16, (size, half), lambda side, p: (0, shift))
    return call(
        tall_kernel,
        (2,),
        [
            (lhs, (tokens, size), lambda side, p: (0, row_tile(side, p))),
            (rhs, (tokens, half), lambda side, p: (0, p[1])),
            (got, (size, half), lambda side, p: (row_tile(side, p), shift)),
        ]
        + extra,
        [out, out],
        prefetch=(place,),
        aliases=aliases,
    )


def unit_part(pairs, col_half):
    width = sum(rhs.shape[1] // 2 for _, rhs in pairs)
    out, at = None, 0
    for lhs, rhs in pairs:
        out = product_part(lhs, rhs, col_half, out, at, width)
        at += rhs.shape[1] // 2
    return out


def unit_sums(pairs, shard, col_half, got):
    width = sum(rhs.shape[1] // 2 for _, rhs in pairs)
    out, at = None, 0
    for lhs, rhs in pairs:
        out = product_sums(lhs, rhs, shard, col_half, got, out, at, width)
        at += rhs.shape[1] // 2
    return out


class Fast:
    def __init__(self):
        self.near = lax.axis_index("near")
        self.core = lax.axis_index("core")
        self.shard = lax.axis_index("shard")
        self.place = jnp.stack([self.shard, self.near, self.core]).astype(jnp.int32)

    def ordered(self, mine, got, axis, at=0):
        first = lax.axis_index(axis) == 0
        return jnp.stack([jnp.where(first, mine, got), jnp.where(first, got, mine)], axis=at)

    def split(self, stack, axis, at=0):
        me = lax.axis_index(axis)
        return pick(stack, 1 - me, at), pick(stack, me, at)

    def quarter(self, stacked, layer):
        size = stacked.shape[1] // 4
        start = (self.near * 2 + self.core) * size
        return lax.dynamic_slice(stacked, (layer, start, 0), (1, size, stacked.shape[2]))[0]

    def assemble_own(self, members, layer, place):
        rows = members[0].shape[1]
        widths = [member.shape[2] for member in members]
        size = rows // 2

        def kernel(place_ref, *refs):
            at = 0
            for member_ref, member_width in zip(refs, widths):
                refs[-1][:, at : at + member_width] = member_ref[...]
                at += member_width

        ins = [
            (member, (None, size, member.shape[2]), lambda s, p: (layer, s, 0))
            for member in members
        ]
        shape = (2 * rows, sum(widths))
        block = (size, sum(widths))
        return call(
            kernel,
            (2,),
            ins,
            [(shape, members[0].dtype, block, lambda s, p: (p[0] * 2 + s, 0))],
            prefetch=(place,),
        )[0]

    def assemble_rest(self, whole, pieces):
        size, width = pieces[0].shape

        def out_block(step, place):
            shard, near = place[0], place[1]
            return (1 - shard) * 2 + jnp.where(step == 0, near, 1 - near), 0

        def kernel(place_ref, *refs):
            out_ref, core = refs[-1], place_ref[2]
            for step in range(2):
                for mine in range(2):

                    @pl.when(jnp.logical_and(pl.program_id(0) == step, core == mine))
                    def _(step=step, mine=mine):
                        out_ref[mine * size : (mine + 1) * size] = refs[step][...]
                        out_ref[(1 - mine) * size : (2 - mine) * size] = refs[2 + step][...]

        ins = [(piece, (size, width), lambda s, p: (0, 0)) for piece in pieces]
        ins.append((whole, None, None))
        return call(
            kernel,
            (2,),
            ins,
            [(whole.shape, whole.dtype, (2 * size, width), out_block)],
            prefetch=(self.place,),
            aliases={5: 0},
        )[0]

    def final(self, mine, got, layer, parts):
        rows = mine.shape[1]
        widths = [width for width, _ in parts]

        def out_block(step, place):
            near = place[1]
            return layer, jnp.where(step == 0, near, 1 - near), 0

        def kernel(place_ref, mine_ref, got_ref, *refs):
            outs, core = refs[-len(parts) :], place_ref[2]
            for first in range(2):
                low, high = (mine_ref, got_ref) if first == 0 else (got_ref, mine_ref)

                @pl.when(core == first)
                def _(low=low, high=high):
                    at = 0
                    for out_ref, width in zip(outs, widths):
                        out_ref[:, :width] = low[:, at : at + width].astype(f32)
                        out_ref[:, width:] = high[:, at : at + width].astype(f32)
                        at += width

        block = (None, rows, mine.shape[2])
        ins = [(array, block, lambda i, p: (i, 0, 0)) for array in (mine, got)]
        aliases = {}
        for at, (_, into) in enumerate(parts):
            if into is not None:
                aliases[1 + len(ins)] = at
                ins.append((into, None, None))
        return call(
            kernel,
            (2,),
            ins,
            [
                ((2, 2 * rows, 2 * width), f32, (None, rows, 2 * width), out_block)
                for width in widths
            ],
            prefetch=(self.place,),
            aliases=aliases,
        )

    def far_swap(self, value, name):
        step = 1 if name == "z1" else 2
        return lax.ppermute(value, "far", [(i, i ^ step) for i in range(4)])

    def any_swap(self, value, name):
        return self.far_swap(value, name) if name in ("z1", "z2") else swap(value, name)


def ada_product(silu, w_ada):
    layers, rows, width = w_ada.shape
    tile = width // 2

    def kernel(silu_ref, w_ref, out_ref):
        out_ref[...] = mm(silu_ref[...], w_ref[...])

    return call(
        kernel,
        (layers, 2),
        [
            (silu, silu.shape, lambda l, j: (0, 0)),
            (w_ada, (None, rows, tile), lambda l, j: (l, 0, j)),
        ],
        [
            (
                (silu.shape[0], layers * width),
                f32,
                (silu.shape[0], tile),
                lambda l, j: (0, 2 * l + j),
            )
        ],
    )[0]


def ada_back(mods, w_ada):
    layers, rows, width = w_ada.shape
    tile = width // 2

    def kernel(mods_ref, w_ref, out_ref):
        first = jnp.logical_and(pl.program_id(0) == 0, pl.program_id(1) == 0)

        @pl.when(first)
        def _():
            out_ref[...] = jnp.zeros(out_ref.shape, f32)

        out_ref[...] += mm_t(mods_ref[...], w_ref[...])

    return call(
        kernel,
        (layers, 2),
        [
            (mods, (mods.shape[0], tile), lambda l, j: (0, 2 * l + j)),
            (w_ada, (None, rows, tile), lambda l, j: (l, 0, j)),
        ],
        [((mods.shape[0], rows), f32, (mods.shape[0], rows), lambda l, j: (0, 0))],
    )[0]


def ada_weight(silu, mods, start, width, layer, layers, into, place):
    count, rows = silu[1]
    tile = 768 if width % 768 == 0 and start % 768 == 0 else width
    first = start // tile

    def kernel(place_ref, silu_ref, mods_ref, *refs):
        refs[-1][...] = t_mm(silu_ref[...], mods_ref[...])

    ins = [silu, (mods, (count, tile), lambda j, p: (0, first + j))]
    aliases = {}
    if into is not None:
        aliases = {3: 0}
        ins.append((into, None, None))
    return call(
        kernel,
        (width // tile,),
        ins,
        [((layers, rows, width), f32, (None, rows, tile), lambda j, p: (layer, 0, j))],
        prefetch=(place,),
        aliases=aliases,
    )[0]


def add(a, b):
    return (a.astype(f32) + b.astype(f32)).astype(bf16)


def silu_grad(cond_value, grad_silu):
    _, silu_pull = jax.vjp(jax.nn.silu, cond_value)
    return silu_pull(grad_silu)[0]


def owned_biases(mod_every, bias_sums, shard, widths, shard_count):
    totals, at = [jnp.sum(mod_every.astype(f32), axis=0)], 0
    for width in widths[1:]:
        totals.append(bias_sums[at : at + width * shard_count])
        at += width * shard_count
    return [
        lax.dynamic_slice_in_dim(total, shard * width, width, 0)
        for total, width in zip(totals, widths)
    ]


def unpack_biases(bias_all, widths):
    cuts = np.cumsum(widths)[:-1]
    parts = [
        jnp.moveaxis(part, 0, 1).reshape(bias_all.shape[1], -1).astype(f32)
        for part in jnp.split(bias_all, cuts, axis=2)
    ]
    return [[part[l] for part in parts] for l in range(bias_all.shape[1])]


def in_order(outputs, dh, condition_grad, g_w_ada, biases, weights):
    return (
        outputs,
        dh,
        condition_grad,
        g_w_ada,
        biases[0],
        weights[0],
        biases[1],
        weights[1],
        biases[2],
        weights[2],
        biases[3],
        weights[3],
        biases[4],
    )


def local_plain(
    latents,
    condition,
    output_grad,
    w_ada,
    b_ada,
    query_key_value_weight,
    b_qv,
    output_matrix_weight,
    b_proj,
    first_linear_weight,
    b_fc1,
    second_linear_weight,
    b_fc2,
):
    layer_count, owned_rows, ada_width = w_ada.shape
    seq_count, length, features = latents.shape
    shard, shards = lax.axis_index("shard"), lax.axis_size("shard")
    every = ("far", "near", "core", "shard")
    biases = (b_ada, b_qv, b_proj, b_fc1, b_fc2)
    widths = [b.shape[1] for b in biases]

    cond_value = condition.astype(f32)
    silu_low = jax.nn.silu(cond_value).astype(bf16)
    silu_group = lax.all_gather(silu_low, "shard", axis=0, tiled=True)
    silu_mine = lax.dynamic_slice_in_dim(silu_group, shard * owned_rows, owned_rows, 1)
    bias_all = lax.all_gather(jnp.concatenate(biases, axis=1), "shard", axis=0)
    full_biases = unpack_biases(bias_all, widths)
    mod_part = jnp.concatenate([mm(silu_mine, w_ada[l]) for l in range(layer_count)], axis=1)
    mod = lax.psum_scatter(mod_part, "shard", scatter_dimension=0, tiled=True)
    mod = mod.reshape(seq_count, layer_count, ada_width)
    silu_every = lax.all_gather(silu_low, every, axis=0, tiled=True)

    tokens = seq_count * length
    stream, blocks, weights = latents.astype(f32).reshape(tokens, features), [], []
    for l in range(layer_count):
        block = Block(mod[:, l] + full_biases[l][0], full_biases[l][1:], seq_count, length)
        full = [
            lax.all_gather(w[l], "shard", axis=0, tiled=True)
            for w in (
                query_key_value_weight,
                output_matrix_weight,
                first_linear_weight,
                second_linear_weight,
            )
        ]
        full[:2] = [jnp.concatenate(full[:2], axis=1)]
        block.attention(stream, full[0])
        block.hidden_layer(full[1])
        stream = block.output_layer(full[2], bf16 if l == layer_count - 1 else f32)
        blocks.append(block)
        weights.append(full)

    hidden_width = first_linear_weight.shape[2]

    def reduce(pair):
        grad = t_mm(*pair).astype(bf16)
        grad = lax.psum_scatter(grad, "shard", scatter_dimension=0, tiled=True)
        return lax.psum(grad, ("far", "near", "core")).astype(f32)

    dh = output_grad.reshape(tokens, features)
    grads, ada, owned, grad_silu = [None] * layer_count, None, [None] * layer_count, 0.0
    silu_owned = lax.dynamic_slice_in_dim(silu_every, shard * owned_rows, owned_rows, 1)
    for l in reversed(range(layer_count)):
        block, full = blocks[l], weights[l]
        second = block.back_start(dh)
        first = block.back_hidden(full[2])
        out = block.back_middle(full[1], full[0])
        qkv = block.back_attention()
        dh = block.back_end(full[0], block.grad_qkv)
        block.gate_sum()
        sums = packed_sums([block], silu_low, 8 * features + hidden_width)
        grad_mod = sums[0, :, : 6 * features]
        bias_sums = sums[1, 0, : 4 * features + hidden_width]
        grads[l] = [reduce(pair) for pair in (qkv, out, first, second)]
        mod_every = lax.all_gather(grad_mod, every, axis=0, tiled=True)
        silu = (silu_owned, silu_owned.shape, lambda j, p: (0, 0))
        place = jnp.zeros((1,), jnp.int32)
        ada = ada_weight(silu, mod_every, 0, ada_width, l, layer_count, ada, place)
        sums = lax.psum(bias_sums.astype(f32), every)
        owned[l] = owned_biases(mod_every, sums, shard, widths, shards)
        mods_group = lax.all_gather(grad_mod, "shard", axis=0, tiled=True)
        grad_silu = grad_silu + mm_t(mods_group, w_ada[l])
    by_owner = grad_silu.reshape(shards, seq_count, owned_rows)
    got = lax.all_to_all(by_owner, "shard", 0, 0)
    grad_silu = jnp.moveaxis(got, 0, 1).reshape(seq_count, features)
    return in_order(
        stream.reshape(latents.shape),
        dh.reshape(latents.shape),
        silu_grad(cond_value, grad_silu),
        ada,
        [jnp.stack([o[m] for o in owned]) for m in range(5)],
        [jnp.stack([g[m] for g in grads]) for m in range(4)],
    )


def local_fast(
    latents,
    condition,
    output_grad,
    w_ada,
    b_ada,
    query_key_value_weight,
    b_qv,
    output_matrix_weight,
    b_proj,
    first_linear_weight,
    b_fc1,
    second_linear_weight,
    b_fc2,
):
    comm = Fast()
    layer_count, owned_rows, ada_width = w_ada.shape
    seq_count, length, features = latents.shape
    tokens = seq_count * length
    shard = comm.shard
    biases = (b_ada, b_qv, b_proj, b_fc1, b_fc2)
    widths = [b.shape[1] for b in biases]

    chunk_of = []
    for l in range(layer_count):
        chunk_of.append((l, (query_key_value_weight, output_matrix_weight)))
        chunk_of.append((l, (first_linear_weight,)))
        chunk_of.append((l, (second_linear_weight,)))
    chunks = len(chunk_of)
    sends = []
    for l, members in chunk_of:
        quarters = [comm.quarter(member, l) for member in members]
        sends.append(quarters[0] if len(quarters) == 1 else jnp.concatenate(quarters, axis=1))

    cond_value = condition.astype(f32)
    silu_low = jax.nn.silu(cond_value).astype(bf16)
    bias_mine = jnp.concatenate(biases, axis=1)
    latents_flat = latents.reshape(tokens, features)
    stream = latents_flat
    pieces = [[None] * 4 for _ in range(chunks)]
    weights = [None] * chunks
    blocks = [None] * layer_count
    outputs, place = None, comm.place + 0
    for step in range(0, chunks + 2):
        live = {}
        if step < chunks:
            live["a"] = swap(sends[step], "shard")
        at = step - 1
        if 0 <= at < chunks:
            live["b"] = swap(pieces[at][0], "near")
            live["a2"] = swap(pieces[at][0], "core")
        at = step - 2
        if 0 <= at < chunks:
            live["b2"] = swap(pieces[at][1], "core")
        if step == 0:
            live["silu"] = swap(silu_low, "shard")
        elif step == 1:
            live["bias"] = swap(bias_mine, "shard")
        elif step == 2:
            live["mod"] = swap(mod_send, "shard")
        at = step - 3
        if at >= 0:
            l, part = at // 3, at % 3
            block = blocks[l]
            if part == 0:
                block.attention(stream, weights[at])
                live["done"] = block.mlp_in
            elif part == 1:
                block.hidden_layer(weights[at])
                live["done"] = block.hidden
            else:
                stream = block.output_layer(weights[at], f32)
                live["done"] = stream
        if step + 1 < chunks:
            live["send"] = sends[step + 1]
        early = {0: (0, 1), 1: (2,), 2: (3, 4), 5: (5,)}.get(step, ())
        live["own"] = [
            comm.assemble_own(chunk_of[k][1], chunk_of[k][0], place) for k in early
        ]
        live["place"] = place
        if step == 1:
            live["mod_send"], live["mod_keep"] = mod_send, mod_keep
        live = gate(live)
        for k, own in zip(early, live["own"]):
            weights[k] = own
        place = live["place"]
        if step + 1 < chunks:
            sends[step + 1] = live["send"]
        if step < chunks:
            pieces[step][0] = live["a"]
        if at >= 0:
            if part == 0:
                block.mlp_in = live["done"]
            elif part == 1:
                block.hidden = live["done"]
            else:
                stream = live["done"]
        at = step - 1
        if 0 <= at < chunks:
            pieces[at][1], pieces[at][2] = live["b"], live["a2"]
        at = step - 2
        if 0 <= at < chunks:
            pieces[at][3] = live["b2"]
            weights[at] = comm.assemble_rest(weights[at], pieces[at])
        if step == 0:
            silu_pair = comm.ordered(silu_low, live["silu"], "shard")
            silu_pair = silu_pair.reshape(2 * seq_count, features)
            silu_mine = lax.dynamic_slice_in_dim(silu_pair, shard * owned_rows, owned_rows, 1)
            mod_part = ada_product(silu_mine, w_ada)
            mod_send, mod_keep = comm.split(mod_part.reshape(2, seq_count, -1), "shard")
        elif step == 1:
            mod_send, mod_keep = live["mod_send"], live["mod_keep"]
            full_biases = unpack_biases(comm.ordered(bias_mine, live["bias"], "shard"), widths)
        elif step == 2:
            mod = (mod_keep + live["mod"]).reshape(seq_count, layer_count, ada_width)
            for l in range(layer_count):
                blocks[l] = Block(
                    mod[:, l] + full_biases[l][0], full_biases[l][1:], seq_count, length
                )
            stream = stream.astype(f32)

    units = 3 * layer_count
    last_step = units + 5
    pairs, core_send, first_send, keep, late, total, back, both = [
        [None] * units for _ in range(8)
    ]
    packed, ada = None, None
    bias_width = 2 * sum(widths[1:])
    packed_width = layer_count * ada_width + features
    small_plan = {
        (units + 1, 0): "z2",
        (units + 1, 1): "z1",
        (units + 2, 0): "near",
        (units + 2, 1): "shard",
        (units + 3, 0): "core",
    }
    dh = output_grad.reshape(tokens, features)
    next_in = dh
    weight_out, arrived = [None] * 4, None
    for step in range(0, last_step + 1):

        def unit_at(lag):
            return step - lag if 0 <= step - lag < units else None

        on_core, on_shard, on_near = unit_at(1), unit_at(2), unit_at(3)
        on_far, on_back, on_end = unit_at(4), unit_at(5), unit_at(6)
        live, fin = {}, {}
        if arrived is not None:
            weight_out = finish(comm, *arrived, layer_count, features, weight_out)
            fin["finals"], arrived = weight_out, None
        if on_core is not None:
            live["core"] = swap(core_send[on_core], "core")
        if on_shard is not None:
            fin["shard"] = swap(first_send[on_shard], "shard")
        if on_near is not None:
            fin["near"] = swap(late[on_near], "near")
        if on_far is not None:
            fin["far"] = lax.psum(total[on_far], "far")
        if on_back is not None:
            fin["back"] = swap(back[on_back], "near")
        if on_end is not None:
            fin["end"] = swap(both[on_end], "core")
        if (step, 0) in small_plan:
            live["small"] = comm.any_swap(packed, small_plan[step, 0])
        if step == units + 3:
            live["silu"] = swap(silu_send, "shard")
        if on_core is not None:
            if step == units:
                last = blocks[layer_count - 1]
                got, next_in, last.hidden = gate((live.pop("core"), next_in, last.hidden))
            else:
                got, next_in = gate((live.pop("core"), next_in))
            pairs[on_core][0] = (pairs[on_core][0][0], next_in)
            made = tuple(unit_sums(pairs[on_core], shard, comm.core, got))
            (live if step < units else fin)["made"] = made
        if step < units:
            l, part = layer_count - 1 - step // 3, step % 3
            block = blocks[l]
            w_attn, w_fc1, w_fc2 = weights[3 * l : 3 * l + 3]
            if part == 0:
                if step:
                    next_in = blocks[l + 1].back_end(weights[3 * (l + 1)], next_in)
                pairs[step] = [block.back_start(next_in)]
                next_in = block.grad_out
            elif part == 1:
                block.grad_out = next_in
                pairs[step] = [block.back_hidden(w_fc2)]
                next_in = block.grad_pre
            else:
                block.grad_pre = next_in
                middle = block.back_middle(w_fc1, w_attn)
                next_in = block.grad_attn
            live["next"] = next_in
        if step == units:
            dh = blocks[0].back_end(weights[0], next_in)
            outputs = last.output_layer(weights[3 * layer_count - 1], bf16)
            for block in blocks:
                block.gate_sum()
            fin["packed"] = packed_sums(blocks, silu_low, packed_width)
            fin["outputs"] = outputs, dh
        live = gate(live) if live else live
        if "made" in live:
            first_send[on_core], keep[on_core] = live["made"]
        if "small" in live:
            packed = pack(packed, live["small"])
        if step == units + 3:
            grad_silu = comm.ordered(silu_keep, live["silu"], "shard", at=1)
            grad_silu = grad_silu.reshape(seq_count, features)
            count = packed.shape[0] - 1
            every = packed[:count].reshape(count * seq_count, packed_width)
            owned = [
                owned_biases(
                    every[:, l * ada_width : (l + 1) * ada_width],
                    packed[count, l, :bias_width].astype(f32),
                    shard,
                    widths,
                    2,
                )
                for l in range(layer_count)
            ]
            silu_block = (every.shape[0], owned_rows)
            silu_at = layer_count * ada_width // owned_rows
            for l in range(layer_count):
                ada = ada_weight(
                    (every, silu_block, lambda j, p: (0, silu_at + p[0])),
                    every,
                    l * ada_width,
                    ada_width,
                    l,
                    layer_count,
                    ada,
                    comm.place,
                )
            fin["ada"] = ada
        if (step, 1) in small_plan:
            fin["small"] = comm.any_swap(packed, small_plan[step, 1])
        if step == units + 2:
            fin["mods"] = swap(mods_mine, "shard")
        if step < units:
            next_in = live["next"]
            if part < 2:
                pairs[step] = [(pairs[step][0][0], next_in)]
            else:
                block.grad_attn = next_in
                pairs[step] = [block.back_attention(), middle]
                next_in = block.grad_qkv
            fin["next"] = next_in
            fin["send"] = unit_part(pairs[step], 1 - comm.core)
        if step == last_step:
            live = fin
        else:
            live = gate(fin)
        if "finals" in live:
            weight_out = live["finals"]
        if "made" in live:
            first_send[on_core], keep[on_core] = live["made"]
        if step < units:
            core_send[step], next_in = live["send"], live["next"]
            pairs[step][0] = (pairs[step][0][0], next_in)
        if on_shard is not None:
            shape = (2, keep[on_shard].shape[0] // 2, keep[on_shard].shape[1])
            sent, kept = comm.split(keep[on_shard].reshape(shape), "near")
            got_sent, got_kept = comm.split(live["shard"].reshape(shape), "near")
            late[on_shard], total[on_shard] = add(sent, got_sent), add(kept, got_kept)
        if on_near is not None:
            total[on_near] = add(total[on_near], live["near"])
        if on_far is not None:
            back[on_far] = live["far"]
        if on_back is not None:
            both[on_back] = jnp.stack([back[on_back], live["back"]])
        if on_end is not None:
            arrived = both[on_end], live["end"], on_end
        if "ada" in live:
            ada = live["ada"]
        if step == units:
            outputs, dh = live["outputs"]
            packed = live["packed"]
            mods_mine = packed[0, :, : layer_count * ada_width]
        if "small" in live:
            packed = pack(packed, live["small"])
        if step == units + 2:
            mods_both = comm.ordered(mods_mine, live["mods"], "shard")
            silu_part = ada_back(mods_both.reshape(2 * seq_count, -1), w_ada)
            silu_send, silu_keep = comm.split(
                silu_part.reshape(2, seq_count, owned_rows), "shard"
            )
    weight_out = finish(comm, *arrived, layer_count, features, weight_out)
    return in_order(
        outputs.reshape(latents.shape),
        dh.reshape(latents.shape),
        silu_grad(cond_value, grad_silu),
        ada,
        [jnp.stack([o[m] for o in owned]) for m in range(5)],
        weight_out,
    )


def pack(mine, got):
    count = mine.shape[0] - 1
    return jnp.concatenate([mine[:count], got[:count], add(mine[count:], got[count:])], 0)


def finish(comm, mine, got, unit, layer_count, features, weight_out):
    layer, part = layer_count - 1 - unit // 3, unit % 3
    width = mine.shape[2]
    qkv, out, first, second = weight_out
    if part == 0:
        (second,) = comm.final(mine, got, layer, [(width, second)])
    elif part == 1:
        (first,) = comm.final(mine, got, layer, [(width, first)])
    else:
        half = features // 2
        qkv, out = comm.final(mine, got, layer, [(width - half, qkv), (half, out)])
    return [qkv, out, first, second]


def solution(mesh):
    rep, shard = mesh.shape["rep"], mesh.shape["shard"]
    core = 2 if rep % 2 == 0 else 1
    near = 2 if rep == 16 else 1
    far = rep // (core * near)
    fast = (far, near, core, shard) == (4, 2, 2, 2)
    fine = Mesh(
        np.asarray(mesh.devices).reshape(far, near, core, shard),
        ("far", "near", "core", "shard"),
    )
    every = ("far", "near", "core", "shard")
    row, row3 = P(every, None), P(every, None, None)
    bias, weight = P(None, "shard"), P(None, "shard", None)
    return jax.shard_map(
        local_fast if fast else local_plain,
        mesh=fine,
        in_specs=(
            row3, row, row3, weight, bias, weight, bias, weight, bias, weight, bias, weight, bias,
        ),
        out_specs=(
            row3, row3, row, weight, bias, weight, bias, weight, bias, weight, bias, weight, bias,
        ),
        check_vma=False,
    )
```

```python
import functools

import jax
import jax.numpy as jnp
import numpy as np
from jax import lax
from jax.experimental import pallas as pl
from jax.experimental.pallas import tpu as pltpu
from jax.sharding import Mesh
from jax.sharding import PartitionSpec as P

HEADS = 12
eps = 1e-06
f32 = jnp.float32
bf16 = jnp.bfloat16


def normalize(rows):
    centred = rows - jnp.mean(rows, axis=-1, keepdims=True)
    inverse = lax.rsqrt(jnp.mean(centred * centred, axis=-1, keepdims=True) + eps)
    return (centred * inverse, inverse)


def norm_back(upstream, normed, inverse):
    return inverse * (
        upstream
        - jnp.mean(upstream, axis=-1, keepdims=True)
        - normed * jnp.mean(upstream * normed, axis=-1, keepdims=True)
    )


def gelu_and_slope(u):
    square = u * u
    t = jnp.tanh(u * (0.7978845608028654 + 0.7978845608028654 * 0.044715 * square))
    half = 0.5 + 0.5 * t
    inner_slope = 0.7978845608028654 + 3.0 * 0.7978845608028654 * 0.044715 * square
    return u * half, half + 0.5 * u * (1.0 - t * t) * inner_slope


def mm(a, b):
    return jnp.dot(a, b, preferred_element_type=f32)


def mm_t(a, b):
    return lax.dot_general(a, b, (((1,), (1,)), ((), ())), preferred_element_type=f32)


def t_mm(a, b):
    return lax.dot_general(a, b, (((0,), (0,)), ((), ())), preferred_element_type=f32)


def pick(array, index, axis=0):
    return lax.dynamic_index_in_dim(array, index, axis, keepdims=False)


SWAP = [(0, 1), (1, 0)]
CHEAP = pl.CostEstimate(flops=1, bytes_accessed=1, transcendentals=0)
PARAMS = pltpu.CompilerParams(vmem_limit_bytes=60 * 2**20)


def swap(value, axis):
    return lax.ppermute(value, axis, SWAP)


def gate(tree):
    values, shape = jax.tree.flatten(tree)
    count = len(values)

    def nothing(*refs):
        pass

    out = pl.pallas_call(
        nothing,
        out_shape=[jax.ShapeDtypeStruct(v.shape, v.dtype) for v in values],
        in_specs=[pl.BlockSpec(memory_space=pl.ANY)] * count,
        out_specs=[pl.BlockSpec(memory_space=pl.ANY)] * count,
        input_output_aliases={i: i for i in range(count)},
        cost_estimate=CHEAP,
        compiler_params=PARAMS,
    )(*values)
    return jax.tree.unflatten(shape, out)


def call(kernel, grid, ins, outs, prefetch=(), aliases=None):
    def spec(block, index, once=False):
        if block is None:
            return pl.BlockSpec(memory_space=pl.ANY)
        if once:
            return pl.BlockSpec(block, index, pipeline_mode=pl.Buffered(1))
        return pl.BlockSpec(block, index)

    return pl.pallas_call(
        kernel,
        out_shape=[jax.ShapeDtypeStruct(shape, dtype) for shape, dtype, _, _ in outs],
        grid_spec=pltpu.PrefetchScalarGridSpec(
            num_scalar_prefetch=len(prefetch),
            grid=grid,
            in_specs=[spec(*entry[1:]) for entry in ins],
            out_specs=[spec(block, index) for _, _, block, index in outs],
        ),
        input_output_aliases=aliases or {},
        cost_estimate=CHEAP,
        compiler_params=PARAMS,
    )(*prefetch, *[entry[0] for entry in ins])


class Block:
    def __init__(self, mod, biases, seq_count, length):
        self.mod = mod.reshape(seq_count, 6, -1)
        self.biases = biases
        self.seq_count, self.length = seq_count, length
        self.features = self.mod.shape[2]

    def rows(self, array):
        return (array, (self.length, array.shape[1]), lambda s: (s, 0))

    def rows_out(self, width, dtype):
        shape = (self.seq_count * self.length, width)
        return (shape, dtype, (self.length, width), lambda s: (s, 0))

    def mods(self):
        return (self.mod, (None, 6, self.features), lambda s: (s, 0, 0))

    def sums_out(self):
        return (
            (self.seq_count, 8, self.features),
            f32,
            (None, 8, self.features),
            lambda s: (s, 0, 0),
        )

    @staticmethod
    def whole(array):
        return (array, array.shape, lambda s: (0,) * array.ndim, True)

    @staticmethod
    def columns(array, start, width):
        return (array, (array.shape[0], width), lambda s: (0, start // width), True)

    def attention(self, stream, w_attn):
        features, length = self.features, self.length
        bias_qv = self.biases[0]
        bias = jnp.concatenate(
            [bias_qv[:features], jnp.zeros((features,), f32), bias_qv[features:], self.biases[1]]
        )[None]
        head = features // HEADS
        factor = head ** (-0.5)

        def kernel(
            stream_ref, mod_ref, w_ref, bias_ref,
            in_ref, qkv_ref, out_ref, branch_ref, middle_ref, mlp_ref,
        ):
            normed, _ = normalize(stream_ref[...])
            attn_in = (normed * (1.0 + mod_ref[1:2]) + mod_ref[0:1]).astype(bf16)
            in_ref[...] = attn_in
            wide = 3 * features
            for at in range(0, wide, features):
                columns = slice(at, at + features)
                qkv_ref[:, columns] = (
                    mm(attn_in, w_ref[:, columns]) + bias_ref[:, columns]
                ).astype(bf16)
            for start in range(0, features, 128):
                q, k, v = [
                    qkv_ref[:, part * features + start : part * features + start + 128]
                    for part in range(3)
                ]
                total = jnp.zeros((length, 128), f32)
                for mask in head_masks(length, head):
                    probs = probs_of(jnp.where(mask, q, 0), k, factor).astype(bf16)
                    total = total + mm(probs, jnp.where(mask, v, 0))
                out_ref[:, start : start + 128] = total.astype(bf16)
            branch = mm(out_ref[...], w_ref[:, wide:]) + bias_ref[:, wide:]
            middle = stream_ref[...] + mod_ref[2:3] * branch
            normed, _ = normalize(middle)
            branch_ref[...] = branch
            middle_ref[...] = middle
            mlp_ref[...] = (normed * (1.0 + mod_ref[4:5]) + mod_ref[3:4]).astype(bf16)

        self.stream = stream
        self.attn_in, self.qkv, self.attn_out, self.branch, self.middle, self.mlp_in = call(
            kernel,
            (self.seq_count,),
            [self.rows(stream), self.mods(), self.whole(w_attn), self.whole(bias)],
            [
                self.rows_out(features, bf16),
                self.rows_out(3 * features, bf16),
                self.rows_out(features, bf16),
                self.rows_out(features, f32),
                self.rows_out(features, f32),
                self.rows_out(features, bf16),
            ],
        )

    def hidden_layer(self, w_fc1):
        hidden, tile, tokens = w_fc1.shape[1], self.features, self.seq_count * self.length

        def kernel(in_ref, w_ref, bias_ref, slope_ref, hidden_ref):
            value, slope = gelu_and_slope(mm(in_ref[...], w_ref[...]) + bias_ref[...])
            slope_ref[...] = slope.astype(bf16)
            hidden_ref[...] = value.astype(bf16)

        out = ((tokens, hidden), bf16, (tokens, tile), lambda j: (0, j))
        self.slope, self.hidden = call(
            kernel,
            (hidden // tile,),
            [
                (self.mlp_in, (tokens, self.features), lambda j: (0, 0)),
                (w_fc1, (self.features, tile), lambda j: (0, j)),
                (self.biases[2][None], (1, tile), lambda j: (0, j)),
            ],
            [out, out],
        )

    def output_layer(self, w_fc2, dtype):
        def kernel(hidden_ref, middle_ref, mod_ref, w_ref, bias_ref, output_ref, stream_ref):
            output = mm(hidden_ref[...], w_ref[...]) + bias_ref[...]
            output_ref[...] = output
            stream_ref[...] = (middle_ref[...] + mod_ref[5:6] * output).astype(dtype)

        self.output, stream = call(
            kernel,
            (self.seq_count,),
            [
                self.rows(self.hidden),
                self.rows(self.middle),
                self.mods(),
                self.whole(w_fc2),
                self.whole(self.biases[3][None]),
            ],
            [self.rows_out(self.features, f32), self.rows_out(self.features, dtype)],
        )
        return stream

    def back_start(self, dh):
        def kernel(dh_ref, mod_ref, grad_ref, sums_ref):
            grad_out = (mod_ref[5:6] * dh_ref[...].astype(f32)).astype(bf16)
            grad_ref[...] = grad_out
            sums_ref[0:1] = jnp.sum(grad_out.astype(f32), axis=0, keepdims=True)

        self.dh = dh
        self.grad_out, self.sums_out2 = call(
            kernel,
            (self.seq_count,),
            [self.rows(dh), self.mods()],
            [self.rows_out(self.features, bf16), self.sums_out()],
        )
        return (self.hidden, self.grad_out)

    def back_hidden(self, w_fc2):
        hidden, tile, tokens = w_fc2.shape[0], self.features, self.seq_count * self.length

        def kernel(grad_ref, slope_ref, w_ref, out_ref, sum_ref):
            grad_hidden = mm_t(grad_ref[...], w_ref[...])
            grad_pre = (grad_hidden * slope_ref[...].astype(f32)).astype(bf16)
            out_ref[...] = grad_pre
            sum_ref[...] = jnp.sum(grad_pre.astype(f32), axis=0, keepdims=True)

        self.grad_pre, self.sum_fc1 = call(
            kernel,
            (hidden // tile,),
            [
                (self.grad_out, (tokens, self.features), lambda j: (0, 0)),
                (self.slope, (tokens, tile), lambda j: (0, j)),
                (w_fc2, (tile, self.features), lambda j: (j, 0)),
            ],
            [
                ((tokens, hidden), bf16, (tokens, tile), lambda j: (0, j)),
                ((1, hidden), f32, (1, tile), lambda j: (0, j)),
            ],
        )
        return (self.mlp_in, self.grad_pre)

    def back_middle(self, w_fc1, w_attn):
        def kernel(
            grad_ref, w1_ref, dh_ref, middle_ref, mod_ref, branch_ref, wo_ref,
            mid_ref, gb_ref, ga_ref, sums_ref,
        ):
            grad_in = mm_t(grad_ref[...], w1_ref[...])
            normed, inverse = normalize(middle_ref[...])
            dh = dh_ref[...].astype(f32)
            mid = dh + norm_back(grad_in * (1.0 + mod_ref[4:5]), normed, inverse)
            grad_branch = (mod_ref[2:3] * mid).astype(bf16)
            mid_ref[...] = mid
            gb_ref[...] = grad_branch
            ga_ref[...] = mm_t(grad_branch, wo_ref[...]).astype(bf16)
            for at, value in enumerate(
                (
                    mid * branch_ref[...],
                    grad_in,
                    grad_in * normed,
                    grad_branch.astype(f32),
                )
            ):
                sums_ref[at : at + 1] = jnp.sum(value, axis=0, keepdims=True)

        self.grad_mid, self.grad_branch, self.grad_attn, self.sums_mid = call(
            kernel,
            (self.seq_count,),
            [
                self.rows(self.grad_pre),
                self.whole(w_fc1),
                self.rows(self.dh),
                self.rows(self.middle),
                self.mods(),
                self.rows(self.branch),
                self.columns(w_attn, 3 * self.features, self.features),
            ],
            [
                self.rows_out(self.features, f32),
                self.rows_out(self.features, bf16),
                self.rows_out(self.features, bf16),
                self.sums_out(),
            ],
        )
        return (self.attn_out, self.grad_branch)

    def gate_sum(self):
        def kernel(dh_ref, output_ref, sums_ref):
            product = dh_ref[...].astype(f32) * output_ref[...]
            sums_ref[0:1] = jnp.sum(product, axis=0, keepdims=True)

        self.sums_gate = call(
            kernel,
            (self.seq_count,),
            [self.rows(self.dh), self.rows(self.output)],
            [self.sums_out()],
        )[0]

    def back_attention(self):
        self.grad_qkv = attention_backward(self.qkv, self.grad_attn, self.seq_count)
        return (self.attn_in, self.grad_qkv)

    def back_end(self, w_attn, grad_qkv):
        features = self.features

        def kernel(grad_ref, w_ref, stream_ref, mod_ref, mid_ref, dh_ref, sums_ref):
            grad_qkv = grad_ref[...]
            grad_in = mm_t(grad_qkv, w_ref[...])
            normed, inverse = normalize(stream_ref[...].astype(f32))
            dh_ref[...] = mid_ref[...] + norm_back(
                grad_in * (1.0 + mod_ref[1:2]), normed, inverse
            )
            for at, value in enumerate((grad_in, grad_in * normed)):
                sums_ref[at : at + 1] = jnp.sum(value, axis=0, keepdims=True)
            for part in range(3):
                columns = grad_qkv[:, part * features : (part + 1) * features].astype(f32)
                sums_ref[2 + part : 3 + part] = jnp.sum(columns, axis=0, keepdims=True)

        dh, self.sums_end = call(
            kernel,
            (self.seq_count,),
            [
                self.rows(grad_qkv),
                self.columns(w_attn, 0, 3 * features),
                self.rows(self.stream),
                self.mods(),
                self.rows(self.grad_mid),
            ],
            [self.rows_out(features, f32), self.sums_out()],
        )
        return dh

    def sum_parts(self):
        return [self.sums_end, self.sums_mid, self.sums_gate, self.sums_out2, self.sum_fc1]


def packed_sums(blocks, silu_low, width):
    seq_count, features = silu_low.shape
    parts = [part for block in blocks for part in block.sum_parts()]

    def kernel(*refs):
        silu_ref, out_ref = refs[-2], refs[-1]
        out_ref[...] = jnp.zeros(out_ref.shape, bf16)
        for l in range(len(blocks)):
            end, mid, gate_m, out2, fc1 = refs[5 * l : 5 * l + 5]
            rows = [(end, 0), (end, 1), (mid, 0), (mid, 1), (mid, 2), (gate_m, 0)]
            for s in range(seq_count):
                for k, (ref, row) in enumerate(rows):
                    at = (6 * l + k) * features
                    out_ref[0, s : s + 1, at : at + features] = ref[s, row : row + 1].astype(
                        bf16
                    )
            at = 0
            for ref, row in ((end, 2), (end, 4), (mid, 3), (fc1, None), (out2, 0)):
                if row is None:
                    total = ref[...]
                else:
                    total = ref[0, row : row + 1]
                    for s in range(1, seq_count):
                        total = total + ref[s, row : row + 1]
                out_ref[1, l : l + 1, at : at + total.shape[1]] = total.astype(bf16)
                at += total.shape[1]
        at = 6 * len(blocks) * features
        out_ref[0, :, at : at + features] = silu_ref[...]

    shape = (2, seq_count, width)
    return call(
        kernel,
        (1,),
        [Block.whole(part) for part in parts + [silu_low]],
        [(shape, bf16, shape, lambda s: (0, 0, 0))],
    )[0]


def probs_of(q, k, factor):
    scores = mm_t(q, k) * factor
    raised = jnp.exp(scores - jnp.max(scores, axis=-1, keepdims=True))
    return raised * (1.0 / jnp.sum(raised, axis=-1, keepdims=True))


def head_masks(rows, head):
    lane = lax.broadcasted_iota(jnp.int32, (rows, 128), 1)
    return [jnp.logical_and(lane >= at, lane < at + head) for at in range(0, 128, head)]


def attention_backward(qkv, grad, count):
    tokens, triple = qkv.shape
    width, length, head = triple // 3, tokens // count, triple // 3 // HEADS
    tile = 384 if width % 384 == 0 else width
    steps = width // tile
    factor = head ** (-0.5)

    def kernel(q_ref, k_ref, v_ref, g_ref, out_ref):
        for start in range(0, tile, 128):
            group = slice(start, start + 128)
            q, k, v, g = q_ref[:, group], k_ref[:, group], v_ref[:, group], g_ref[:, group]
            grad_q = jnp.zeros((length, 128), f32)
            grad_k = jnp.zeros((length, 128), f32)
            grad_v = jnp.zeros((length, 128), f32)
            for mask in head_masks(length, head):
                own_q, own_g = jnp.where(mask, q, 0), jnp.where(mask, g, 0)
                probs = probs_of(own_q, k, factor)
                grad_probs = mm_t(own_g, v)
                row_terms = jnp.sum(grad_probs * probs, axis=-1, keepdims=True)
                grad_scores = (probs * (grad_probs - row_terms)).astype(bf16)
                grad_q = grad_q + mm(grad_scores, jnp.where(mask, k, 0))
                grad_k = grad_k + t_mm(grad_scores, own_q)
                grad_v = grad_v + t_mm(probs.astype(bf16), own_g)
            at = pl.program_id(1) * tile + start
            for part, value in enumerate((grad_q * factor, grad_k * factor, grad_v)):
                columns = pl.ds(pl.multiple_of(part * width + at, 128), 128)
                out_ref[:, columns] = value.astype(bf16)

    def part(which):
        return (qkv, (length, tile), lambda s, g: (s, which * steps + g))

    return call(
        kernel,
        (count, steps),
        [part(0), part(1), part(2), (grad, (length, tile), lambda s, g: (s, g))],
        [((tokens, triple), bf16, (length, triple), lambda s, g: (s, 0))],
    )[0]


TILE = 384


def product_part(lhs, rhs, col_half, into, at, width):
    tokens, rows = lhs.shape
    half = rhs.shape[1] // 2
    tile = TILE if half > 1024 else min(rows, 4 * TILE)
    shift = at // half
    place = jnp.asarray(col_half, jnp.int32).reshape(1)
    ins = [
        (lhs, (tokens, tile), lambda i, p: (0, i)),
        (rhs, (tokens, half), lambda i, p: (0, p[0])),
    ]
    aliases = {}
    if into is not None:
        aliases = {3: 0}
        ins.append((into, None, None))

    def kernel(place_ref, lhs_ref, rhs_ref, *refs):
        refs[-1][...] = t_mm(lhs_ref[...], rhs_ref[...]).astype(bf16)

    return call(
        kernel,
        (rows // tile,),
        ins,
        [((rows, width), bf16, (tile, half), lambda i, p: (i, shift))],
        prefetch=(place,),
        aliases=aliases,
    )[0]


def product_sums(lhs, rhs, shard, col_half, got, into, at, width):
    tokens, rows = lhs.shape
    half = rhs.shape[1] // 2
    place = jnp.stack([shard, col_half]).astype(jnp.int32)
    size = rows // 2
    shape = (size, width)
    aliases = {}
    if into is not None:
        aliases = {4: 0, 5: 1}
    extra = [(part, None, None) for part in into or ()]
    if half > TILE or rows <= 2 * TILE:
        tile = 512 if half % 512 == 0 and at % 512 == 0 else TILE
        tiles, shift = half // tile, at // tile

        def kernel(place_ref, lhs_ref, rhs_ref, got_ref, *refs):
            send_ref, keep_ref = refs[-2:]
            total = t_mm(lhs_ref[...], rhs_ref[...]) + got_ref[...].astype(f32)
            total = total.astype(bf16)
            first = place_ref[0] == 0
            send_ref[...] = jnp.where(first, total[size:], total[:size])
            keep_ref[...] = jnp.where(first, total[:size], total[size:])

        out = (shape, bf16, (size, tile), lambda j, p: (0, shift + j))
        return call(
            kernel,
            (tiles,),
            [
                (lhs, (tokens, rows), lambda j, p: (0, 0)),
                (rhs, (tokens, tile), lambda j, p: (0, p[1] * tiles + j)),
                (got, (rows, tile), lambda j, p: (0, shift + j)),
            ]
            + extra,
            [out, out],
            prefetch=(place,),
            aliases=aliases,
        )
    shift = at // half

    def row_tile(side, p):
        return jnp.where(side == 0, 1 - p[0], p[0])

    def tall_kernel(place_ref, lhs_ref, rhs_ref, got_ref, *refs):
        send_ref, keep_ref = refs[-2:]
        total = t_mm(lhs_ref[...], rhs_ref[...]) + got_ref[...].astype(f32)

        @pl.when(pl.program_id(0) == 0)
        def _():
            send_ref[...] = total.astype(bf16)

        @pl.when(pl.program_id(0) == 1)
        def _():
            keep_ref[...] = total.astype(bf16)

    out = (shape, bf16, (size, half), lambda side, p: (0, shift))
    return call(
        tall_kernel,
        (2,),
        [
            (lhs, (tokens, size), lambda side, p: (0, row_tile(side, p))),
            (rhs, (tokens, half), lambda side, p: (0, p[1])),
            (got, (size, half), lambda side, p: (row_tile(side, p), shift)),
        ]
        + extra,
        [out, out],
        prefetch=(place,),
        aliases=aliases,
    )


def unit_part(pairs, col_half):
    width = sum(rhs.shape[1] // 2 for _, rhs in pairs)
    out, at = None, 0
    for lhs, rhs in pairs:
        out = product_part(lhs, rhs, col_half, out, at, width)
        at += rhs.shape[1] // 2
    return out


def unit_sums(pairs, shard, col_half, got):
    width = sum(rhs.shape[1] // 2 for _, rhs in pairs)
    out, at = None, 0
    for lhs, rhs in pairs:
        out = product_sums(lhs, rhs, shard, col_half, got, out, at, width)
        at += rhs.shape[1] // 2
    return out


class Fast:
    def __init__(self):
        self.near = lax.axis_index("near")
        self.core = lax.axis_index("core")
        self.shard = lax.axis_index("shard")
        self.place = jnp.stack([self.shard, self.near, self.core]).astype(jnp.int32)

    def ordered(self, mine, got, axis, at=0):
        first = lax.axis_index(axis) == 0
        return jnp.stack([jnp.where(first, mine, got), jnp.where(first, got, mine)], axis=at)

    def split(self, stack, axis, at=0):
        me = lax.axis_index(axis)
        return pick(stack, 1 - me, at), pick(stack, me, at)

    def quarter(self, stacked, layer):
        size = stacked.shape[1] // 4
        start = (self.near * 2 + self.core) * size
        return lax.dynamic_slice(stacked, (layer, start, 0), (1, size, stacked.shape[2]))[0]

    def assemble_own(self, members, layer, place):
        rows = members[0].shape[1]
        widths = [member.shape[2] for member in members]
        size = rows // 2

        def kernel(place_ref, *refs):
            at = 0
            for member_ref, member_width in zip(refs, widths):
                refs[-1][:, at : at + member_width] = member_ref[...]
                at += member_width

        ins = [
            (member, (None, size, member.shape[2]), lambda s, p: (layer, s, 0))
            for member in members
        ]
        shape = (2 * rows, sum(widths))
        block = (size, sum(widths))
        return call(
            kernel,
            (2,),
            ins,
            [(shape, members[0].dtype, block, lambda s, p: (p[0] * 2 + s, 0))],
            prefetch=(place,),
        )[0]

    def assemble_rest(self, whole, pieces):
        size, width = pieces[0].shape

        def out_block(step, place):
            shard, near = place[0], place[1]
            return (1 - shard) * 2 + jnp.where(step == 0, near, 1 - near), 0

        def kernel(place_ref, *refs):
            out_ref, core = refs[-1], place_ref[2]
            for step in range(2):
                for mine in range(2):

                    @pl.when(jnp.logical_and(pl.program_id(0) == step, core == mine))
                    def _(step=step, mine=mine):
                        out_ref[mine * size : (mine + 1) * size] = refs[step][...]
                        out_ref[(1 - mine) * size : (2 - mine) * size] = refs[2 + step][...]

        ins = [(piece, (size, width), lambda s, p: (0, 0)) for piece in pieces]
        ins.append((whole, None, None))
        return call(
            kernel,
            (2,),
            ins,
            [(whole.shape, whole.dtype, (2 * size, width), out_block)],
            prefetch=(self.place,),
            aliases={5: 0},
        )[0]

    def final(self, mine, got, layer, parts):
        rows = mine.shape[1]
        widths = [width for width, _ in parts]

        def out_block(step, place):
            near = place[1]
            return layer, jnp.where(step == 0, near, 1 - near), 0

        def kernel(place_ref, mine_ref, got_ref, *refs):
            outs, core = refs[-len(parts) :], place_ref[2]
            for first in range(2):
                low, high = (mine_ref, got_ref) if first == 0 else (got_ref, mine_ref)

                @pl.when(core == first)
                def _(low=low, high=high):
                    at = 0
                    for out_ref, width in zip(outs, widths):
                        out_ref[:, :width] = low[:, at : at + width].astype(f32)
                        out_ref[:, width:] = high[:, at : at + width].astype(f32)
                        at += width

        block = (None, rows, mine.shape[2])
        ins = [(array, block, lambda i, p: (i, 0, 0)) for array in (mine, got)]
        aliases = {}
        for at, (_, into) in enumerate(parts):
            if into is not None:
                aliases[1 + len(ins)] = at
                ins.append((into, None, None))
        return call(
            kernel,
            (2,),
            ins,
            [
                ((2, 2 * rows, 2 * width), f32, (None, rows, 2 * width), out_block)
                for width in widths
            ],
            prefetch=(self.place,),
            aliases=aliases,
        )

    def far_swap(self, value, name):
        step = 1 if name == "z1" else 2
        return lax.ppermute(value, "far", [(i, i ^ step) for i in range(4)])

    def far_side(self, name):
        far = lax.axis_index("far")
        return far % 2 if name == "z1" else far // 2

    def far_split(self, mine, got, name):
        side = self.far_side(name)
        shape = (2, mine.shape[0] // 2, mine.shape[1])
        mine, got = mine.reshape(shape), got.reshape(shape)
        return (
            add(pick(mine, 1 - side), pick(got, 1 - side)),
            add(pick(mine, side), pick(got, side)),
        )

    def far_ordered(self, mine, got, name):
        first = self.far_side(name) == 0
        return jnp.concatenate([jnp.where(first, mine, got), jnp.where(first, got, mine)], 0)

    def any_swap(self, value, name):
        return self.far_swap(value, name) if name in ("z1", "z2") else swap(value, name)


def ada_product(silu, w_ada):
    layers, rows, width = w_ada.shape
    tile = width // 2

    def kernel(silu_ref, w_ref, out_ref):
        out_ref[...] = mm(silu_ref[...], w_ref[...])

    return call(
        kernel,
        (layers, 2),
        [
            (silu, silu.shape, lambda l, j: (0, 0)),
            (w_ada, (None, rows, tile), lambda l, j: (l, 0, j)),
        ],
        [
            (
                (silu.shape[0], layers * width),
                f32,
                (silu.shape[0], tile),
                lambda l, j: (0, 2 * l + j),
            )
        ],
    )[0]


def ada_back(mods, w_ada):
    layers, rows, width = w_ada.shape
    tile = width // 2

    def kernel(mods_ref, w_ref, out_ref):
        first = jnp.logical_and(pl.program_id(0) == 0, pl.program_id(1) == 0)

        @pl.when(first)
        def _():
            out_ref[...] = jnp.zeros(out_ref.shape, f32)

        out_ref[...] += mm_t(mods_ref[...], w_ref[...])

    return call(
        kernel,
        (layers, 2),
        [
            (mods, (mods.shape[0], tile), lambda l, j: (0, 2 * l + j)),
            (w_ada, (None, rows, tile), lambda l, j: (l, 0, j)),
        ],
        [((mods.shape[0], rows), f32, (mods.shape[0], rows), lambda l, j: (0, 0))],
    )[0]


def ada_weight(silu, mods, start, width, layer, layers, into, place):
    count, rows = silu[1]
    tile = 768 if width % 768 == 0 and start % 768 == 0 else width
    first = start // tile

    def kernel(place_ref, silu_ref, mods_ref, *refs):
        refs[-1][...] = t_mm(silu_ref[...], mods_ref[...])

    ins = [silu, (mods, (count, tile), lambda j, p: (0, first + j))]
    aliases = {}
    if into is not None:
        aliases = {3: 0}
        ins.append((into, None, None))
    return call(
        kernel,
        (width // tile,),
        ins,
        [((layers, rows, width), f32, (None, rows, tile), lambda j, p: (layer, 0, j))],
        prefetch=(place,),
        aliases=aliases,
    )[0]


def add(a, b):
    return (a.astype(f32) + b.astype(f32)).astype(bf16)


def silu_grad(cond_value, grad_silu):
    _, silu_pull = jax.vjp(jax.nn.silu, cond_value)
    return silu_pull(grad_silu)[0]


def owned_biases(mod_every, bias_sums, shard, widths, shard_count):
    totals, at = [jnp.sum(mod_every.astype(f32), axis=0)], 0
    for width in widths[1:]:
        totals.append(bias_sums[at : at + width * shard_count])
        at += width * shard_count
    return [
        lax.dynamic_slice_in_dim(total, shard * width, width, 0)
        for total, width in zip(totals, widths)
    ]


def unpack_biases(bias_all, widths):
    cuts = np.cumsum(widths)[:-1]
    parts = [
        jnp.moveaxis(part, 0, 1).reshape(bias_all.shape[1], -1).astype(f32)
        for part in jnp.split(bias_all, cuts, axis=2)
    ]
    return [[part[l] for part in parts] for l in range(bias_all.shape[1])]


def in_order(outputs, dh, condition_grad, g_w_ada, biases, weights):
    return (
        outputs,
        dh,
        condition_grad,
        g_w_ada,
        biases[0],
        weights[0],
        biases[1],
        weights[1],
        biases[2],
        weights[2],
        biases[3],
        weights[3],
        biases[4],
    )


def local_plain(
    latents,
    condition,
    output_grad,
    w_ada,
    b_ada,
    query_key_value_weight,
    b_qv,
    output_matrix_weight,
    b_proj,
    first_linear_weight,
    b_fc1,
    second_linear_weight,
    b_fc2,
):
    layer_count, owned_rows, ada_width = w_ada.shape
    seq_count, length, features = latents.shape
    shard, shards = lax.axis_index("shard"), lax.axis_size("shard")
    every = ("far", "near", "core", "shard")
    biases = (b_ada, b_qv, b_proj, b_fc1, b_fc2)
    widths = [b.shape[1] for b in biases]

    cond_value = condition.astype(f32)
    silu_low = jax.nn.silu(cond_value).astype(bf16)
    silu_group = lax.all_gather(silu_low, "shard", axis=0, tiled=True)
    silu_mine = lax.dynamic_slice_in_dim(silu_group, shard * owned_rows, owned_rows, 1)
    bias_all = lax.all_gather(jnp.concatenate(biases, axis=1), "shard", axis=0)
    full_biases = unpack_biases(bias_all, widths)
    mod_part = jnp.concatenate([mm(silu_mine, w_ada[l]) for l in range(layer_count)], axis=1)
    mod = lax.psum_scatter(mod_part, "shard", scatter_dimension=0, tiled=True)
    mod = mod.reshape(seq_count, layer_count, ada_width)
    silu_every = lax.all_gather(silu_low, every, axis=0, tiled=True)

    tokens = seq_count * length
    stream, blocks, weights = latents.astype(f32).reshape(tokens, features), [], []
    for l in range(layer_count):
        block = Block(mod[:, l] + full_biases[l][0], full_biases[l][1:], seq_count, length)
        full = [
            lax.all_gather(w[l], "shard", axis=0, tiled=True)
            for w in (
                query_key_value_weight,
                output_matrix_weight,
                first_linear_weight,
                second_linear_weight,
            )
        ]
        full[:2] = [jnp.concatenate(full[:2], axis=1)]
        block.attention(stream, full[0])
        block.hidden_layer(full[1])
        stream = block.output_layer(full[2], bf16 if l == layer_count - 1 else f32)
        blocks.append(block)
        weights.append(full)

    hidden_width = first_linear_weight.shape[2]

    def reduce(pair):
        grad = t_mm(*pair).astype(bf16)
        grad = lax.psum_scatter(grad, "shard", scatter_dimension=0, tiled=True)
        return lax.psum(grad, ("far", "near", "core")).astype(f32)

    dh = output_grad.reshape(tokens, features)
    grads, ada, owned, grad_silu = [None] * layer_count, None, [None] * layer_count, 0.0
    silu_owned = lax.dynamic_slice_in_dim(silu_every, shard * owned_rows, owned_rows, 1)
    for l in reversed(range(layer_count)):
        block, full = blocks[l], weights[l]
        second = block.back_start(dh)
        first = block.back_hidden(full[2])
        out = block.back_middle(full[1], full[0])
        qkv = block.back_attention()
        dh = block.back_end(full[0], block.grad_qkv)
        block.gate_sum()
        sums = packed_sums([block], silu_low, 8 * features + hidden_width)
        grad_mod = sums[0, :, : 6 * features]
        bias_sums = sums[1, 0, : 4 * features + hidden_width]
        grads[l] = [reduce(pair) for pair in (qkv, out, first, second)]
        mod_every = lax.all_gather(grad_mod, every, axis=0, tiled=True)
        silu = (silu_owned, silu_owned.shape, lambda j, p: (0, 0))
        place = jnp.zeros((1,), jnp.int32)
        ada = ada_weight(silu, mod_every, 0, ada_width, l, layer_count, ada, place)
        sums = lax.psum(bias_sums.astype(f32), every)
        owned[l] = owned_biases(mod_every, sums, shard, widths, shards)
        mods_group = lax.all_gather(grad_mod, "shard", axis=0, tiled=True)
        grad_silu = grad_silu + mm_t(mods_group, w_ada[l])
    by_owner = grad_silu.reshape(shards, seq_count, owned_rows)
    got = lax.all_to_all(by_owner, "shard", 0, 0)
    grad_silu = jnp.moveaxis(got, 0, 1).reshape(seq_count, features)
    return in_order(
        stream.reshape(latents.shape),
        dh.reshape(latents.shape),
        silu_grad(cond_value, grad_silu),
        ada,
        [jnp.stack([o[m] for o in owned]) for m in range(5)],
        [jnp.stack([g[m] for g in grads]) for m in range(4)],
    )


def local_fast(
    latents,
    condition,
    output_grad,
    w_ada,
    b_ada,
    query_key_value_weight,
    b_qv,
    output_matrix_weight,
    b_proj,
    first_linear_weight,
    b_fc1,
    second_linear_weight,
    b_fc2,
):
    comm = Fast()
    layer_count, owned_rows, ada_width = w_ada.shape
    seq_count, length, features = latents.shape
    tokens = seq_count * length
    shard = comm.shard
    biases = (b_ada, b_qv, b_proj, b_fc1, b_fc2)
    widths = [b.shape[1] for b in biases]

    chunk_of = []
    for l in range(layer_count):
        chunk_of.append((l, (query_key_value_weight, output_matrix_weight)))
        chunk_of.append((l, (first_linear_weight,)))
        chunk_of.append((l, (second_linear_weight,)))
    chunks = len(chunk_of)
    sends = []
    for l, members in chunk_of:
        quarters = [comm.quarter(member, l) for member in members]
        sends.append(quarters[0] if len(quarters) == 1 else jnp.concatenate(quarters, axis=1))

    cond_value = condition.astype(f32)
    silu_low = jax.nn.silu(cond_value).astype(bf16)
    bias_mine = jnp.concatenate(biases, axis=1)
    latents_flat = latents.reshape(tokens, features)
    stream = latents_flat
    pieces = [[None] * 4 for _ in range(chunks)]
    weights = [None] * chunks
    blocks = [None] * layer_count
    outputs, place = None, comm.place + 0
    for step in range(0, chunks + 2):
        live = {}
        if step < chunks:
            live["a"] = swap(sends[step], "shard")
        at = step - 1
        if 0 <= at < chunks:
            live["b"] = swap(pieces[at][0], "near")
            live["a2"] = swap(pieces[at][0], "core")
        at = step - 2
        if 0 <= at < chunks:
            live["b2"] = swap(pieces[at][1], "core")
        if step == 0:
            live["later"] = silu_low, bias_mine
        elif step == 1:
            live["silu"] = swap(silu_low, "shard")
            live["bias"] = swap(bias_mine, "shard")
        elif step == 2:
            live["a2"], silu_mine = gate((live["a2"], silu_mine))
            mod_part = ada_product(silu_mine, w_ada)
            mod_send, mod_keep = comm.split(mod_part.reshape(2, seq_count, -1), "shard")
            live["mod"] = swap(mod_send, "shard")
        at = step - 3
        if at >= 0:
            l, part = at // 3, at % 3
            block = blocks[l]
            if part == 0:
                block.attention(stream, weights[at])
                live["done"] = block.mlp_in
            elif part == 1:
                block.hidden_layer(weights[at])
                live["done"] = block.hidden
            else:
                stream = block.output_layer(weights[at], f32)
                live["done"] = stream
        if step + 1 < chunks:
            live["send"] = sends[step + 1]
        early = {0: (0, 1), 1: (2, 3), 4: (4,), 5: (5,)}.get(step, ())
        live["own"] = [
            comm.assemble_own(chunk_of[k][1], chunk_of[k][0], place) for k in early
        ]
        live["place"] = place
        live = gate(live)
        for k, own in zip(early, live["own"]):
            weights[k] = own
        place = live["place"]
        if step + 1 < chunks:
            sends[step + 1] = live["send"]
        if step < chunks:
            pieces[step][0] = live["a"]
        if at >= 0:
            if part == 0:
                block.mlp_in = live["done"]
            elif part == 1:
                block.hidden = live["done"]
            else:
                stream = live["done"]
        at = step - 1
        if 0 <= at < chunks:
            pieces[at][1], pieces[at][2] = live["b"], live["a2"]
        at = step - 2
        if 0 <= at < chunks:
            pieces[at][3] = live["b2"]
            weights[at] = comm.assemble_rest(weights[at], pieces[at])
        if step == 0:
            silu_low, bias_mine = live["later"]
        elif step == 1:
            silu_pair = comm.ordered(silu_low, live["silu"], "shard")
            silu_pair = silu_pair.reshape(2 * seq_count, features)
            silu_mine = lax.dynamic_slice_in_dim(silu_pair, shard * owned_rows, owned_rows, 1)
            full_biases = unpack_biases(comm.ordered(bias_mine, live["bias"], "shard"), widths)
        elif step == 2:
            mod = (mod_keep + live["mod"]).reshape(seq_count, layer_count, ada_width)
            for l in range(layer_count):
                blocks[l] = Block(
                    mod[:, l] + full_biases[l][0], full_biases[l][1:], seq_count, length
                )
            stream = stream.astype(f32)

    units = 3 * layer_count
    last_step = units + 5
    pairs, core_send, first_send, keep, late, total, back, both = [
        [None] * units for _ in range(8)
    ]
    packed, ada = None, None
    bias_width = 2 * sum(widths[1:])
    packed_width = layer_count * ada_width + features
    small_plan = {
        (units + 1, 0): "z2",
        (units + 1, 1): "z1",
        (units + 2, 0): "near",
        (units + 2, 1): "shard",
        (units + 3, 0): "core",
    }
    dh = output_grad.reshape(tokens, features)
    next_in = dh
    weight_out, arrived = [None] * 4, []
    by_pairs = units // 2
    far_step = {0: 4, 1: 6, 2: 7, 4: 8, 5: 9}
    back_step = {0: 6, 1: 7, 2: 8, 3: 9, 4: 9, 5: 10}
    for step in range(0, last_step + 1):

        def unit_at(lag):
            return step - lag if 0 <= step - lag < units else None

        on_core, on_shard, on_near = unit_at(1), unit_at(2), unit_at(3)
        on_far = [unit for unit, at in far_step.items() if at == step]
        on_far = on_far[0] if on_far else None
        on_back = [unit for unit in (unit_at(5), unit_at(6)) if back_step.get(unit) == step]
        on_end = [unit for unit in (unit_at(6), unit_at(7)) if back_step.get(unit) == step - 1]
        out_far = by_pairs if unit_at(4) == by_pairs else None
        in_far = by_pairs if unit_at(5) == by_pairs else None
        live, fin = {}, {}
        if arrived:
            for entry in arrived:
                weight_out = finish(comm, *entry, layer_count, features, weight_out)
            fin["finals"], arrived = weight_out, []
        if on_core is not None:
            live["core"] = swap(core_send[on_core], "core")
        if on_shard is not None:
            fin["shard"] = swap(first_send[on_shard], "shard")
        if on_near is not None:
            fin["near"] = swap(late[on_near], "near")
        if on_far is not None:
            far = lax.psum(total[on_far], "far")
            if on_far:
                fin["far"] = far
        if step == far_step[0] + 1:
            fin["far"] = far
        waiting = [unit for unit, at in far_step.items() if at == step + 1 and at > unit + 4]
        if waiting:
            fin["hold"] = total[waiting[0]]
        if out_far is not None:
            live["z1"] = comm.far_swap(late[out_far], "z1")
        if in_far is not None:
            live["z2_back"] = comm.far_swap(total[in_far], "z2")
        if on_back:
            fin["back"] = [swap(back[unit], "near") for unit in on_back]
        if on_end:
            ends = [swap(both[unit], "core") for unit in on_end]
            (live if last_step - 2 <= step < last_step else fin)["end"] = ends
        if (step, 0) in small_plan:
            live["small"] = comm.any_swap(packed, small_plan[step, 0])
        if on_core is not None:
            got = live.pop("core")
            made = tuple(unit_sums(pairs[on_core], shard, comm.core, got))
            (live if step < units else fin)["made"] = made
        if step < units:
            l, part = layer_count - 1 - step // 3, step % 3
            block = blocks[l]
            w_attn, w_fc1, w_fc2 = weights[3 * l : 3 * l + 3]
            if part == 0:
                if step:
                    next_in = blocks[l + 1].back_end(weights[3 * (l + 1)], next_in)
                pairs[step] = [block.back_start(next_in)]
                next_in = block.grad_out
            elif part == 1:
                block.grad_out = next_in
                pairs[step] = [block.back_hidden(w_fc2)]
                next_in = block.grad_pre
            else:
                block.grad_pre = next_in
                middle = block.back_middle(w_fc1, w_attn)
                next_in = block.grad_attn
            live["next"] = next_in
        if step == units:
            dh = blocks[0].back_end(weights[0], next_in)
            outputs = blocks[layer_count - 1].output_layer(weights[3 * layer_count - 1], bf16)
            for block in blocks:
                block.gate_sum()
            fin["packed"] = packed_sums(blocks, silu_low, packed_width)
            fin["outputs"] = outputs, dh
        if step == units + 2:
            live["mods"] = mods_got
        live = gate(live) if live else live
        if step == units + 2:
            mods_both = comm.ordered(mods_mine, live["mods"], "shard")
            fin["silu_part"] = ada_back(mods_both.reshape(2 * seq_count, -1), w_ada)
        if "made" in live:
            first_send[on_core], keep[on_core] = live["made"]
        if "end" in live:
            for unit, got in zip(on_end, live["end"]):
                entry = both[unit], got, unit
                weight_out = finish(comm, *entry, layer_count, features, weight_out)
            fin["finals"], on_end = weight_out, []
        if out_far is not None:
            late[out_far], total[out_far] = comm.far_split(total[out_far], live["z1"], "z2")
            fin["z2"] = comm.far_swap(late[out_far], "z2")
        if in_far is not None:
            total[in_far] = comm.far_ordered(total[in_far], live["z2_back"], "z2")
            fin["z1_back"] = comm.far_swap(total[in_far], "z1")
        if "small" in live:
            packed = pack(packed, live["small"])
        if step == units + 3:
            fin["silu"] = swap(silu_send, "shard")
        if step == units + 3:
            count = packed.shape[0] - 1
            every = packed[:count].reshape(count * seq_count, packed_width)
            owned = [
                owned_biases(
                    every[:, l * ada_width : (l + 1) * ada_width],
                    packed[count, l, :bias_width].astype(f32),
                    shard,
                    widths,
                    2,
                )
                for l in range(layer_count)
            ]
            silu_block = (every.shape[0], owned_rows)
            silu_at = layer_count * ada_width // owned_rows
            for l in range(layer_count):
                ada = ada_weight(
                    (every, silu_block, lambda j, p: (0, silu_at + p[0])),
                    every,
                    l * ada_width,
                    ada_width,
                    l,
                    layer_count,
                    ada,
                    comm.place,
                )
            fin["ada"] = ada
        if (step, 1) in small_plan:
            fin["small"] = comm.any_swap(packed, small_plan[step, 1])
        if step == units + 1:
            fin["mods"] = swap(mods_mine, "shard")
        if step < units:
            next_in = live["next"]
            if part < 2:
                pairs[step] = [(pairs[step][0][0], next_in)]
            else:
                block.grad_attn = next_in
                pairs[step] = [block.back_attention(), middle]
                next_in = block.grad_qkv
            fin["next"] = next_in
            fin["send"] = unit_part(pairs[step], 1 - comm.core)
        if step == last_step:
            live = fin
        else:
            live = gate(fin)
        if "finals" in live:
            weight_out = live["finals"]
        if "made" in live:
            first_send[on_core], keep[on_core] = live["made"]
        if step < units:
            core_send[step], next_in = live["send"], live["next"]
            pairs[step][0] = (pairs[step][0][0], next_in)
        if on_shard is not None:
            shape = (2, keep[on_shard].shape[0] // 2, keep[on_shard].shape[1])
            sent, kept = comm.split(keep[on_shard].reshape(shape), "near")
            got_sent, got_kept = comm.split(live["shard"].reshape(shape), "near")
            late[on_shard], total[on_shard] = add(sent, got_sent), add(kept, got_kept)
        if on_near is not None and on_near == by_pairs:
            late[on_near], total[on_near] = comm.far_split(total[on_near], live["near"], "z1")
        elif on_near is not None:
            total[on_near] = add(total[on_near], live["near"])
        if out_far is not None:
            total[out_far] = add(total[out_far], live["z2"])
        if in_far is not None:
            back[in_far] = comm.far_ordered(total[in_far], live["z1_back"], "z1")
        if "hold" in live:
            total[waiting[0]] = live["hold"]
        if "far" in live:
            back[on_far or 0] = live["far"]
        for unit, got in zip(on_back, live.get("back", ())):
            both[unit] = jnp.stack([back[unit], got])
        for unit, got in zip(on_end, live.get("end", ())):
            arrived.append((both[unit], got, unit))
        if "ada" in live:
            ada = live["ada"]
        if "silu" in live:
            grad_silu = comm.ordered(silu_keep, live["silu"], "shard", at=1)
            grad_silu = grad_silu.reshape(seq_count, features)
        if step == units:
            outputs, dh = live["outputs"]
            packed = live["packed"]
            mods_mine = packed[0, :, : layer_count * ada_width]
        if "small" in live:
            packed = pack(packed, live["small"])
        if "mods" in live:
            mods_got = live["mods"]
        if "silu_part" in live:
            silu_part = live["silu_part"]
            silu_send, silu_keep = comm.split(
                silu_part.reshape(2, seq_count, owned_rows), "shard"
            )
    for entry in arrived:
        weight_out = finish(comm, *entry, layer_count, features, weight_out)
    return in_order(
        outputs.reshape(latents.shape),
        dh.reshape(latents.shape),
        silu_grad(cond_value, grad_silu),
        ada,
        [jnp.stack([o[m] for o in owned]) for m in range(5)],
        weight_out,
    )


def pack(mine, got):
    count = mine.shape[0] - 1
    return jnp.concatenate([mine[:count], got[:count], add(mine[count:], got[count:])], 0)


def finish(comm, mine, got, unit, layer_count, features, weight_out):
    layer, part = layer_count - 1 - unit // 3, unit % 3
    width = mine.shape[2]
    qkv, out, first, second = weight_out
    if part == 0:
        (second,) = comm.final(mine, got, layer, [(width, second)])
    elif part == 1:
        (first,) = comm.final(mine, got, layer, [(width, first)])
    else:
        half = features // 2
        qkv, out = comm.final(mine, got, layer, [(width - half, qkv), (half, out)])
    return [qkv, out, first, second]


def solution(mesh):
    rep, shard = mesh.shape["rep"], mesh.shape["shard"]
    core = 2 if rep % 2 == 0 else 1
    near = 2 if rep == 16 else 1
    far = rep // (core * near)
    fast = (far, near, core, shard) == (4, 2, 2, 2)
    fine = Mesh(
        np.asarray(mesh.devices).reshape(far, near, core, shard),
        ("far", "near", "core", "shard"),
    )
    every = ("far", "near", "core", "shard")
    row, row3 = P(every, None), P(every, None, None)
    bias, weight = P(None, "shard"), P(None, "shard", None)
    return jax.shard_map(
        local_fast if fast else local_plain,
        mesh=fine,
        in_specs=(
            row3, row, row3, weight, bias, weight, bias, weight, bias, weight, bias, weight, bias,
        ),
        out_specs=(
            row3, row3, row, weight, bias, weight, bias, weight, bias, weight, bias, weight, bias,
        ),
        check_vma=False,
    )
```

```python
import functools

import jax
import jax.numpy as jnp
import numpy as np
from jax import lax
from jax.experimental import pallas as pl
from jax.experimental.pallas import tpu as pltpu
from jax.sharding import Mesh
from jax.sharding import PartitionSpec as P

HEADS = 12
eps = 1e-06
f32 = jnp.float32
bf16 = jnp.bfloat16


def normalize(rows):
    centred = rows - jnp.mean(rows, axis=-1, keepdims=True)
    inverse = lax.rsqrt(jnp.mean(centred * centred, axis=-1, keepdims=True) + eps)
    return (centred * inverse, inverse)


def norm_back(upstream, normed, inverse):
    return inverse * (
        upstream
        - jnp.mean(upstream, axis=-1, keepdims=True)
        - normed * jnp.mean(upstream * normed, axis=-1, keepdims=True)
    )


def gelu_and_slope(u):
    square = u * u
    t = jnp.tanh(u * (0.7978845608028654 + 0.7978845608028654 * 0.044715 * square))
    half = 0.5 + 0.5 * t
    inner_slope = 0.7978845608028654 + 3.0 * 0.7978845608028654 * 0.044715 * square
    return u * half, half + 0.5 * u * (1.0 - t * t) * inner_slope


def mm(a, b):
    return jnp.dot(a, b, preferred_element_type=f32)


def mm_t(a, b):
    return lax.dot_general(a, b, (((1,), (1,)), ((), ())), preferred_element_type=f32)


def t_mm(a, b):
    return lax.dot_general(a, b, (((0,), (0,)), ((), ())), preferred_element_type=f32)


def pick(array, index, axis=0):
    return lax.dynamic_index_in_dim(array, index, axis, keepdims=False)


SWAP = [(0, 1), (1, 0)]
CHEAP = pl.CostEstimate(flops=1, bytes_accessed=1, transcendentals=0)
PARAMS = pltpu.CompilerParams(vmem_limit_bytes=60 * 2**20)


def swap(value, axis):
    return lax.ppermute(value, axis, SWAP)


def gate(tree):
    values, shape = jax.tree.flatten(tree)
    count = len(values)

    def nothing(*refs):
        pass

    out = pl.pallas_call(
        nothing,
        out_shape=[jax.ShapeDtypeStruct(v.shape, v.dtype) for v in values],
        in_specs=[pl.BlockSpec(memory_space=pl.ANY)] * count,
        out_specs=[pl.BlockSpec(memory_space=pl.ANY)] * count,
        input_output_aliases={i: i for i in range(count)},
        cost_estimate=CHEAP,
        compiler_params=PARAMS,
    )(*values)
    return jax.tree.unflatten(shape, out)


def call(kernel, grid, ins, outs, prefetch=(), aliases=None):
    def spec(block, index, once=False):
        if block is None:
            return pl.BlockSpec(memory_space=pl.ANY)
        if once:
            return pl.BlockSpec(block, index, pipeline_mode=pl.Buffered(1))
        return pl.BlockSpec(block, index)

    return pl.pallas_call(
        kernel,
        out_shape=[jax.ShapeDtypeStruct(shape, dtype) for shape, dtype, _, _ in outs],
        grid_spec=pltpu.PrefetchScalarGridSpec(
            num_scalar_prefetch=len(prefetch),
            grid=grid,
            in_specs=[spec(*entry[1:]) for entry in ins],
            out_specs=[spec(block, index) for _, _, block, index in outs],
        ),
        input_output_aliases=aliases or {},
        cost_estimate=CHEAP,
        compiler_params=PARAMS,
    )(*prefetch, *[entry[0] for entry in ins])


class Block:
    def __init__(self, mod, biases, seq_count, length):
        self.mod = mod.reshape(seq_count, 6, -1)
        self.biases = biases
        self.seq_count, self.length = seq_count, length
        self.features = self.mod.shape[2]

    def rows(self, array):
        return (array, (self.length, array.shape[1]), lambda s: (s, 0))

    def rows_out(self, width, dtype):
        shape = (self.seq_count * self.length, width)
        return (shape, dtype, (self.length, width), lambda s: (s, 0))

    def mods(self):
        return (self.mod, (None, 6, self.features), lambda s: (s, 0, 0))

    def sums_out(self):
        return (
            (self.seq_count, 8, self.features),
            f32,
            (None, 8, self.features),
            lambda s: (s, 0, 0),
        )

    @staticmethod
    def whole(array):
        return (array, array.shape, lambda s: (0,) * array.ndim, True)

    @staticmethod
    def columns(array, start, width):
        return (array, (array.shape[0], width), lambda s: (0, start // width), True)

    def attention(self, stream, w_attn):
        features, length = self.features, self.length
        bias_qv = self.biases[0]
        bias = jnp.concatenate(
            [bias_qv[:features], jnp.zeros((features,), f32), bias_qv[features:], self.biases[1]]
        )[None]
        head = features // HEADS
        factor = head ** (-0.5)

        def kernel(
            stream_ref, mod_ref, w_ref, bias_ref,
            in_ref, qkv_ref, out_ref, branch_ref, middle_ref, mlp_ref,
        ):
            normed, _ = normalize(stream_ref[...])
            attn_in = (normed * (1.0 + mod_ref[1:2]) + mod_ref[0:1]).astype(bf16)
            in_ref[...] = attn_in
            wide = 3 * features
            for at in range(0, wide, features):
                columns = slice(at, at + features)
                qkv_ref[:, columns] = (
                    mm(attn_in, w_ref[:, columns]) + bias_ref[:, columns]
                ).astype(bf16)
            for start in range(0, features, 128):
                q, k, v = [
                    qkv_ref[:, part * features + start : part * features + start + 128]
                    for part in range(3)
                ]
                total = jnp.zeros((length, 128), f32)
                for mask in head_masks(length, head):
                    probs = probs_of(jnp.where(mask, q, 0), k, factor).astype(bf16)
                    total = total + mm(probs, jnp.where(mask, v, 0))
                out_ref[:, start : start + 128] = total.astype(bf16)
            branch = mm(out_ref[...], w_ref[:, wide:]) + bias_ref[:, wide:]
            middle = stream_ref[...] + mod_ref[2:3] * branch
            normed, _ = normalize(middle)
            branch_ref[...] = branch
            middle_ref[...] = middle
            mlp_ref[...] = (normed * (1.0 + mod_ref[4:5]) + mod_ref[3:4]).astype(bf16)

        self.stream = stream
        self.attn_in, self.qkv, self.attn_out, self.branch, self.middle, self.mlp_in = call(
            kernel,
            (self.seq_count,),
            [self.rows(stream), self.mods(), self.whole(w_attn), self.whole(bias)],
            [
                self.rows_out(features, bf16),
                self.rows_out(3 * features, bf16),
                self.rows_out(features, bf16),
                self.rows_out(features, f32),
                self.rows_out(features, f32),
                self.rows_out(features, bf16),
            ],
        )

    def hidden_layer(self, w_fc1):
        hidden, tile, tokens = w_fc1.shape[1], self.features, self.seq_count * self.length

        def kernel(in_ref, w_ref, bias_ref, slope_ref, hidden_ref):
            value, slope = gelu_and_slope(mm(in_ref[...], w_ref[...]) + bias_ref[...])
            slope_ref[...] = slope.astype(bf16)
            hidden_ref[...] = value.astype(bf16)

        out = ((tokens, hidden), bf16, (tokens, tile), lambda j: (0, j))
        self.slope, self.hidden = call(
            kernel,
            (hidden // tile,),
            [
                (self.mlp_in, (tokens, self.features), lambda j: (0, 0)),
                (w_fc1, (self.features, tile), lambda j: (0, j)),
                (self.biases[2][None], (1, tile), lambda j: (0, j)),
            ],
            [out, out],
        )

    def output_layer(self, w_fc2, dtype):
        def kernel(hidden_ref, middle_ref, mod_ref, w_ref, bias_ref, output_ref, stream_ref):
            output = mm(hidden_ref[...], w_ref[...]) + bias_ref[...]
            output_ref[...] = output
            stream_ref[...] = (middle_ref[...] + mod_ref[5:6] * output).astype(dtype)

        self.output, stream = call(
            kernel,
            (self.seq_count,),
            [
                self.rows(self.hidden),
                self.rows(self.middle),
                self.mods(),
                self.whole(w_fc2),
                self.whole(self.biases[3][None]),
            ],
            [self.rows_out(self.features, f32), self.rows_out(self.features, dtype)],
        )
        return stream

    def back_start(self, dh):
        def kernel(dh_ref, mod_ref, grad_ref, sums_ref):
            grad_out = (mod_ref[5:6] * dh_ref[...].astype(f32)).astype(bf16)
            grad_ref[...] = grad_out
            sums_ref[0:1] = jnp.sum(grad_out.astype(f32), axis=0, keepdims=True)

        self.dh = dh
        self.grad_out, self.sums_out2 = call(
            kernel,
            (self.seq_count,),
            [self.rows(dh), self.mods()],
            [self.rows_out(self.features, bf16), self.sums_out()],
        )
        return (self.hidden, self.grad_out)

    def back_hidden(self, w_fc2):
        hidden, tile, tokens = w_fc2.shape[0], self.features, self.seq_count * self.length

        def kernel(grad_ref, slope_ref, w_ref, out_ref, sum_ref):
            grad_hidden = mm_t(grad_ref[...], w_ref[...])
            grad_pre = (grad_hidden * slope_ref[...].astype(f32)).astype(bf16)
            out_ref[...] = grad_pre
            sum_ref[...] = jnp.sum(grad_pre.astype(f32), axis=0, keepdims=True)

        self.grad_pre, self.sum_fc1 = call(
            kernel,
            (hidden // tile,),
            [
                (self.grad_out, (tokens, self.features), lambda j: (0, 0)),
                (self.slope, (tokens, tile), lambda j: (0, j)),
                (w_fc2, (tile, self.features), lambda j: (j, 0)),
            ],
            [
                ((tokens, hidden), bf16, (tokens, tile), lambda j: (0, j)),
                ((1, hidden), f32, (1, tile), lambda j: (0, j)),
            ],
        )
        return (self.mlp_in, self.grad_pre)

    def back_middle(self, w_fc1, w_attn):
        def kernel(
            grad_ref, w1_ref, dh_ref, middle_ref, mod_ref, branch_ref, wo_ref,
            mid_ref, gb_ref, ga_ref, sums_ref,
        ):
            grad_in = mm_t(grad_ref[...], w1_ref[...])
            normed, inverse = normalize(middle_ref[...])
            dh = dh_ref[...].astype(f32)
            mid = dh + norm_back(grad_in * (1.0 + mod_ref[4:5]), normed, inverse)
            grad_branch = (mod_ref[2:3] * mid).astype(bf16)
            mid_ref[...] = mid
            gb_ref[...] = grad_branch
            ga_ref[...] = mm_t(grad_branch, wo_ref[...]).astype(bf16)
            for at, value in enumerate(
                (
                    mid * branch_ref[...],
                    grad_in,
                    grad_in * normed,
                    grad_branch.astype(f32),
                )
            ):
                sums_ref[at : at + 1] = jnp.sum(value, axis=0, keepdims=True)

        self.grad_mid, self.grad_branch, self.grad_attn, self.sums_mid = call(
            kernel,
            (self.seq_count,),
            [
                self.rows(self.grad_pre),
                self.whole(w_fc1),
                self.rows(self.dh),
                self.rows(self.middle),
                self.mods(),
                self.rows(self.branch),
                self.columns(w_attn, 3 * self.features, self.features),
            ],
            [
                self.rows_out(self.features, f32),
                self.rows_out(self.features, bf16),
                self.rows_out(self.features, bf16),
                self.sums_out(),
            ],
        )
        return (self.attn_out, self.grad_branch)

    def gate_sum(self):
        def kernel(dh_ref, output_ref, sums_ref):
            product = dh_ref[...].astype(f32) * output_ref[...]
            sums_ref[0:1] = jnp.sum(product, axis=0, keepdims=True)

        self.sums_gate = call(
            kernel,
            (self.seq_count,),
            [self.rows(self.dh), self.rows(self.output)],
            [self.sums_out()],
        )[0]

    def back_attention(self):
        self.grad_qkv = attention_backward(self.qkv, self.grad_attn, self.seq_count)
        return (self.attn_in, self.grad_qkv)

    def back_end(self, w_attn, grad_qkv):
        features = self.features

        def kernel(grad_ref, w_ref, stream_ref, mod_ref, mid_ref, dh_ref, sums_ref):
            grad_qkv = grad_ref[...]
            grad_in = mm_t(grad_qkv, w_ref[...])
            normed, inverse = normalize(stream_ref[...].astype(f32))
            dh_ref[...] = mid_ref[...] + norm_back(
                grad_in * (1.0 + mod_ref[1:2]), normed, inverse
            )
            for at, value in enumerate((grad_in, grad_in * normed)):
                sums_ref[at : at + 1] = jnp.sum(value, axis=0, keepdims=True)
            for part in range(3):
                columns = grad_qkv[:, part * features : (part + 1) * features].astype(f32)
                sums_ref[2 + part : 3 + part] = jnp.sum(columns, axis=0, keepdims=True)

        dh, self.sums_end = call(
            kernel,
            (self.seq_count,),
            [
                self.rows(grad_qkv),
                self.columns(w_attn, 0, 3 * features),
                self.rows(self.stream),
                self.mods(),
                self.rows(self.grad_mid),
            ],
            [self.rows_out(features, f32), self.sums_out()],
        )
        return dh

    def sum_parts(self):
        return [self.sums_end, self.sums_mid, self.sums_gate, self.sums_out2, self.sum_fc1]


def packed_sums(blocks, silu_low, width):
    seq_count, features = silu_low.shape
    parts = [part for block in blocks for part in block.sum_parts()]

    def kernel(*refs):
        silu_ref, out_ref = refs[-2], refs[-1]
        out_ref[...] = jnp.zeros(out_ref.shape, bf16)
        for l in range(len(blocks)):
            end, mid, gate_m, out2, fc1 = refs[5 * l : 5 * l + 5]
            rows = [(end, 0), (end, 1), (mid, 0), (mid, 1), (mid, 2), (gate_m, 0)]
            for s in range(seq_count):
                for k, (ref, row) in enumerate(rows):
                    at = (6 * l + k) * features
                    out_ref[0, s : s + 1, at : at + features] = ref[s, row : row + 1].astype(
                        bf16
                    )
            at = 0
            for ref, row in ((end, 2), (end, 4), (mid, 3), (fc1, None), (out2, 0)):
                if row is None:
                    total = ref[...]
                else:
                    total = ref[0, row : row + 1]
                    for s in range(1, seq_count):
                        total = total + ref[s, row : row + 1]
                out_ref[1, l : l + 1, at : at + total.shape[1]] = total.astype(bf16)
                at += total.shape[1]
        at = 6 * len(blocks) * features
        out_ref[0, :, at : at + features] = silu_ref[...]

    shape = (2, seq_count, width)
    return call(
        kernel,
        (1,),
        [Block.whole(part) for part in parts + [silu_low]],
        [(shape, bf16, shape, lambda s: (0, 0, 0))],
    )[0]


def probs_of(q, k, factor):
    scores = mm_t(q, k) * factor
    raised = jnp.exp(scores - jnp.max(scores, axis=-1, keepdims=True))
    return raised * (1.0 / jnp.sum(raised, axis=-1, keepdims=True))


def head_masks(rows, head):
    lane = lax.broadcasted_iota(jnp.int32, (rows, 128), 1)
    return [jnp.logical_and(lane >= at, lane < at + head) for at in range(0, 128, head)]


def attention_backward(qkv, grad, count):
    tokens, triple = qkv.shape
    width, length, head = triple // 3, tokens // count, triple // 3 // HEADS
    tile = 384 if width % 384 == 0 else width
    steps = width // tile
    factor = head ** (-0.5)

    def kernel(q_ref, k_ref, v_ref, g_ref, out_ref):
        for start in range(0, tile, 128):
            group = slice(start, start + 128)
            q, k, v, g = q_ref[:, group], k_ref[:, group], v_ref[:, group], g_ref[:, group]
            grad_q = jnp.zeros((length, 128), f32)
            grad_k = jnp.zeros((length, 128), f32)
            grad_v = jnp.zeros((length, 128), f32)
            for mask in head_masks(length, head):
                own_q, own_g = jnp.where(mask, q, 0), jnp.where(mask, g, 0)
                probs = probs_of(own_q, k, factor)
                grad_probs = mm_t(own_g, v)
                row_terms = jnp.sum(grad_probs * probs, axis=-1, keepdims=True)
                grad_scores = (probs * (grad_probs - row_terms)).astype(bf16)
                grad_q = grad_q + mm(grad_scores, jnp.where(mask, k, 0))
                grad_k = grad_k + t_mm(grad_scores, own_q)
                grad_v = grad_v + t_mm(probs.astype(bf16), own_g)
            at = pl.program_id(1) * tile + start
            for part, value in enumerate((grad_q * factor, grad_k * factor, grad_v)):
                columns = pl.ds(pl.multiple_of(part * width + at, 128), 128)
                out_ref[:, columns] = value.astype(bf16)

    def part(which):
        return (qkv, (length, tile), lambda s, g: (s, which * steps + g))

    return call(
        kernel,
        (count, steps),
        [part(0), part(1), part(2), (grad, (length, tile), lambda s, g: (s, g))],
        [((tokens, triple), bf16, (length, triple), lambda s, g: (s, 0))],
    )[0]


TILE = 384


def product_part(lhs, rhs, col_half, into, at, width):
    tokens, rows = lhs.shape
    half = rhs.shape[1] // 2
    tile = TILE if half > 1024 else min(rows, 4 * TILE)
    shift = at // half
    place = jnp.asarray(col_half, jnp.int32).reshape(1)
    ins = [
        (lhs, (tokens, tile), lambda i, p: (0, i)),
        (rhs, (tokens, half), lambda i, p: (0, p[0])),
    ]
    aliases = {}
    if into is not None:
        aliases = {3: 0}
        ins.append((into, None, None))

    def kernel(place_ref, lhs_ref, rhs_ref, *refs):
        refs[-1][...] = t_mm(lhs_ref[...], rhs_ref[...]).astype(bf16)

    return call(
        kernel,
        (rows // tile,),
        ins,
        [((rows, width), bf16, (tile, half), lambda i, p: (i, shift))],
        prefetch=(place,),
        aliases=aliases,
    )[0]


def product_sums(lhs, rhs, shard, col_half, got, into, at, width):
    tokens, rows = lhs.shape
    half = rhs.shape[1] // 2
    place = jnp.stack([shard, col_half]).astype(jnp.int32)
    size = rows // 2
    shape = (size, width)
    aliases = {}
    if into is not None:
        aliases = {4: 0, 5: 1}
    extra = [(part, None, None) for part in into or ()]
    if half > TILE or rows <= 2 * TILE:
        tile = 512 if half % 512 == 0 and at % 512 == 0 else TILE
        tiles, shift = half // tile, at // tile

        def kernel(place_ref, lhs_ref, rhs_ref, got_ref, *refs):
            send_ref, keep_ref = refs[-2:]
            total = t_mm(lhs_ref[...], rhs_ref[...]) + got_ref[...].astype(f32)
            total = total.astype(bf16)
            first = place_ref[0] == 0
            send_ref[...] = jnp.where(first, total[size:], total[:size])
            keep_ref[...] = jnp.where(first, total[:size], total[size:])

        out = (shape, bf16, (size, tile), lambda j, p: (0, shift + j))
        return call(
            kernel,
            (tiles,),
            [
                (lhs, (tokens, rows), lambda j, p: (0, 0)),
                (rhs, (tokens, tile), lambda j, p: (0, p[1] * tiles + j)),
                (got, (rows, tile), lambda j, p: (0, shift + j)),
            ]
            + extra,
            [out, out],
            prefetch=(place,),
            aliases=aliases,
        )
    shift = at // half

    def row_tile(side, p):
        return jnp.where(side == 0, 1 - p[0], p[0])

    def tall_kernel(place_ref, lhs_ref, rhs_ref, got_ref, *refs):
        send_ref, keep_ref = refs[-2:]
        total = t_mm(lhs_ref[...], rhs_ref[...]) + got_ref[...].astype(f32)

        @pl.when(pl.program_id(0) == 0)
        def _():
            send_ref[...] = total.astype(bf16)

        @pl.when(pl.program_id(0) == 1)
        def _():
            keep_ref[...] = total.astype(bf16)

    out = (shape, bf16, (size, half), lambda side, p: (0, shift))
    return call(
        tall_kernel,
        (2,),
        [
            (lhs, (tokens, size), lambda side, p: (0, row_tile(side, p))),
            (rhs, (tokens, half), lambda side, p: (0, p[1])),
            (got, (size, half), lambda side, p: (row_tile(side, p), shift)),
        ]
        + extra,
        [out, out],
        prefetch=(place,),
        aliases=aliases,
    )


def unit_part(pairs, col_half):
    width = sum(rhs.shape[1] // 2 for _, rhs in pairs)
    out, at = None, 0
    for lhs, rhs in pairs:
        out = product_part(lhs, rhs, col_half, out, at, width)
        at += rhs.shape[1] // 2
    return out


def unit_sums(pairs, shard, col_half, got):
    width = sum(rhs.shape[1] // 2 for _, rhs in pairs)
    out, at = None, 0
    for lhs, rhs in pairs:
        out = product_sums(lhs, rhs, shard, col_half, got, out, at, width)
        at += rhs.shape[1] // 2
    return out


class Fast:
    def __init__(self):
        self.near = lax.axis_index("near")
        self.core = lax.axis_index("core")
        self.shard = lax.axis_index("shard")
        self.place = jnp.stack([self.shard, self.near, self.core]).astype(jnp.int32)

    def ordered(self, mine, got, axis, at=0):
        first = lax.axis_index(axis) == 0
        return jnp.stack([jnp.where(first, mine, got), jnp.where(first, got, mine)], axis=at)

    def split(self, stack, axis, at=0):
        me = lax.axis_index(axis)
        return pick(stack, 1 - me, at), pick(stack, me, at)

    def quarter(self, stacked, layer):
        size = stacked.shape[1] // 4
        start = (self.near * 2 + self.core) * size
        return lax.dynamic_slice(stacked, (layer, start, 0), (1, size, stacked.shape[2]))[0]

    def assemble_own(self, members, layer, place):
        rows = members[0].shape[1]
        widths = [member.shape[2] for member in members]
        size = rows // 2

        def kernel(place_ref, *refs):
            at = 0
            for member_ref, member_width in zip(refs, widths):
                refs[-1][:, at : at + member_width] = member_ref[...]
                at += member_width

        ins = [
            (member, (None, size, member.shape[2]), lambda s, p: (layer, s, 0))
            for member in members
        ]
        shape = (2 * rows, sum(widths))
        block = (size, sum(widths))
        return call(
            kernel,
            (2,),
            ins,
            [(shape, members[0].dtype, block, lambda s, p: (p[0] * 2 + s, 0))],
            prefetch=(place,),
        )[0]

    def assemble_rest(self, whole, pieces):
        size, width = pieces[0].shape

        def out_block(step, place):
            shard, near = place[0], place[1]
            return (1 - shard) * 2 + jnp.where(step == 0, near, 1 - near), 0

        def kernel(place_ref, *refs):
            out_ref, core = refs[-1], place_ref[2]
            for step in range(2):
                for mine in range(2):

                    @pl.when(jnp.logical_and(pl.program_id(0) == step, core == mine))
                    def _(step=step, mine=mine):
                        out_ref[mine * size : (mine + 1) * size] = refs[step][...]
                        out_ref[(1 - mine) * size : (2 - mine) * size] = refs[2 + step][...]

        ins = [(piece, (size, width), lambda s, p: (0, 0)) for piece in pieces]
        ins.append((whole, None, None))
        return call(
            kernel,
            (2,),
            ins,
            [(whole.shape, whole.dtype, (2 * size, width), out_block)],
            prefetch=(self.place,),
            aliases={5: 0},
        )[0]

    def final(self, mine, got, layer, parts):
        rows = mine.shape[1]
        widths = [width for width, _ in parts]

        def out_block(step, place):
            near = place[1]
            return layer, jnp.where(step == 0, near, 1 - near), 0

        def kernel(place_ref, mine_ref, got_ref, *refs):
            outs, core = refs[-len(parts) :], place_ref[2]
            for first in range(2):
                low, high = (mine_ref, got_ref) if first == 0 else (got_ref, mine_ref)

                @pl.when(core == first)
                def _(low=low, high=high):
                    at = 0
                    for out_ref, width in zip(outs, widths):
                        out_ref[:, :width] = low[:, at : at + width].astype(f32)
                        out_ref[:, width:] = high[:, at : at + width].astype(f32)
                        at += width

        block = (None, rows, mine.shape[2])
        ins = [(array, block, lambda i, p: (i, 0, 0)) for array in (mine, got)]
        aliases = {}
        for at, (_, into) in enumerate(parts):
            if into is not None:
                aliases[1 + len(ins)] = at
                ins.append((into, None, None))
        return call(
            kernel,
            (2,),
            ins,
            [
                ((2, 2 * rows, 2 * width), f32, (None, rows, 2 * width), out_block)
                for width in widths
            ],
            prefetch=(self.place,),
            aliases=aliases,
        )

    def far_swap(self, value, name):
        step = 1 if name == "z1" else 2
        return lax.ppermute(value, "far", [(i, i ^ step) for i in range(4)])

    def far_side(self, name):
        far = lax.axis_index("far")
        return far % 2 if name == "z1" else far // 2

    def far_split(self, mine, got, name):
        side = self.far_side(name)
        shape = (2, mine.shape[0] // 2, mine.shape[1])
        mine, got = mine.reshape(shape), got.reshape(shape)
        return (
            add(pick(mine, 1 - side), pick(got, 1 - side)),
            add(pick(mine, side), pick(got, side)),
        )

    def far_ordered(self, mine, got, name):
        first = self.far_side(name) == 0
        return jnp.concatenate([jnp.where(first, mine, got), jnp.where(first, got, mine)], 0)

    def any_swap(self, value, name):
        return self.far_swap(value, name) if name in ("z1", "z2") else swap(value, name)


def ada_product(silu, w_ada):
    layers, rows, width = w_ada.shape
    tile = width // 2

    def kernel(silu_ref, w_ref, out_ref):
        out_ref[...] = mm(silu_ref[...], w_ref[...])

    return call(
        kernel,
        (layers, 2),
        [
            (silu, silu.shape, lambda l, j: (0, 0)),
            (w_ada, (None, rows, tile), lambda l, j: (l, 0, j)),
        ],
        [
            (
                (silu.shape[0], layers * width),
                f32,
                (silu.shape[0], tile),
                lambda l, j: (0, 2 * l + j),
            )
        ],
    )[0]


def ada_back(mods, w_ada):
    layers, rows, width = w_ada.shape
    tile = width // 2

    def kernel(mods_ref, w_ref, out_ref):
        first = jnp.logical_and(pl.program_id(0) == 0, pl.program_id(1) == 0)

        @pl.when(first)
        def _():
            out_ref[...] = jnp.zeros(out_ref.shape, f32)

        out_ref[...] += mm_t(mods_ref[...], w_ref[...])

    return call(
        kernel,
        (layers, 2),
        [
            (mods, (mods.shape[0], tile), lambda l, j: (0, 2 * l + j)),
            (w_ada, (None, rows, tile), lambda l, j: (l, 0, j)),
        ],
        [((mods.shape[0], rows), f32, (mods.shape[0], rows), lambda l, j: (0, 0))],
    )[0]


def ada_weight(silu, mods, start, width, layer, layers, into, place):
    count, rows = silu[1]
    tile = 768 if width % 768 == 0 and start % 768 == 0 else width
    first = start // tile

    def kernel(place_ref, silu_ref, mods_ref, *refs):
        refs[-1][...] = t_mm(silu_ref[...], mods_ref[...])

    ins = [silu, (mods, (count, tile), lambda j, p: (0, first + j))]
    aliases = {}
    if into is not None:
        aliases = {3: 0}
        ins.append((into, None, None))
    return call(
        kernel,
        (width // tile,),
        ins,
        [((layers, rows, width), f32, (None, rows, tile), lambda j, p: (layer, 0, j))],
        prefetch=(place,),
        aliases=aliases,
    )[0]


def add(a, b):
    return (a.astype(f32) + b.astype(f32)).astype(bf16)


def silu_grad(cond_value, grad_silu):
    _, silu_pull = jax.vjp(jax.nn.silu, cond_value)
    return silu_pull(grad_silu)[0]


def owned_biases(mod_every, bias_sums, shard, widths, shard_count):
    totals, at = [jnp.sum(mod_every.astype(f32), axis=0)], 0
    for width in widths[1:]:
        totals.append(bias_sums[at : at + width * shard_count])
        at += width * shard_count
    return [
        lax.dynamic_slice_in_dim(total, shard * width, width, 0)
        for total, width in zip(totals, widths)
    ]


def unpack_biases(bias_all, widths):
    cuts = np.cumsum(widths)[:-1]
    parts = [
        jnp.moveaxis(part, 0, 1).reshape(bias_all.shape[1], -1).astype(f32)
        for part in jnp.split(bias_all, cuts, axis=2)
    ]
    return [[part[l] for part in parts] for l in range(bias_all.shape[1])]


def in_order(outputs, dh, condition_grad, g_w_ada, biases, weights):
    return (
        outputs,
        dh,
        condition_grad,
        g_w_ada,
        biases[0],
        weights[0],
        biases[1],
        weights[1],
        biases[2],
        weights[2],
        biases[3],
        weights[3],
        biases[4],
    )


def local_plain(
    latents,
    condition,
    output_grad,
    w_ada,
    b_ada,
    query_key_value_weight,
    b_qv,
    output_matrix_weight,
    b_proj,
    first_linear_weight,
    b_fc1,
    second_linear_weight,
    b_fc2,
):
    layer_count, owned_rows, ada_width = w_ada.shape
    seq_count, length, features = latents.shape
    shard, shards = lax.axis_index("shard"), lax.axis_size("shard")
    every = ("far", "near", "core", "shard")
    biases = (b_ada, b_qv, b_proj, b_fc1, b_fc2)
    widths = [b.shape[1] for b in biases]

    cond_value = condition.astype(f32)
    silu_low = jax.nn.silu(cond_value).astype(bf16)
    silu_group = lax.all_gather(silu_low, "shard", axis=0, tiled=True)
    silu_mine = lax.dynamic_slice_in_dim(silu_group, shard * owned_rows, owned_rows, 1)
    bias_all = lax.all_gather(jnp.concatenate(biases, axis=1), "shard", axis=0)
    full_biases = unpack_biases(bias_all, widths)
    mod_part = jnp.concatenate([mm(silu_mine, w_ada[l]) for l in range(layer_count)], axis=1)
    mod = lax.psum_scatter(mod_part, "shard", scatter_dimension=0, tiled=True)
    mod = mod.reshape(seq_count, layer_count, ada_width)
    silu_every = lax.all_gather(silu_low, every, axis=0, tiled=True)

    tokens = seq_count * length
    stream, blocks, weights = latents.astype(f32).reshape(tokens, features), [], []
    for l in range(layer_count):
        block = Block(mod[:, l] + full_biases[l][0], full_biases[l][1:], seq_count, length)
        full = [
            lax.all_gather(w[l], "shard", axis=0, tiled=True)
            for w in (
                query_key_value_weight,
                output_matrix_weight,
                first_linear_weight,
                second_linear_weight,
            )
        ]
        full[:2] = [jnp.concatenate(full[:2], axis=1)]
        block.attention(stream, full[0])
        block.hidden_layer(full[1])
        stream = block.output_layer(full[2], bf16 if l == layer_count - 1 else f32)
        blocks.append(block)
        weights.append(full)

    hidden_width = first_linear_weight.shape[2]

    def reduce(pair):
        grad = t_mm(*pair).astype(bf16)
        grad = lax.psum_scatter(grad, "shard", scatter_dimension=0, tiled=True)
        return lax.psum(grad, ("far", "near", "core")).astype(f32)

    dh = output_grad.reshape(tokens, features)
    grads, ada, owned, grad_silu = [None] * layer_count, None, [None] * layer_count, 0.0
    silu_owned = lax.dynamic_slice_in_dim(silu_every, shard * owned_rows, owned_rows, 1)
    for l in reversed(range(layer_count)):
        block, full = blocks[l], weights[l]
        second = block.back_start(dh)
        first = block.back_hidden(full[2])
        out = block.back_middle(full[1], full[0])
        qkv = block.back_attention()
        dh = block.back_end(full[0], block.grad_qkv)
        block.gate_sum()
        sums = packed_sums([block], silu_low, 8 * features + hidden_width)
        grad_mod = sums[0, :, : 6 * features]
        bias_sums = sums[1, 0, : 4 * features + hidden_width]
        grads[l] = [reduce(pair) for pair in (qkv, out, first, second)]
        mod_every = lax.all_gather(grad_mod, every, axis=0, tiled=True)
        silu = (silu_owned, silu_owned.shape, lambda j, p: (0, 0))
        place = jnp.zeros((1,), jnp.int32)
        ada = ada_weight(silu, mod_every, 0, ada_width, l, layer_count, ada, place)
        sums = lax.psum(bias_sums.astype(f32), every)
        owned[l] = owned_biases(mod_every, sums, shard, widths, shards)
        mods_group = lax.all_gather(grad_mod, "shard", axis=0, tiled=True)
        grad_silu = grad_silu + mm_t(mods_group, w_ada[l])
    by_owner = grad_silu.reshape(shards, seq_count, owned_rows)
    got = lax.all_to_all(by_owner, "shard", 0, 0)
    grad_silu = jnp.moveaxis(got, 0, 1).reshape(seq_count, features)
    return in_order(
        stream.reshape(latents.shape),
        dh.reshape(latents.shape),
        silu_grad(cond_value, grad_silu),
        ada,
        [jnp.stack([o[m] for o in owned]) for m in range(5)],
        [jnp.stack([g[m] for g in grads]) for m in range(4)],
    )


def local_fast(
    latents,
    condition,
    output_grad,
    w_ada,
    b_ada,
    query_key_value_weight,
    b_qv,
    output_matrix_weight,
    b_proj,
    first_linear_weight,
    b_fc1,
    second_linear_weight,
    b_fc2,
):
    comm = Fast()
    layer_count, owned_rows, ada_width = w_ada.shape
    seq_count, length, features = latents.shape
    tokens = seq_count * length
    shard = comm.shard
    biases = (b_ada, b_qv, b_proj, b_fc1, b_fc2)
    widths = [b.shape[1] for b in biases]

    chunk_of = []
    for l in range(layer_count):
        chunk_of.append((l, (query_key_value_weight, output_matrix_weight)))
        chunk_of.append((l, (first_linear_weight,)))
        chunk_of.append((l, (second_linear_weight,)))
    chunks = len(chunk_of)
    sends = []
    for l, members in chunk_of:
        quarters = [comm.quarter(member, l) for member in members]
        sends.append(quarters[0] if len(quarters) == 1 else jnp.concatenate(quarters, axis=1))

    cond_value = condition.astype(f32)
    silu_low = jax.nn.silu(cond_value).astype(bf16)
    bias_mine = jnp.concatenate(biases, axis=1)
    latents_flat = latents.reshape(tokens, features)
    stream = latents_flat
    pieces = [[None] * 4 for _ in range(chunks)]
    weights = [None] * chunks
    blocks = [None] * layer_count
    outputs, place = None, comm.place + 0
    sends[0], silu_low = gate((sends[0], silu_low))
    stream = stream.astype(f32)
    for step in range(0, chunks + 1):
        live = {}
        if step < chunks:
            live["a"] = swap(sends[step], "shard")
        at = step - 1
        if 0 <= at < chunks:
            live["b"] = swap(pieces[at][0], "near")
            live["a2"] = swap(pieces[at][0], "core")
        if step == 0:
            live["silu"] = swap(silu_low, "shard")
            live["later"] = bias_mine
        elif step == 1:
            live["bias"] = swap(bias_mine, "shard")
            live["a2"], silu_mine = gate((live["a2"], silu_mine))
            mod_part = ada_product(silu_mine, w_ada)
            mod_send, mod_keep = comm.split(mod_part.reshape(2, seq_count, -1), "shard")
            live["mod"] = swap(mod_send, "shard")
        at = step - 2
        if at >= 0:
            pieces[at][3] = swap(pieces[at][1], "core")
            weights[at] = comm.assemble_rest(weights[at], pieces[at])
            l, part = at // 3, at % 3
            block = blocks[l]
            if part == 0:
                block.attention(stream, weights[at])
                live["done"] = block.mlp_in
            elif part == 1:
                block.hidden_layer(weights[at])
                live["done"] = block.hidden
            else:
                stream = block.output_layer(weights[at], f32)
                live["done"] = stream
        if step + 1 < chunks:
            live["send"] = sends[step + 1]
        early = {0: (0, 1, 2), 1: (3,), 3: (4,), 4: (5,)}.get(step, ())
        live["own"] = [
            comm.assemble_own(chunk_of[k][1], chunk_of[k][0], place) for k in early
        ]
        live["place"] = place
        live = gate(live)
        for k, own in zip(early, live["own"]):
            weights[k] = own
        place = live["place"]
        if step + 1 < chunks:
            sends[step + 1] = live["send"]
        if step < chunks:
            pieces[step][0] = live["a"]
        if at >= 0:
            if part == 0:
                block.mlp_in = live["done"]
            elif part == 1:
                block.hidden = live["done"]
            else:
                stream = live["done"]
        at = step - 1
        if 0 <= at < chunks:
            pieces[at][1], pieces[at][2] = live["b"], live["a2"]
        if step == 0:
            bias_mine = live["later"]
            silu_pair = comm.ordered(silu_low, live["silu"], "shard")
            silu_pair = silu_pair.reshape(2 * seq_count, features)
            silu_mine = lax.dynamic_slice_in_dim(silu_pair, shard * owned_rows, owned_rows, 1)
        elif step == 1:
            full_biases = unpack_biases(comm.ordered(bias_mine, live["bias"], "shard"), widths)
            mod = (mod_keep + live["mod"]).reshape(seq_count, layer_count, ada_width)
            for l in range(layer_count):
                blocks[l] = Block(
                    mod[:, l] + full_biases[l][0], full_biases[l][1:], seq_count, length
                )
    at = chunks - 1
    pieces[at][3] = swap(pieces[at][1], "core")
    weights[at] = comm.assemble_rest(weights[at], pieces[at])

    units = 3 * layer_count
    last_step = units + 5
    pairs, core_send, first_send, keep, late, total, back, both = [
        [None] * units for _ in range(8)
    ]
    packed, ada = None, None
    bias_width = 2 * sum(widths[1:])
    packed_width = layer_count * ada_width + features
    small_plan = {
        (units + 1, 0): "z2",
        (units + 1, 1): "z1",
        (units + 2, 0): "near",
        (units + 2, 1): "shard",
        (units + 3, 0): "core",
    }
    dh = output_grad.reshape(tokens, features)
    next_in = dh
    weight_out, arrived = [None] * 4, []
    by_pairs = units // 2
    far_step = {0: 4, 1: 6, 2: 7, 4: 8, 5: 9}
    back_step = {0: 6, 1: 7, 2: 8, 3: 9, 4: 9, 5: 10}
    end_step = {0: 8, 1: 8, 2: 9, 3: 10, 4: 10, 5: 11}
    for step in range(0, last_step + 1):

        def unit_at(lag):
            return step - lag if 0 <= step - lag < units else None

        on_core, on_shard, on_near = unit_at(1), unit_at(2), unit_at(3)
        on_far = [unit for unit, at in far_step.items() if at == step]
        on_far = on_far[0] if on_far else None
        on_back = [unit for unit in (unit_at(5), unit_at(6)) if back_step.get(unit) == step]
        on_end = [unit for unit, at in end_step.items() if at == step]
        out_far = by_pairs if unit_at(4) == by_pairs else None
        in_far = by_pairs if unit_at(5) == by_pairs else None
        live, fin = {}, {}
        if arrived:
            for entry in arrived:
                weight_out = finish(comm, *entry, layer_count, features, weight_out)
            fin["finals"], arrived = weight_out, []
        if on_core is not None:
            live["core"] = swap(core_send[on_core], "core")
        if on_shard is not None:
            fin["shard"] = swap(first_send[on_shard], "shard")
        if on_near is not None:
            fin["near"] = swap(late[on_near], "near")
        if on_far is not None:
            far = lax.psum(total[on_far], "far")
            if on_far:
                fin["far"] = far
        if step == far_step[0] + 1:
            fin["far"] = far
        waiting = [unit for unit, at in far_step.items() if at == step + 1 and at > unit + 4]
        if waiting:
            fin["hold"] = total[waiting[0]]
        if out_far is not None:
            live["z1"] = comm.far_swap(late[out_far], "z1")
        if in_far is not None:
            live["z2_back"] = comm.far_swap(total[in_far], "z2")
        if on_back:
            fin["back"] = [swap(back[unit], "near") for unit in on_back]
        if on_end:
            ends = [swap(both[unit], "core") for unit in on_end]
            (live if last_step - 3 <= step < last_step else fin)["end"] = ends
        if (step, 0) in small_plan:
            live["small"] = comm.any_swap(packed, small_plan[step, 0])
        if on_core is not None:
            got = live.pop("core")
            made = tuple(unit_sums(pairs[on_core], shard, comm.core, got))
            (live if step < units else fin)["made"] = made
        if step < units:
            l, part = layer_count - 1 - step // 3, step % 3
            block = blocks[l]
            w_attn, w_fc1, w_fc2 = weights[3 * l : 3 * l + 3]
            if part == 0:
                if step:
                    next_in = blocks[l + 1].back_end(weights[3 * (l + 1)], next_in)
                pairs[step] = [block.back_start(next_in)]
                next_in = block.grad_out
            elif part == 1:
                block.grad_out = next_in
                pairs[step] = [block.back_hidden(w_fc2)]
                next_in = block.grad_pre
            else:
                block.grad_pre = next_in
                middle = block.back_middle(w_fc1, w_attn)
                next_in = block.grad_attn
            live["next"] = next_in
        if step == units:
            dh = blocks[0].back_end(weights[0], next_in)
            outputs = blocks[layer_count - 1].output_layer(weights[3 * layer_count - 1], bf16)
            for block in blocks:
                block.gate_sum()
            fin["packed"] = packed_sums(blocks, silu_low, packed_width)
            fin["outputs"] = outputs, dh
        if step == units + 3:
            live["mods"] = mods_got
        live = gate(live) if live else live
        if step == units + 3:
            mods_both = comm.ordered(mods_mine, live["mods"], "shard")
            fin["silu_part"] = ada_back(mods_both.reshape(2 * seq_count, -1), w_ada)
        if "made" in live:
            first_send[on_core], keep[on_core] = live["made"]
        if "end" in live:
            for unit, got in zip(on_end, live["end"]):
                entry = both[unit], got, unit
                weight_out = finish(comm, *entry, layer_count, features, weight_out)
            fin["finals"], on_end = weight_out, []
        if out_far is not None:
            late[out_far], total[out_far] = comm.far_split(total[out_far], live["z1"], "z2")
            fin["z2"] = comm.far_swap(late[out_far], "z2")
        if in_far is not None:
            total[in_far] = comm.far_ordered(total[in_far], live["z2_back"], "z2")
            fin["z1_back"] = comm.far_swap(total[in_far], "z1")
        if "small" in live:
            packed = pack(packed, live["small"])
        if step == units + 4:
            fin["silu"] = swap(silu_send, "shard")
        if step == units + 3:
            count = packed.shape[0] - 1
            every = packed[:count].reshape(count * seq_count, packed_width)
            owned = [
                owned_biases(
                    every[:, l * ada_width : (l + 1) * ada_width],
                    packed[count, l, :bias_width].astype(f32),
                    shard,
                    widths,
                    2,
                )
                for l in range(layer_count)
            ]
            silu_block = (every.shape[0], owned_rows)
            silu_at = layer_count * ada_width // owned_rows
            for l in range(layer_count):
                ada = ada_weight(
                    (every, silu_block, lambda j, p: (0, silu_at + p[0])),
                    every,
                    l * ada_width,
                    ada_width,
                    l,
                    layer_count,
                    ada,
                    comm.place,
                )
            fin["ada"] = ada
        if (step, 1) in small_plan:
            fin["small"] = comm.any_swap(packed, small_plan[step, 1])
        if step == units + 2:
            fin["mods"] = swap(mods_mine, "shard")
        if step < units:
            next_in = live["next"]
            if part < 2:
                pairs[step] = [(pairs[step][0][0], next_in)]
            else:
                block.grad_attn = next_in
                pairs[step] = [block.back_attention(), middle]
                next_in = block.grad_qkv
            fin["next"] = next_in
            fin["send"] = unit_part(pairs[step], 1 - comm.core)
        if step == last_step:
            live = fin
        else:
            live = gate(fin)
        if "finals" in live:
            weight_out = live["finals"]
        if "made" in live:
            first_send[on_core], keep[on_core] = live["made"]
        if step < units:
            core_send[step], next_in = live["send"], live["next"]
            pairs[step][0] = (pairs[step][0][0], next_in)
        if on_shard is not None:
            shape = (2, keep[on_shard].shape[0] // 2, keep[on_shard].shape[1])
            sent, kept = comm.split(keep[on_shard].reshape(shape), "near")
            got_sent, got_kept = comm.split(live["shard"].reshape(shape), "near")
            late[on_shard], total[on_shard] = add(sent, got_sent), add(kept, got_kept)
        if on_near is not None and on_near == by_pairs:
            late[on_near], total[on_near] = comm.far_split(total[on_near], live["near"], "z1")
        elif on_near is not None:
            total[on_near] = add(total[on_near], live["near"])
        if out_far is not None:
            total[out_far] = add(total[out_far], live["z2"])
        if in_far is not None:
            back[in_far] = comm.far_ordered(total[in_far], live["z1_back"], "z1")
        if "hold" in live:
            total[waiting[0]] = live["hold"]
        if "far" in live:
            back[on_far or 0] = live["far"]
        for unit, got in zip(on_back, live.get("back", ())):
            both[unit] = jnp.stack([back[unit], got])
        for unit, got in zip(on_end, live.get("end", ())):
            arrived.append((both[unit], got, unit))
        if "ada" in live:
            ada = live["ada"]
        if "silu" in live:
            grad_silu = comm.ordered(silu_keep, live["silu"], "shard", at=1)
            grad_silu = grad_silu.reshape(seq_count, features)
        if step == units:
            outputs, dh = live["outputs"]
            packed = live["packed"]
            mods_mine = packed[0, :, : layer_count * ada_width]
        if "small" in live:
            packed = pack(packed, live["small"])
        if "mods" in live:
            mods_got = live["mods"]
        if "silu_part" in live:
            silu_part = live["silu_part"]
            silu_send, silu_keep = comm.split(
                silu_part.reshape(2, seq_count, owned_rows), "shard"
            )
    for entry in arrived:
        weight_out = finish(comm, *entry, layer_count, features, weight_out)
    return in_order(
        outputs.reshape(latents.shape),
        dh.reshape(latents.shape),
        silu_grad(cond_value, grad_silu),
        ada,
        [jnp.stack([o[m] for o in owned]) for m in range(5)],
        weight_out,
    )


def pack(mine, got):
    count = mine.shape[0] - 1
    return jnp.concatenate([mine[:count], got[:count], add(mine[count:], got[count:])], 0)


def finish(comm, mine, got, unit, layer_count, features, weight_out):
    layer, part = layer_count - 1 - unit // 3, unit % 3
    width = mine.shape[2]
    qkv, out, first, second = weight_out
    if part == 0:
        (second,) = comm.final(mine, got, layer, [(width, second)])
    elif part == 1:
        (first,) = comm.final(mine, got, layer, [(width, first)])
    else:
        half = features // 2
        qkv, out = comm.final(mine, got, layer, [(width - half, qkv), (half, out)])
    return [qkv, out, first, second]


def solution(mesh):
    rep, shard = mesh.shape["rep"], mesh.shape["shard"]
    core = 2 if rep % 2 == 0 else 1
    near = 2 if rep == 16 else 1
    far = rep // (core * near)
    fast = (far, near, core, shard) == (4, 2, 2, 2)
    fine = Mesh(
        np.asarray(mesh.devices).reshape(far, near, core, shard),
        ("far", "near", "core", "shard"),
    )
    every = ("far", "near", "core", "shard")
    row, row3 = P(every, None), P(every, None, None)
    bias, weight = P(None, "shard"), P(None, "shard", None)
    return jax.shard_map(
        local_fast if fast else local_plain,
        mesh=fine,
        in_specs=(
            row3, row, row3, weight, bias, weight, bias, weight, bias, weight, bias, weight, bias,
        ),
        out_specs=(
            row3, row3, row, weight, bias, weight, bias, weight, bias, weight, bias, weight, bias,
        ),
        check_vma=False,
    )
```

```python
import functools

import jax
import jax.numpy as jnp
import numpy as np
from jax import lax
from jax.experimental import pallas as pl
from jax.experimental.pallas import tpu as pltpu
from jax.sharding import Mesh
from jax.sharding import PartitionSpec as P

HEADS = 12
eps = 1e-06
f32 = jnp.float32
bf16 = jnp.bfloat16


def normalize(rows):
    centred = rows - jnp.mean(rows, axis=-1, keepdims=True)
    inverse = lax.rsqrt(jnp.mean(centred * centred, axis=-1, keepdims=True) + eps)
    return (centred * inverse, inverse)


def norm_back(upstream, normed, inverse):
    return inverse * (
        upstream
        - jnp.mean(upstream, axis=-1, keepdims=True)
        - normed * jnp.mean(upstream * normed, axis=-1, keepdims=True)
    )


def gelu_and_slope(u):
    square = u * u
    t = jnp.tanh(u * (0.7978845608028654 + 0.7978845608028654 * 0.044715 * square))
    half = 0.5 + 0.5 * t
    inner_slope = 0.7978845608028654 + 3.0 * 0.7978845608028654 * 0.044715 * square
    return u * half, half + 0.5 * u * (1.0 - t * t) * inner_slope


def mm(a, b):
    return jnp.dot(a, b, preferred_element_type=f32)


def mm_t(a, b):
    return lax.dot_general(a, b, (((1,), (1,)), ((), ())), preferred_element_type=f32)


def t_mm(a, b):
    return lax.dot_general(a, b, (((0,), (0,)), ((), ())), preferred_element_type=f32)


def pick(array, index, axis=0):
    return lax.dynamic_index_in_dim(array, index, axis, keepdims=False)


SWAP = [(0, 1), (1, 0)]
CHEAP = pl.CostEstimate(flops=1, bytes_accessed=1, transcendentals=0)
PARAMS = pltpu.CompilerParams(vmem_limit_bytes=63 * 2**20)


def swap(value, axis):
    return lax.ppermute(value, axis, SWAP)


def gate(tree):
    values, shape = jax.tree.flatten(tree)
    count = len(values)

    def nothing(*refs):
        pass

    out = pl.pallas_call(
        nothing,
        out_shape=[jax.ShapeDtypeStruct(v.shape, v.dtype) for v in values],
        in_specs=[pl.BlockSpec(memory_space=pl.ANY)] * count,
        out_specs=[pl.BlockSpec(memory_space=pl.ANY)] * count,
        input_output_aliases={i: i for i in range(count)},
        cost_estimate=CHEAP,
        compiler_params=PARAMS,
    )(*values)
    return jax.tree.unflatten(shape, out)


def call(kernel, grid, ins, outs, prefetch=(), aliases=None):
    def spec(block, index, once=False):
        if block is None:
            return pl.BlockSpec(memory_space=pl.ANY)
        if once:
            return pl.BlockSpec(block, index, pipeline_mode=pl.Buffered(1))
        return pl.BlockSpec(block, index)

    return pl.pallas_call(
        kernel,
        out_shape=[jax.ShapeDtypeStruct(shape, dtype) for shape, dtype, _, _ in outs],
        grid_spec=pltpu.PrefetchScalarGridSpec(
            num_scalar_prefetch=len(prefetch),
            grid=grid,
            in_specs=[spec(*entry[1:]) for entry in ins],
            out_specs=[spec(block, index) for _, _, block, index in outs],
        ),
        input_output_aliases=aliases or {},
        cost_estimate=CHEAP,
        compiler_params=PARAMS,
    )(*prefetch, *[entry[0] for entry in ins])


class Block:
    def __init__(self, mod, biases, seq_count, length):
        self.mod = mod.reshape(seq_count, 6, -1)
        self.biases = biases
        self.seq_count, self.length = seq_count, length
        self.features = self.mod.shape[2]

    def rows(self, array):
        return (array, (self.length, array.shape[1]), lambda s: (s, 0))

    def rows_out(self, width, dtype):
        shape = (self.seq_count * self.length, width)
        return (shape, dtype, (self.length, width), lambda s: (s, 0))

    def mods(self):
        return (self.mod, (None, 6, self.features), lambda s: (s, 0, 0))

    def sums_out(self):
        return (
            (self.seq_count, 8, self.features),
            f32,
            (None, 8, self.features),
            lambda s: (s, 0, 0),
        )

    @staticmethod
    def whole(array):
        return (array, array.shape, lambda s: (0,) * array.ndim, True)

    @staticmethod
    def columns(array, start, width):
        return (array, (array.shape[0], width), lambda s: (0, start // width), True)

    def attention(self, stream, w_attn):
        features, length = self.features, self.length
        bias_qv = self.biases[0]
        bias = jnp.concatenate(
            [bias_qv[:features], jnp.zeros((features,), f32), bias_qv[features:], self.biases[1]]
        )[None]
        head = features // HEADS
        factor = head ** (-0.5)

        def kernel(
            stream_ref, mod_ref, w_ref, bias_ref,
            in_ref, qkv_ref, out_ref, branch_ref, middle_ref, mlp_ref,
        ):
            normed, _ = normalize(stream_ref[...])
            attn_in = (normed * (1.0 + mod_ref[1:2]) + mod_ref[0:1]).astype(bf16)
            in_ref[...] = attn_in
            wide = 3 * features
            for at in range(0, wide, features):
                columns = slice(at, at + features)
                qkv_ref[:, columns] = (
                    mm(attn_in, w_ref[:, columns]) + bias_ref[:, columns]
                ).astype(bf16)
            for start in range(0, features, 128):
                q, k, v = [
                    qkv_ref[:, part * features + start : part * features + start + 128]
                    for part in range(3)
                ]
                total = jnp.zeros((length, 128), f32)
                for mask in head_masks(length, head):
                    probs = probs_of(jnp.where(mask, q, 0), k, factor).astype(bf16)
                    total = total + mm(probs, jnp.where(mask, v, 0))
                out_ref[:, start : start + 128] = total.astype(bf16)
            branch = mm(out_ref[...], w_ref[:, wide:]) + bias_ref[:, wide:]
            middle = stream_ref[...] + mod_ref[2:3] * branch
            normed, _ = normalize(middle)
            branch_ref[...] = branch
            middle_ref[...] = middle
            mlp_ref[...] = (normed * (1.0 + mod_ref[4:5]) + mod_ref[3:4]).astype(bf16)

        self.stream = stream
        self.attn_in, self.qkv, self.attn_out, self.branch, self.middle, self.mlp_in = call(
            kernel,
            (self.seq_count,),
            [self.rows(stream), self.mods(), self.whole(w_attn), self.whole(bias)],
            [
                self.rows_out(features, bf16),
                self.rows_out(3 * features, bf16),
                self.rows_out(features, bf16),
                self.rows_out(features, f32),
                self.rows_out(features, f32),
                self.rows_out(features, bf16),
            ],
        )

    def hidden_layer(self, w_fc1):
        hidden, tile, tokens = w_fc1.shape[1], self.features, self.seq_count * self.length

        def kernel(in_ref, w_ref, bias_ref, slope_ref, hidden_ref):
            value, slope = gelu_and_slope(mm(in_ref[...], w_ref[...]) + bias_ref[...])
            slope_ref[...] = slope.astype(bf16)
            hidden_ref[...] = value.astype(bf16)

        out = ((tokens, hidden), bf16, (tokens, tile), lambda j: (0, j))
        self.slope, self.hidden = call(
            kernel,
            (hidden // tile,),
            [
                (self.mlp_in, (tokens, self.features), lambda j: (0, 0)),
                (w_fc1, (self.features, tile), lambda j: (0, j)),
                (self.biases[2][None], (1, tile), lambda j: (0, j)),
            ],
            [out, out],
        )

    def output_layer(self, w_fc2, dtype):
        def kernel(hidden_ref, middle_ref, mod_ref, w_ref, bias_ref, output_ref, stream_ref):
            output = mm(hidden_ref[...], w_ref[...]) + bias_ref[...]
            output_ref[...] = output
            stream_ref[...] = (middle_ref[...] + mod_ref[5:6] * output).astype(dtype)

        self.output, stream = call(
            kernel,
            (self.seq_count,),
            [
                self.rows(self.hidden),
                self.rows(self.middle),
                self.mods(),
                self.whole(w_fc2),
                self.whole(self.biases[3][None]),
            ],
            [self.rows_out(self.features, f32), self.rows_out(self.features, dtype)],
        )
        return stream

    def back_start(self, dh):
        def kernel(dh_ref, mod_ref, grad_ref, sums_ref):
            grad_out = (mod_ref[5:6] * dh_ref[...].astype(f32)).astype(bf16)
            grad_ref[...] = grad_out
            sums_ref[0:1] = jnp.sum(grad_out.astype(f32), axis=0, keepdims=True)

        self.dh = dh
        self.grad_out, self.sums_out2 = call(
            kernel,
            (self.seq_count,),
            [self.rows(dh), self.mods()],
            [self.rows_out(self.features, bf16), self.sums_out()],
        )
        return (self.hidden, self.grad_out)

    def back_hidden(self, w_fc2):
        hidden, tile, tokens = w_fc2.shape[0], self.features, self.seq_count * self.length

        def kernel(grad_ref, slope_ref, w_ref, out_ref, sum_ref):
            grad_hidden = mm_t(grad_ref[...], w_ref[...])
            grad_pre = (grad_hidden * slope_ref[...].astype(f32)).astype(bf16)
            out_ref[...] = grad_pre
            sum_ref[...] = jnp.sum(grad_pre.astype(f32), axis=0, keepdims=True)

        self.grad_pre, self.sum_fc1 = call(
            kernel,
            (hidden // tile,),
            [
                (self.grad_out, (tokens, self.features), lambda j: (0, 0)),
                (self.slope, (tokens, tile), lambda j: (0, j)),
                (w_fc2, (tile, self.features), lambda j: (j, 0)),
            ],
            [
                ((tokens, hidden), bf16, (tokens, tile), lambda j: (0, j)),
                ((1, hidden), f32, (1, tile), lambda j: (0, j)),
            ],
        )
        return (self.mlp_in, self.grad_pre)

    def back_middle(self, w_fc1, w_attn):
        def kernel(
            grad_ref, w1_ref, dh_ref, middle_ref, mod_ref, branch_ref, wo_ref,
            mid_ref, gb_ref, ga_ref, sums_ref,
        ):
            grad_in = mm_t(grad_ref[...], w1_ref[...])
            normed, inverse = normalize(middle_ref[...])
            dh = dh_ref[...].astype(f32)
            mid = dh + norm_back(grad_in * (1.0 + mod_ref[4:5]), normed, inverse)
            grad_branch = (mod_ref[2:3] * mid).astype(bf16)
            mid_ref[...] = mid
            gb_ref[...] = grad_branch
            ga_ref[...] = mm_t(grad_branch, wo_ref[...]).astype(bf16)
            for at, value in enumerate(
                (
                    mid * branch_ref[...],
                    grad_in,
                    grad_in * normed,
                    grad_branch.astype(f32),
                )
            ):
                sums_ref[at : at + 1] = jnp.sum(value, axis=0, keepdims=True)

        self.grad_mid, self.grad_branch, self.grad_attn, self.sums_mid = call(
            kernel,
            (self.seq_count,),
            [
                self.rows(self.grad_pre),
                self.whole(w_fc1),
                self.rows(self.dh),
                self.rows(self.middle),
                self.mods(),
                self.rows(self.branch),
                self.columns(w_attn, 3 * self.features, self.features),
            ],
            [
                self.rows_out(self.features, f32),
                self.rows_out(self.features, bf16),
                self.rows_out(self.features, bf16),
                self.sums_out(),
            ],
        )
        return (self.attn_out, self.grad_branch)

    def gate_sum(self):
        def kernel(dh_ref, output_ref, sums_ref):
            product = dh_ref[...].astype(f32) * output_ref[...]
            sums_ref[0:1] = jnp.sum(product, axis=0, keepdims=True)

        self.sums_gate = call(
            kernel,
            (self.seq_count,),
            [self.rows(self.dh), self.rows(self.output)],
            [self.sums_out()],
        )[0]

    def back_attention(self):
        self.grad_qkv = attention_backward(self.qkv, self.grad_attn, self.seq_count)
        return (self.attn_in, self.grad_qkv)

    def back_end(self, w_attn, grad_qkv):
        features = self.features

        def kernel(grad_ref, w_ref, stream_ref, mod_ref, mid_ref, dh_ref, sums_ref):
            grad_qkv = grad_ref[...]
            grad_in = mm_t(grad_qkv, w_ref[...])
            normed, inverse = normalize(stream_ref[...].astype(f32))
            dh_ref[...] = mid_ref[...] + norm_back(
                grad_in * (1.0 + mod_ref[1:2]), normed, inverse
            )
            for at, value in enumerate((grad_in, grad_in * normed)):
                sums_ref[at : at + 1] = jnp.sum(value, axis=0, keepdims=True)
            for part in range(3):
                columns = grad_qkv[:, part * features : (part + 1) * features].astype(f32)
                sums_ref[2 + part : 3 + part] = jnp.sum(columns, axis=0, keepdims=True)

        dh, self.sums_end = call(
            kernel,
            (self.seq_count,),
            [
                self.rows(grad_qkv),
                self.columns(w_attn, 0, 3 * features),
                self.rows(self.stream),
                self.mods(),
                self.rows(self.grad_mid),
            ],
            [self.rows_out(features, f32), self.sums_out()],
        )
        return dh

    def sum_parts(self):
        return [self.sums_end, self.sums_mid, self.sums_gate, self.sums_out2, self.sum_fc1]


def packed_sums(blocks, silu_low, width):
    seq_count, features = silu_low.shape
    parts = [part for block in blocks for part in block.sum_parts()]

    def kernel(*refs):
        silu_ref, out_ref = refs[-2], refs[-1]
        out_ref[...] = jnp.zeros(out_ref.shape, bf16)
        for l in range(len(blocks)):
            end, mid, gate_m, out2, fc1 = refs[5 * l : 5 * l + 5]
            rows = [(end, 0), (end, 1), (mid, 0), (mid, 1), (mid, 2), (gate_m, 0)]
            for s in range(seq_count):
                for k, (ref, row) in enumerate(rows):
                    at = (6 * l + k) * features
                    out_ref[0, s : s + 1, at : at + features] = ref[s, row : row + 1].astype(
                        bf16
                    )
            at = 0
            for ref, row in ((end, 2), (end, 4), (mid, 3), (fc1, None), (out2, 0)):
                if row is None:
                    total = ref[...]
                else:
                    total = ref[0, row : row + 1]
                    for s in range(1, seq_count):
                        total = total + ref[s, row : row + 1]
                out_ref[1, l : l + 1, at : at + total.shape[1]] = total.astype(bf16)
                at += total.shape[1]
        at = 6 * len(blocks) * features
        out_ref[0, :, at : at + features] = silu_ref[...]

    shape = (2, seq_count, width)
    return call(
        kernel,
        (1,),
        [Block.whole(part) for part in parts + [silu_low]],
        [(shape, bf16, shape, lambda s: (0, 0, 0))],
    )[0]


def probs_of(q, k, factor):
    scores = mm_t(q, k) * factor
    raised = jnp.exp(scores - jnp.max(scores, axis=-1, keepdims=True))
    return raised * (1.0 / jnp.sum(raised, axis=-1, keepdims=True))


def head_masks(rows, head):
    lane = lax.broadcasted_iota(jnp.int32, (rows, 128), 1)
    return [jnp.logical_and(lane >= at, lane < at + head) for at in range(0, 128, head)]


def attention_backward(qkv, grad, count):
    tokens, triple = qkv.shape
    width, length, head = triple // 3, tokens // count, triple // 3 // HEADS
    tile = 384 if width % 384 == 0 else width
    steps = width // tile
    factor = head ** (-0.5)

    def kernel(q_ref, k_ref, v_ref, g_ref, out_ref):
        for start in range(0, tile, 128):
            group = slice(start, start + 128)
            q, k, v, g = q_ref[:, group], k_ref[:, group], v_ref[:, group], g_ref[:, group]
            grad_q = jnp.zeros((length, 128), f32)
            grad_k = jnp.zeros((length, 128), f32)
            grad_v = jnp.zeros((length, 128), f32)
            for mask in head_masks(length, head):
                own_q, own_g = jnp.where(mask, q, 0), jnp.where(mask, g, 0)
                probs = probs_of(own_q, k, factor)
                grad_probs = mm_t(own_g, v)
                row_terms = jnp.sum(grad_probs * probs, axis=-1, keepdims=True)
                grad_scores = (probs * (grad_probs - row_terms)).astype(bf16)
                grad_q = grad_q + mm(grad_scores, jnp.where(mask, k, 0))
                grad_k = grad_k + t_mm(grad_scores, own_q)
                grad_v = grad_v + t_mm(probs.astype(bf16), own_g)
            at = pl.program_id(1) * tile + start
            for part, value in enumerate((grad_q * factor, grad_k * factor, grad_v)):
                columns = pl.ds(pl.multiple_of(part * width + at, 128), 128)
                out_ref[:, columns] = value.astype(bf16)

    def part(which):
        return (qkv, (length, tile), lambda s, g: (s, which * steps + g))

    return call(
        kernel,
        (count, steps),
        [part(0), part(1), part(2), (grad, (length, tile), lambda s, g: (s, g))],
        [((tokens, triple), bf16, (length, triple), lambda s, g: (s, 0))],
    )[0]


TILE = 384


def product_part(lhs, rhs, col_half, into, at, width):
    tokens, rows = lhs.shape
    half = rhs.shape[1] // 2
    tile = TILE if half > 1024 else min(rows, 4 * TILE)
    shift = at // half
    place = jnp.asarray(col_half, jnp.int32).reshape(1)
    ins = [
        (lhs, (tokens, tile), lambda i, p: (0, i)),
        (rhs, (tokens, half), lambda i, p: (0, p[0])),
    ]
    aliases = {}
    if into is not None:
        aliases = {3: 0}
        ins.append((into, None, None))

    def kernel(place_ref, lhs_ref, rhs_ref, *refs):
        refs[-1][...] = t_mm(lhs_ref[...], rhs_ref[...]).astype(bf16)

    return call(
        kernel,
        (rows // tile,),
        ins,
        [((rows, width), bf16, (tile, half), lambda i, p: (i, shift))],
        prefetch=(place,),
        aliases=aliases,
    )[0]


def product_sums(lhs, rhs, shard, col_half, got, into, at, width):
    tokens, rows = lhs.shape
    half = rhs.shape[1] // 2
    place = jnp.stack([shard, col_half]).astype(jnp.int32)
    size = rows // 2
    shape = (size, width)
    aliases = {}
    if into is not None:
        aliases = {4: 0, 5: 1}
    extra = [(part, None, None) for part in into or ()]
    if half > TILE or rows <= 2 * TILE:
        tile = 512 if half % 512 == 0 and at % 512 == 0 else TILE
        tiles, shift = half // tile, at // tile

        def kernel(place_ref, lhs_ref, rhs_ref, got_ref, *refs):
            send_ref, keep_ref = refs[-2:]
            total = t_mm(lhs_ref[...], rhs_ref[...]) + got_ref[...].astype(f32)
            total = total.astype(bf16)
            first = place_ref[0] == 0
            send_ref[...] = jnp.where(first, total[size:], total[:size])
            keep_ref[...] = jnp.where(first, total[:size], total[size:])

        out = (shape, bf16, (size, tile), lambda j, p: (0, shift + j))
        return call(
            kernel,
            (tiles,),
            [
                (lhs, (tokens, rows), lambda j, p: (0, 0)),
                (rhs, (tokens, tile), lambda j, p: (0, p[1] * tiles + j)),
                (got, (rows, tile), lambda j, p: (0, shift + j)),
            ]
            + extra,
            [out, out],
            prefetch=(place,),
            aliases=aliases,
        )
    shift = at // half

    def row_tile(side, p):
        return jnp.where(side == 0, 1 - p[0], p[0])

    def tall_kernel(place_ref, lhs_ref, rhs_ref, got_ref, *refs):
        send_ref, keep_ref = refs[-2:]
        total = t_mm(lhs_ref[...], rhs_ref[...]) + got_ref[...].astype(f32)

        @pl.when(pl.program_id(0) == 0)
        def _():
            send_ref[...] = total.astype(bf16)

        @pl.when(pl.program_id(0) == 1)
        def _():
            keep_ref[...] = total.astype(bf16)

    out = (shape, bf16, (size, half), lambda side, p: (0, shift))
    return call(
        tall_kernel,
        (2,),
        [
            (lhs, (tokens, size), lambda side, p: (0, row_tile(side, p))),
            (rhs, (tokens, half), lambda side, p: (0, p[1])),
            (got, (size, half), lambda side, p: (row_tile(side, p), shift)),
        ]
        + extra,
        [out, out],
        prefetch=(place,),
        aliases=aliases,
    )


def unit_part(pairs, col_half):
    width = sum(rhs.shape[1] // 2 for _, rhs in pairs)
    out, at = None, 0
    for lhs, rhs in pairs:
        out = product_part(lhs, rhs, col_half, out, at, width)
        at += rhs.shape[1] // 2
    return out


def unit_sums(pairs, shard, col_half, got):
    width = sum(rhs.shape[1] // 2 for _, rhs in pairs)
    out, at = None, 0
    for lhs, rhs in pairs:
        out = product_sums(lhs, rhs, shard, col_half, got, out, at, width)
        at += rhs.shape[1] // 2
    return out


class Fast:
    def __init__(self):
        self.near = lax.axis_index("near")
        self.core = lax.axis_index("core")
        self.shard = lax.axis_index("shard")
        self.place = jnp.stack([self.shard, self.near, self.core]).astype(jnp.int32)

    def ordered(self, mine, got, axis, at=0):
        first = lax.axis_index(axis) == 0
        return jnp.stack([jnp.where(first, mine, got), jnp.where(first, got, mine)], axis=at)

    def split(self, stack, axis, at=0):
        me = lax.axis_index(axis)
        return pick(stack, 1 - me, at), pick(stack, me, at)

    def quarter(self, stacked, layer):
        size = stacked.shape[1] // 4
        start = (self.near * 2 + self.core) * size
        return lax.dynamic_slice(stacked, (layer, start, 0), (1, size, stacked.shape[2]))[0]

    def assemble_own(self, members, layer, place):
        rows = members[0].shape[1]
        widths = [member.shape[2] for member in members]
        size = rows // 2

        def kernel(place_ref, *refs):
            at = 0
            for member_ref, member_width in zip(refs, widths):
                refs[-1][:, at : at + member_width] = member_ref[...]
                at += member_width

        ins = [
            (member, (None, size, member.shape[2]), lambda s, p: (layer, s, 0))
            for member in members
        ]
        shape = (2 * rows, sum(widths))
        block = (size, sum(widths))
        return call(
            kernel,
            (2,),
            ins,
            [(shape, members[0].dtype, block, lambda s, p: (p[0] * 2 + s, 0))],
            prefetch=(place,),
        )[0]

    def assemble_rest(self, whole, pieces):
        size, width = pieces[0].shape

        def out_block(step, place):
            shard, near = place[0], place[1]
            return (1 - shard) * 2 + jnp.where(step == 0, near, 1 - near), 0

        def kernel(place_ref, *refs):
            out_ref, core = refs[-1], place_ref[2]
            for step in range(2):
                for mine in range(2):

                    @pl.when(jnp.logical_and(pl.program_id(0) == step, core == mine))
                    def _(step=step, mine=mine):
                        out_ref[mine * size : (mine + 1) * size] = refs[step][...]
                        out_ref[(1 - mine) * size : (2 - mine) * size] = refs[2 + step][...]

        ins = [(piece, (size, width), lambda s, p: (0, 0)) for piece in pieces]
        ins.append((whole, None, None))
        return call(
            kernel,
            (2,),
            ins,
            [(whole.shape, whole.dtype, (2 * size, width), out_block)],
            prefetch=(self.place,),
            aliases={5: 0},
        )[0]

    def final(self, mine, got, layer, parts):
        rows = mine.shape[1]
        widths = [width for width, _ in parts]

        def out_block(step, place):
            near = place[1]
            return layer, jnp.where(step == 0, near, 1 - near), 0

        def kernel(place_ref, mine_ref, got_ref, *refs):
            outs, core = refs[-len(parts) :], place_ref[2]
            for first in range(2):
                low, high = (mine_ref, got_ref) if first == 0 else (got_ref, mine_ref)

                @pl.when(core == first)
                def _(low=low, high=high):
                    at = 0
                    for out_ref, width in zip(outs, widths):
                        out_ref[:, :width] = low[:, at : at + width].astype(f32)
                        out_ref[:, width:] = high[:, at : at + width].astype(f32)
                        at += width

        block = (None, rows, mine.shape[2])
        ins = [(array, block, lambda i, p: (i, 0, 0)) for array in (mine, got)]
        aliases = {}
        for at, (_, into) in enumerate(parts):
            if into is not None:
                aliases[1 + len(ins)] = at
                ins.append((into, None, None))
        return call(
            kernel,
            (2,),
            ins,
            [
                ((2, 2 * rows, 2 * width), f32, (None, rows, 2 * width), out_block)
                for width in widths
            ],
            prefetch=(self.place,),
            aliases=aliases,
        )

    def far_swap(self, value, name):
        step = 1 if name == "z1" else 2
        return lax.ppermute(value, "far", [(i, i ^ step) for i in range(4)])

    def far_side(self, name):
        far = lax.axis_index("far")
        return far % 2 if name == "z1" else far // 2

    def far_split(self, mine, got, name):
        side = self.far_side(name)
        shape = (2, mine.shape[0] // 2, mine.shape[1])
        mine, got = mine.reshape(shape), got.reshape(shape)
        return (
            add(pick(mine, 1 - side), pick(got, 1 - side)),
            add(pick(mine, side), pick(got, side)),
        )

    def far_ordered(self, mine, got, name):
        first = self.far_side(name) == 0
        return jnp.concatenate([jnp.where(first, mine, got), jnp.where(first, got, mine)], 0)

    def any_swap(self, value, name):
        return self.far_swap(value, name) if name in ("z1", "z2") else swap(value, name)


def ada_product(silu, w_ada):
    layers, rows, width = w_ada.shape
    tile = width // 2

    def kernel(silu_ref, w_ref, out_ref):
        out_ref[...] = mm(silu_ref[...], w_ref[...])

    return call(
        kernel,
        (layers, 2),
        [
            (silu, silu.shape, lambda l, j: (0, 0)),
            (w_ada, (None, rows, tile), lambda l, j: (l, 0, j)),
        ],
        [
            (
                (silu.shape[0], layers * width),
                f32,
                (silu.shape[0], tile),
                lambda l, j: (0, 2 * l + j),
            )
        ],
    )[0]


def ada_back(mods, w_ada):
    layers, rows, width = w_ada.shape
    tile = width // 2

    def kernel(mods_ref, w_ref, out_ref):
        first = jnp.logical_and(pl.program_id(0) == 0, pl.program_id(1) == 0)

        @pl.when(first)
        def _():
            out_ref[...] = jnp.zeros(out_ref.shape, f32)

        out_ref[...] += mm_t(mods_ref[...], w_ref[...])

    return call(
        kernel,
        (layers, 2),
        [
            (mods, (mods.shape[0], tile), lambda l, j: (0, 2 * l + j)),
            (w_ada, (None, rows, tile), lambda l, j: (l, 0, j)),
        ],
        [((mods.shape[0], rows), f32, (mods.shape[0], rows), lambda l, j: (0, 0))],
    )[0]


def ada_weight(silu, mods, start, width, layer, layers, into, place):
    count, rows = silu[1]
    tile = 768 if width % 768 == 0 and start % 768 == 0 else width
    first = start // tile

    def kernel(place_ref, silu_ref, mods_ref, *refs):
        refs[-1][...] = t_mm(silu_ref[...], mods_ref[...])

    ins = [silu, (mods, (count, tile), lambda j, p: (0, first + j))]
    aliases = {}
    if into is not None:
        aliases = {3: 0}
        ins.append((into, None, None))
    return call(
        kernel,
        (width // tile,),
        ins,
        [((layers, rows, width), f32, (None, rows, tile), lambda j, p: (layer, 0, j))],
        prefetch=(place,),
        aliases=aliases,
    )[0]


def add(a, b):
    return (a.astype(f32) + b.astype(f32)).astype(bf16)


def silu_grad(cond_value, grad_silu):
    _, silu_pull = jax.vjp(jax.nn.silu, cond_value)
    return silu_pull(grad_silu)[0]


def owned_biases(mod_every, bias_sums, shard, widths, shard_count):
    totals, at = [jnp.sum(mod_every.astype(f32), axis=0)], 0
    for width in widths[1:]:
        totals.append(bias_sums[at : at + width * shard_count])
        at += width * shard_count
    return [
        lax.dynamic_slice_in_dim(total, shard * width, width, 0)
        for total, width in zip(totals, widths)
    ]


def unpack_biases(bias_all, widths):
    cuts = np.cumsum(widths)[:-1]
    parts = [
        jnp.moveaxis(part, 0, 1).reshape(bias_all.shape[1], -1).astype(f32)
        for part in jnp.split(bias_all, cuts, axis=2)
    ]
    return [[part[l] for part in parts] for l in range(bias_all.shape[1])]


def in_order(outputs, dh, condition_grad, g_w_ada, biases, weights):
    return (
        outputs,
        dh,
        condition_grad,
        g_w_ada,
        biases[0],
        weights[0],
        biases[1],
        weights[1],
        biases[2],
        weights[2],
        biases[3],
        weights[3],
        biases[4],
    )


def local_plain(
    latents,
    condition,
    output_grad,
    w_ada,
    b_ada,
    query_key_value_weight,
    b_qv,
    output_matrix_weight,
    b_proj,
    first_linear_weight,
    b_fc1,
    second_linear_weight,
    b_fc2,
):
    layer_count, owned_rows, ada_width = w_ada.shape
    seq_count, length, features = latents.shape
    shard, shards = lax.axis_index("shard"), lax.axis_size("shard")
    every = ("far", "near", "core", "shard")
    biases = (b_ada, b_qv, b_proj, b_fc1, b_fc2)
    widths = [b.shape[1] for b in biases]

    cond_value = condition.astype(f32)
    silu_low = jax.nn.silu(cond_value).astype(bf16)
    silu_group = lax.all_gather(silu_low, "shard", axis=0, tiled=True)
    silu_mine = lax.dynamic_slice_in_dim(silu_group, shard * owned_rows, owned_rows, 1)
    bias_all = lax.all_gather(jnp.concatenate(biases, axis=1), "shard", axis=0)
    full_biases = unpack_biases(bias_all, widths)
    mod_part = jnp.concatenate([mm(silu_mine, w_ada[l]) for l in range(layer_count)], axis=1)
    mod = lax.psum_scatter(mod_part, "shard", scatter_dimension=0, tiled=True)
    mod = mod.reshape(seq_count, layer_count, ada_width)
    silu_every = lax.all_gather(silu_low, every, axis=0, tiled=True)

    tokens = seq_count * length
    stream, blocks, weights = latents.astype(f32).reshape(tokens, features), [], []
    for l in range(layer_count):
        block = Block(mod[:, l] + full_biases[l][0], full_biases[l][1:], seq_count, length)
        full = [
            lax.all_gather(w[l], "shard", axis=0, tiled=True)
            for w in (
                query_key_value_weight,
                output_matrix_weight,
                first_linear_weight,
                second_linear_weight,
            )
        ]
        full[:2] = [jnp.concatenate(full[:2], axis=1)]
        block.attention(stream, full[0])
        block.hidden_layer(full[1])
        stream = block.output_layer(full[2], bf16 if l == layer_count - 1 else f32)
        blocks.append(block)
        weights.append(full)

    hidden_width = first_linear_weight.shape[2]

    def reduce(pair):
        grad = t_mm(*pair).astype(bf16)
        grad = lax.psum_scatter(grad, "shard", scatter_dimension=0, tiled=True)
        return lax.psum(grad, ("far", "near", "core")).astype(f32)

    dh = output_grad.reshape(tokens, features)
    grads, ada, owned, grad_silu = [None] * layer_count, None, [None] * layer_count, 0.0
    silu_owned = lax.dynamic_slice_in_dim(silu_every, shard * owned_rows, owned_rows, 1)
    for l in reversed(range(layer_count)):
        block, full = blocks[l], weights[l]
        second = block.back_start(dh)
        first = block.back_hidden(full[2])
        out = block.back_middle(full[1], full[0])
        qkv = block.back_attention()
        dh = block.back_end(full[0], block.grad_qkv)
        block.gate_sum()
        sums = packed_sums([block], silu_low, 8 * features + hidden_width)
        grad_mod = sums[0, :, : 6 * features]
        bias_sums = sums[1, 0, : 4 * features + hidden_width]
        grads[l] = [reduce(pair) for pair in (qkv, out, first, second)]
        mod_every = lax.all_gather(grad_mod, every, axis=0, tiled=True)
        silu = (silu_owned, silu_owned.shape, lambda j, p: (0, 0))
        place = jnp.zeros((1,), jnp.int32)
        ada = ada_weight(silu, mod_every, 0, ada_width, l, layer_count, ada, place)
        sums = lax.psum(bias_sums.astype(f32), every)
        owned[l] = owned_biases(mod_every, sums, shard, widths, shards)
        mods_group = lax.all_gather(grad_mod, "shard", axis=0, tiled=True)
        grad_silu = grad_silu + mm_t(mods_group, w_ada[l])
    by_owner = grad_silu.reshape(shards, seq_count, owned_rows)
    got = lax.all_to_all(by_owner, "shard", 0, 0)
    grad_silu = jnp.moveaxis(got, 0, 1).reshape(seq_count, features)
    return in_order(
        stream.reshape(latents.shape),
        dh.reshape(latents.shape),
        silu_grad(cond_value, grad_silu),
        ada,
        [jnp.stack([o[m] for o in owned]) for m in range(5)],
        [jnp.stack([g[m] for g in grads]) for m in range(4)],
    )


def local_fast(
    latents,
    condition,
    output_grad,
    w_ada,
    b_ada,
    query_key_value_weight,
    b_qv,
    output_matrix_weight,
    b_proj,
    first_linear_weight,
    b_fc1,
    second_linear_weight,
    b_fc2,
):
    comm = Fast()
    layer_count, owned_rows, ada_width = w_ada.shape
    seq_count, length, features = latents.shape
    tokens = seq_count * length
    shard = comm.shard
    biases = (b_ada, b_qv, b_proj, b_fc1, b_fc2)
    widths = [b.shape[1] for b in biases]

    chunk_of = []
    for l in range(layer_count):
        chunk_of.append((l, (query_key_value_weight, output_matrix_weight)))
        chunk_of.append((l, (first_linear_weight,)))
        chunk_of.append((l, (second_linear_weight,)))
    chunks = len(chunk_of)
    sends = []
    for l, members in chunk_of:
        quarters = [comm.quarter(member, l) for member in members]
        sends.append(quarters[0] if len(quarters) == 1 else jnp.concatenate(quarters, axis=1))

    cond_value = condition.astype(f32)
    silu_low = jax.nn.silu(cond_value).astype(bf16)
    bias_mine = jnp.concatenate(biases, axis=1)
    latents_flat = latents.reshape(tokens, features)
    stream = latents_flat
    pieces = [[None] * 4 for _ in range(chunks)]
    weights = [None] * chunks
    blocks = [None] * layer_count
    outputs, place = None, comm.place + 0
    sends[0], silu_low = gate((sends[0], silu_low))
    stream = stream.astype(f32)
    for step in range(0, chunks + 1):
        live = {}
        if step < chunks:
            live["a"] = swap(sends[step], "shard")
        at = step - 1
        if 0 <= at < chunks:
            live["b"] = swap(pieces[at][0], "near")
            live["a2"] = swap(pieces[at][0], "core")
        if step == 0:
            live["silu"] = swap(silu_low, "shard")
            live["later"] = bias_mine
        elif step == 1:
            live["bias"] = swap(bias_mine, "shard")
            live["a2"], silu_mine = gate((live["a2"], silu_mine))
            mod_part = ada_product(silu_mine, w_ada)
            mod_send, mod_keep = comm.split(mod_part.reshape(2, seq_count, -1), "shard")
            live["mod"] = swap(mod_send, "shard")
        at = step - 2
        if at >= 0:
            pieces[at][3] = swap(pieces[at][1], "core")
            weights[at] = comm.assemble_rest(weights[at], pieces[at])
            l, part = at // 3, at % 3
            block = blocks[l]
            if part == 0:
                block.attention(stream, weights[at])
                live["done"] = block.mlp_in
            elif part == 1:
                block.hidden_layer(weights[at])
                live["done"] = block.hidden
            else:
                stream = block.output_layer(weights[at], f32)
                live["done"] = stream
        if step + 1 < chunks:
            live["send"] = sends[step + 1]
        early = {0: (0, 1, 2), 1: (3,), 3: (4,), 4: (5,)}.get(step, ())
        live["own"] = [
            comm.assemble_own(chunk_of[k][1], chunk_of[k][0], place) for k in early
        ]
        live["place"] = place
        live = gate(live)
        for k, own in zip(early, live["own"]):
            weights[k] = own
        place = live["place"]
        if step + 1 < chunks:
            sends[step + 1] = live["send"]
        if step < chunks:
            pieces[step][0] = live["a"]
        if at >= 0:
            if part == 0:
                block.mlp_in = live["done"]
            elif part == 1:
                block.hidden = live["done"]
            else:
                stream = live["done"]
        at = step - 1
        if 0 <= at < chunks:
            pieces[at][1], pieces[at][2] = live["b"], live["a2"]
        if step == 0:
            bias_mine = live["later"]
            silu_pair = comm.ordered(silu_low, live["silu"], "shard")
            silu_pair = silu_pair.reshape(2 * seq_count, features)
            silu_mine = lax.dynamic_slice_in_dim(silu_pair, shard * owned_rows, owned_rows, 1)
        elif step == 1:
            full_biases = unpack_biases(comm.ordered(bias_mine, live["bias"], "shard"), widths)
            mod = (mod_keep + live["mod"]).reshape(seq_count, layer_count, ada_width)
            for l in range(layer_count):
                blocks[l] = Block(
                    mod[:, l] + full_biases[l][0], full_biases[l][1:], seq_count, length
                )
    at = chunks - 1
    pieces[at][3] = swap(pieces[at][1], "core")
    weights[at] = comm.assemble_rest(weights[at], pieces[at])

    units = 3 * layer_count
    last_step = units + 5
    pairs, core_send, first_send, keep, late, total, back, both = [
        [None] * units for _ in range(8)
    ]
    packed, ada = None, None
    bias_width = 2 * sum(widths[1:])
    packed_width = layer_count * ada_width + features
    small_plan = {
        (units + 1, 0): "z2",
        (units + 1, 1): "z1",
        (units + 2, 0): "near",
        (units + 2, 1): "shard",
        (units + 3, 0): "core",
    }
    dh = output_grad.reshape(tokens, features)
    next_in = dh
    weight_out, arrived = [None] * 4, []
    by_pairs = units // 2
    far_step = {0: 4, 1: 6, 2: 7, 4: 8, 5: 9}
    back_step = {0: 6, 1: 7, 2: 8, 3: 9, 4: 9, 5: 10}
    end_step = {0: 8, 1: 8, 2: 9, 3: 10, 4: 10, 5: 11}
    for step in range(0, last_step + 1):

        def unit_at(lag):
            return step - lag if 0 <= step - lag < units else None

        on_core, on_shard, on_near = unit_at(1), unit_at(2), unit_at(3)
        on_far = [unit for unit, at in far_step.items() if at == step]
        on_far = on_far[0] if on_far else None
        on_back = [unit for unit in (unit_at(5), unit_at(6)) if back_step.get(unit) == step]
        on_end = [unit for unit, at in end_step.items() if at == step]
        out_far = by_pairs if unit_at(4) == by_pairs else None
        in_far = by_pairs if unit_at(5) == by_pairs else None
        live, fin = {}, {}
        if arrived:
            for entry in arrived:
                weight_out = finish(comm, *entry, layer_count, features, weight_out)
            fin["finals"], arrived = weight_out, []
        if on_core is not None:
            live["core"] = swap(core_send[on_core], "core")
        if on_shard is not None:
            fin["shard"] = swap(first_send[on_shard], "shard")
        if on_near is not None:
            fin["near"] = swap(late[on_near], "near")
        if on_far is not None:
            far = lax.psum(total[on_far], "far")
            if on_far:
                fin["far"] = far
        if step == far_step[0] + 1:
            fin["far"] = far
        waiting = [unit for unit, at in far_step.items() if at == step + 1 and at > unit + 4]
        if waiting:
            fin["hold"] = total[waiting[0]]
        if out_far is not None:
            live["z1"] = comm.far_swap(late[out_far], "z1")
        if in_far is not None:
            live["z2_back"] = comm.far_swap(total[in_far], "z2")
        if on_back:
            fin["back"] = [swap(back[unit], "near") for unit in on_back]
        if on_end:
            ends = [swap(both[unit], "core") for unit in on_end]
            (live if last_step - 3 <= step < last_step else fin)["end"] = ends
        if (step, 0) in small_plan:
            live["small"] = comm.any_swap(packed, small_plan[step, 0])
        if on_core is not None:
            got = live.pop("core")
            made = tuple(unit_sums(pairs[on_core], shard, comm.core, got))
            (live if step < units else fin)["made"] = made
        if step < units:
            l, part = layer_count - 1 - step // 3, step % 3
            block = blocks[l]
            w_attn, w_fc1, w_fc2 = weights[3 * l : 3 * l + 3]
            if part == 0:
                if step:
                    next_in = blocks[l + 1].back_end(weights[3 * (l + 1)], next_in)
                pairs[step] = [block.back_start(next_in)]
                next_in = block.grad_out
            elif part == 1:
                block.grad_out = next_in
                pairs[step] = [block.back_hidden(w_fc2)]
                next_in = block.grad_pre
            else:
                block.grad_pre = next_in
                middle = block.back_middle(w_fc1, w_attn)
                next_in = block.grad_attn
            live["next"] = next_in
        if step == units:
            dh = blocks[0].back_end(weights[0], next_in)
            outputs = blocks[layer_count - 1].output_layer(weights[3 * layer_count - 1], bf16)
            for block in blocks:
                block.gate_sum()
            fin["packed"] = packed_sums(blocks, silu_low, packed_width)
            fin["outputs"] = outputs, dh
        if step == units + 3:
            live["mods"] = mods_got
        live = gate(live) if live else live
        if step == units + 3:
            mods_both = comm.ordered(mods_mine, live["mods"], "shard")
            fin["silu_part"] = ada_back(mods_both.reshape(2 * seq_count, -1), w_ada)
        if "made" in live:
            first_send[on_core], keep[on_core] = live["made"]
        if "end" in live:
            for unit, got in zip(on_end, live["end"]):
                entry = both[unit], got, unit
                weight_out = finish(comm, *entry, layer_count, features, weight_out)
            fin["finals"], on_end = weight_out, []
        if out_far is not None:
            late[out_far], total[out_far] = comm.far_split(total[out_far], live["z1"], "z2")
            fin["z2"] = comm.far_swap(late[out_far], "z2")
        if in_far is not None:
            total[in_far] = comm.far_ordered(total[in_far], live["z2_back"], "z2")
            fin["z1_back"] = comm.far_swap(total[in_far], "z1")
        if "small" in live:
            packed = pack(packed, live["small"])
        if step == units + 4:
            fin["silu"] = swap(silu_send, "shard")
        if step == units + 3:
            count = packed.shape[0] - 1
            every = packed[:count].reshape(count * seq_count, packed_width)
            owned = [
                owned_biases(
                    every[:, l * ada_width : (l + 1) * ada_width],
                    packed[count, l, :bias_width].astype(f32),
                    shard,
                    widths,
                    2,
                )
                for l in range(layer_count)
            ]
            silu_block = (every.shape[0], owned_rows)
            silu_at = layer_count * ada_width // owned_rows
            for l in range(layer_count):
                ada = ada_weight(
                    (every, silu_block, lambda j, p: (0, silu_at + p[0])),
                    every,
                    l * ada_width,
                    ada_width,
                    l,
                    layer_count,
                    ada,
                    comm.place,
                )
            fin["ada"] = ada
        if (step, 1) in small_plan:
            fin["small"] = comm.any_swap(packed, small_plan[step, 1])
        if step == units + 2:
            fin["mods"] = swap(mods_mine, "shard")
        if step < units:
            next_in = live["next"]
            if part < 2:
                pairs[step] = [(pairs[step][0][0], next_in)]
            else:
                block.grad_attn = next_in
                pairs[step] = [block.back_attention(), middle]
                next_in = block.grad_qkv
            fin["next"] = next_in
            fin["send"] = unit_part(pairs[step], 1 - comm.core)
        if step == last_step:
            live = fin
        else:
            live = gate(fin)
        if "finals" in live:
            weight_out = live["finals"]
        if "made" in live:
            first_send[on_core], keep[on_core] = live["made"]
        if step < units:
            core_send[step], next_in = live["send"], live["next"]
            pairs[step][0] = (pairs[step][0][0], next_in)
        if on_shard is not None:
            shape = (2, keep[on_shard].shape[0] // 2, keep[on_shard].shape[1])
            sent, kept = comm.split(keep[on_shard].reshape(shape), "near")
            got_sent, got_kept = comm.split(live["shard"].reshape(shape), "near")
            late[on_shard], total[on_shard] = add(sent, got_sent), add(kept, got_kept)
        if on_near is not None and on_near == by_pairs:
            late[on_near], total[on_near] = comm.far_split(total[on_near], live["near"], "z1")
        elif on_near is not None:
            total[on_near] = add(total[on_near], live["near"])
        if out_far is not None:
            total[out_far] = add(total[out_far], live["z2"])
        if in_far is not None:
            back[in_far] = comm.far_ordered(total[in_far], live["z1_back"], "z1")
        if "hold" in live:
            total[waiting[0]] = live["hold"]
        if "far" in live:
            back[on_far or 0] = live["far"]
        for unit, got in zip(on_back, live.get("back", ())):
            both[unit] = jnp.stack([back[unit], got])
        for unit, got in zip(on_end, live.get("end", ())):
            arrived.append((both[unit], got, unit))
        if "ada" in live:
            ada = live["ada"]
        if "silu" in live:
            grad_silu = comm.ordered(silu_keep, live["silu"], "shard", at=1)
            grad_silu = grad_silu.reshape(seq_count, features)
        if step == units:
            outputs, dh = live["outputs"]
            packed = live["packed"]
            mods_mine = packed[0, :, : layer_count * ada_width]
        if "small" in live:
            packed = pack(packed, live["small"])
        if "mods" in live:
            mods_got = live["mods"]
        if "silu_part" in live:
            silu_part = live["silu_part"]
            silu_send, silu_keep = comm.split(
                silu_part.reshape(2, seq_count, owned_rows), "shard"
            )
    for entry in arrived:
        weight_out = finish(comm, *entry, layer_count, features, weight_out)
    return in_order(
        outputs.reshape(latents.shape),
        dh.reshape(latents.shape),
        silu_grad(cond_value, grad_silu),
        ada,
        [jnp.stack([o[m] for o in owned]) for m in range(5)],
        weight_out,
    )


def pack(mine, got):
    count = mine.shape[0] - 1
    return jnp.concatenate([mine[:count], got[:count], add(mine[count:], got[count:])], 0)


def finish(comm, mine, got, unit, layer_count, features, weight_out):
    layer, part = layer_count - 1 - unit // 3, unit % 3
    width = mine.shape[2]
    qkv, out, first, second = weight_out
    if part == 0:
        (second,) = comm.final(mine, got, layer, [(width, second)])
    elif part == 1:
        (first,) = comm.final(mine, got, layer, [(width, first)])
    else:
        half = features // 2
        qkv, out = comm.final(mine, got, layer, [(width - half, qkv), (half, out)])
    return [qkv, out, first, second]


def solution(mesh):
    rep, shard = mesh.shape["rep"], mesh.shape["shard"]
    core = 2 if rep % 2 == 0 else 1
    near = 2 if rep == 16 else 1
    far = rep // (core * near)
    fast = (far, near, core, shard) == (4, 2, 2, 2)
    fine = Mesh(
        np.asarray(mesh.devices).reshape(far, near, core, shard),
        ("far", "near", "core", "shard"),
    )
    every = ("far", "near", "core", "shard")
    row, row3 = P(every, None), P(every, None, None)
    bias, weight = P(None, "shard"), P(None, "shard", None)
    return jax.shard_map(
        local_fast if fast else local_plain,
        mesh=fine,
        in_specs=(
            row3, row, row3, weight, bias, weight, bias, weight, bias, weight, bias, weight, bias,
        ),
        out_specs=(
            row3, row3, row, weight, bias, weight, bias, weight, bias, weight, bias, weight, bias,
        ),
        check_vma=False,
    )
```
